128 devices in a mesh: seq: 32 (over y, x, core), exp: 4 (over z).
Axes of the slice: x: 4, y: 4, z: 4, core: 2. Of those that a mesh axis runs over, the one named last changes fastest.
Arguments:
- hidden: bfloat16 [256, 6144], P('seq', 'exp'), may hold values from -6 to 6
- queries: bfloat16 [256, 6144], P('seq', 'exp'), may hold values from -18 to 18
- suffix_row_keys: bfloat16 [256, 1024], P('seq', 'exp'), may hold values from -12 to 12
- suffix_row_values: bfloat16 [256, 1024], P('seq', 'exp'), may hold values from -6 to 6
- prefix_cached_keys: bfloat16 [65536, 1024], P('seq', 'exp'), may hold values from -10 to 10
- prefix_cached_values: bfloat16 [65536, 1024], P('seq', 'exp'), may hold values from -6 to 6
- expert_norm_gain: bfloat16 [6144], replicated, may hold values from 0.099609375 to 1.8984375
- router: bfloat16 [6144, 4], replicated, may hold values from -0.078125 to 0.078125
- gate_weight: bfloat16 [4, 6144, 8192], P('exp', None, 'seq'), may hold values from -0.078125 to 0.078125
- up_weight: bfloat16 [4, 6144, 8192], P('exp', None, 'seq'), may hold values from -0.078125 to 0.078125
- down_weight: bfloat16 [4, 8192, 6144], P('exp', 'seq'), may hold values from -0.0625 to 0.0625
- adapter_down_maps: bfloat16 [64, 4, 16, 8192], P(None, 'exp', None, 'seq'), may hold values from -0.0625 to 0.0625
- adapter_up_maps: bfloat16 [64, 4, 16, 6144], P('seq', 'exp'), may hold values from -1.5 to 1.5
- routes: int32 [256, 2], replicated, may hold values from 0 to 3, all different within a row; in each aligned block of 8 rows (0 to 7, 8 to 15, ...) at most 6 rows name the same one
- tenants: int32 [256], replicated, may hold values from 0 to 63, as said below
- lengths: int32 [64], replicated, may hold values from 1 to 7, as said below
Outputs:
- mixed: bfloat16 [256, 6144], P('seq', 'exp')
The draws below stay inside these ranges and needn't reach their ends.
Inputs may be any that keep to these rules, and one draw needn't show every extreme that they name: `routes`: each row names two different experts; among the 8 rows of one index of seq no expert is named by more than 6 rows, a bound that some block reaches. `tenants`: row r belongs to tenant 2 * (r // 8) or the one after it; ids never fall along the rows; every tenant has at least one row. `lengths`: A tenant's length is at most its number of rows; some tenant has exactly 7 rows and that length.
All inputs are finite; a program needn't handle non-finite values.
Results may differ from the reference program's by a relative error of at most 0.017.
Values may be sent and summed in bfloat16 or wider, within the bound.
A program may use at most 192 MiB of HBM per device.

```python
import math
import jax
import jax.numpy as jnp
import numpy as np
from jax import lax

MODEL_WIDTH = 6144
QUERY_HEADS = 48
KEY_VALUE_HEADS = 8
HEAD_SIZE = 128
HIDDEN_UNITS = 8192
ADAPTER_RANK = 16
ROW_DEV = 8
PREFIX_PER_INDEX = 2048
EXPERT_COUNT = 4
SUFFIX_ROWS = 256
PREFIX_LENGTH = 65536
TENANT_COUNT = 64
CAP = 6
N_SEQ = 32


def tenant_splits(key):
    block_count = SUFFIX_ROWS // ROW_DEV
    splits = jax.random.randint(jax.random.fold_in(key, 11), (block_count,), 1, ROW_DEV)
    full_block = jax.random.randint(jax.random.fold_in(key, 12), (), 0, block_count)
    splits = jnp.where(jnp.arange(block_count) == full_block, ROW_DEV - 1, splits)
    return (splits.astype(jnp.int32), full_block)


def draw_queries(key, part):
    key = jax.random.fold_in(key, 1)
    sampled_inputs = 3.0 * jax.random.normal(key, (SUFFIX_ROWS, QUERY_HEADS, HEAD_SIZE), jnp.float32)
    return jnp.clip(sampled_inputs, -18.0, 18.0).reshape(SUFFIX_ROWS, QUERY_HEADS * HEAD_SIZE).astype(jnp.bfloat16)


def draw_prefix_cached_keys(key, part):
    key = jax.random.fold_in(key, 3)
    sampled_inputs = jax.random.normal(key, (PREFIX_LENGTH, KEY_VALUE_HEADS, HEAD_SIZE), jnp.float32)
    return jnp.clip(sampled_inputs, -10.0, 10.0).reshape(PREFIX_LENGTH, KEY_VALUE_HEADS * HEAD_SIZE).astype(jnp.bfloat16)


def draw_tenants(key, part):
    splits, full_block = tenant_splits(key)
    row_ids = jnp.arange(SUFFIX_ROWS)
    block_ids = row_ids // ROW_DEV
    local_ids = row_ids % ROW_DEV
    return (2 * block_ids + (local_ids >= splits[block_ids]).astype(jnp.int32)).astype(jnp.int32)


def draw_lengths(key, part):
    splits, full_block = tenant_splits(key)
    key = jax.random.fold_in(key, 31)
    counts = jnp.stack([splits, ROW_DEV - splits], axis=1).reshape(-1)
    sampled_inputs = jax.random.randint(key, (TENANT_COUNT,), 1, counts + 1)
    sampled_inputs = jnp.where(jnp.arange(TENANT_COUNT) == 2 * full_block, ROW_DEV - 1, sampled_inputs)
    return sampled_inputs.astype(jnp.int32)


def shard_levels(key, dims, pieces, least, top_value):
    factor_of = 1.0
    for axis_at, shards_of in pieces:
        draws = jax.random.uniform(jax.random.fold_in(jax.random.fold_in(key, 6), axis_at), (shards_of,), jnp.float32, least / len(pieces), top_value / len(pieces))
        factor_of = factor_of * jnp.repeat(jnp.exp(draws), dims[axis_at] // shards_of).reshape((-1,) + (1,) * (len(dims) - 1 - axis_at))
    return factor_of


def routed_block(key, own, number, rows, count, top, limit, lean):
    ranking = jax.random.permutation(key, count)
    packed, usual = shares(count, rows * top, limit, lean, True), shares(count, rows * top, limit, lean, False)
    places = jnp.arange(count)

    def named(sizes, offset_by):
        used = int((sizes > 0).sum())
        fixed = max(1, used // 4)
        passed = fixed + (places - fixed + offset_by * (used - fixed)) % max(1, count - fixed)
        return jnp.zeros((count,), jnp.int32).at[ranking[jnp.where(places < fixed, places, passed)]].set(jnp.asarray(sizes, jnp.int32))

    sizes = jnp.where(number % 4 == 0, named(packed, number // 4), named(usual, number - number // 4 - 1))
    mixed = jax.random.permutation(jax.random.fold_in(own, 3), count)
    giver, sink = mixed[0:count // 2 * 2:2], mixed[1:count // 2 * 2:2]
    slack = jnp.minimum(sizes[giver] - 1, limit - sizes[sink]) // 2
    slack = jnp.where((giver == ranking[0]) | (sink == ranking[0]) | (sizes[sink] == 0), 0, jnp.maximum(slack, 0))
    passed = jax.random.randint(jax.random.fold_in(own, 4), (count // 2,), 0, 1 << 20) % (slack + 1)
    sizes = sizes.at[giver].add(-passed).at[sink].add(passed)
    members = jnp.searchsorted(jnp.cumsum(sizes), jnp.arange(rows * top), side="right").astype(jnp.int32)
    table = members.reshape(top, rows).T
    table = table[jax.random.permutation(jax.random.fold_in(own, 1), rows)]
    offset_by = jax.random.randint(jax.random.fold_in(own, 2), (rows, 1), 0, top)
    return jnp.take_along_axis(table, (jnp.arange(top)[None, :] + offset_by) % top, axis=1)


def shares(count, total, limit, slope, full):
    portions = [(1 << 20) // math.isqrt(grade ** slope) + 1 for grade in range(1, count + 1)]
    largest = limit if full else min(limit, max(-(-total // count), total * portions[0] // sum(portions)))
    least = 1 if total - largest >= count - 1 else 0
    holding, rest = [largest] + [least] * (count - 1), total - largest - least * (count - 1)
    while rest > 0:
        movable = [i for i in range(1, count) if holding[i] < largest] or [i for i in range(1, count) if holding[i] < limit]
        pool, budget = sum([portions[i] for i in movable]), rest
        for i in movable:
            extra = min(limit - holding[i], max(1, budget * portions[i] // pool), rest)
            holding[i] = holding[i] + extra
            rest = rest - extra
    return np.array(holding)


def normal_values(key, extent, spread, bound, split=(), held_as=jnp.bfloat16):
    gain = shard_levels(key, extent, split, -0.22, 0.18) if split else 1.0
    entries = jax.random.normal(key, extent, jnp.float32) * spread * gain
    return jnp.minimum(jnp.maximum(entries, -bound), bound).astype(held_as)


def setup_inputs(seed: int = 0) -> dict:
    keys = jax.random.split(jax.random.key(seed), 17)
    hidden = normal_values(keys[0], (SUFFIX_ROWS, MODEL_WIDTH), 1.0, 6.0, ((0, 32), (1, 4)))
    queries = draw_queries(jax.random.fold_in(keys[16], 71), 0)
    suffix_row_keys = normal_values(keys[2], (SUFFIX_ROWS, KEY_VALUE_HEADS * HEAD_SIZE), 2.0, 12.0, ((0, 32), (1, 4)))
    suffix_row_values = normal_values(keys[3], (SUFFIX_ROWS, KEY_VALUE_HEADS * HEAD_SIZE), 1.0, 6.0, ((0, 32), (1, 4)))
    prefix_cached_keys = draw_prefix_cached_keys(jax.random.fold_in(keys[16], 71), 0)
    prefix_cached_values = normal_values(keys[5], (PREFIX_LENGTH, KEY_VALUE_HEADS * HEAD_SIZE), 1.0, 6.0, ((0, 32), (1, 4)))
    expert_norm_gain = jnp.clip(1.0 + 0.18 * jax.random.normal(keys[6], (MODEL_WIDTH,), jnp.float32), 0.099609375, 1.8984375).astype(jnp.bfloat16)
    router = normal_values(keys[7], (MODEL_WIDTH, EXPERT_COUNT), MODEL_WIDTH ** -0.5, 0.078125)
    gate_weight = normal_values(keys[8], (EXPERT_COUNT, MODEL_WIDTH, HIDDEN_UNITS), MODEL_WIDTH ** -0.5, 0.078125, ((0, 4), (2, 32)))
    up_weight = normal_values(keys[9], (EXPERT_COUNT, MODEL_WIDTH, HIDDEN_UNITS), MODEL_WIDTH ** -0.5, 0.078125, ((0, 4), (2, 32)))
    down_weight = normal_values(keys[10], (EXPERT_COUNT, HIDDEN_UNITS, MODEL_WIDTH), HIDDEN_UNITS ** -0.5, 0.0625, ((0, 4), (1, 32)))
    adapter_down_maps = normal_values(keys[11], (TENANT_COUNT, EXPERT_COUNT, ADAPTER_RANK, HIDDEN_UNITS), HIDDEN_UNITS ** -0.5, 0.0625, ((1, 4), (3, 32)))
    adapter_up_maps = normal_values(keys[12], (TENANT_COUNT, EXPERT_COUNT, ADAPTER_RANK, MODEL_WIDTH), ADAPTER_RANK ** -0.5, 1.5, ((0, 32), (1, 4)))
    routes_keys = jax.random.split(jax.random.fold_in(keys[13], 1), SUFFIX_ROWS // ROW_DEV)
    routes_turns = jax.random.permutation(jax.random.fold_in(keys[13], 3), SUFFIX_ROWS // ROW_DEV)
    routes = jax.vmap(lambda own, number: routed_block(jax.random.fold_in(keys[13], 2), own, number, ROW_DEV, EXPERT_COUNT, 2, CAP, 2))(routes_keys, routes_turns).reshape((SUFFIX_ROWS, 2))
    tenants = draw_tenants(jax.random.fold_in(keys[16], 71), 0)
    lengths = draw_lengths(jax.random.fold_in(keys[16], 71), 0)
    return {"hidden": hidden, "queries": queries, "suffix_row_keys": suffix_row_keys, "suffix_row_values": suffix_row_values, "prefix_cached_keys": prefix_cached_keys, "prefix_cached_values": prefix_cached_values, "expert_norm_gain": expert_norm_gain, "router": router, "gate_weight": gate_weight, "up_weight": up_weight, "down_weight": down_weight, "adapter_down_maps": adapter_down_maps, "adapter_up_maps": adapter_up_maps, "routes": routes, "tenants": tenants, "lengths": lengths}


NORM_EPS = 1e-05

def shard_partial(query_rows, key_rows, value_rows):
    scores = jnp.dot(query_rows, key_rows.T, preferred_element_type=jnp.float32) * HEAD_SIZE ** (-0.5)
    row_peak = lax.optimization_barrier(jnp.max(scores, axis=1))
    weights = jnp.exp(scores - row_peak[:, None])
    row_mass = lax.optimization_barrier(jnp.sum(weights, axis=1))
    row_accum = jnp.dot(weights.astype(jnp.bfloat16), value_rows, preferred_element_type=jnp.float32)
    return (row_peak, row_mass, row_accum)

def reference(hidden, queries, suffix_row_keys, suffix_row_values, prefix_cached_keys, prefix_cached_values, expert_norm_gain, router, gate_weight, up_weight, down_weight, adapter_down_maps, adapter_up_maps, routes, tenants, lengths):
    query_group_width = QUERY_HEADS // KEY_VALUE_HEADS
    row_ids = jnp.arange(SUFFIX_ROWS)
    same_tenant = tenants[:, None] == tenants[None, :]
    before_row = row_ids[None, :] < row_ids[:, None]
    position = lax.optimization_barrier(jnp.sum((same_tenant & before_row).astype(jnp.int32), axis=1))
    row_length = jnp.take(lengths, tenants)
    visible = same_tenant & (position[None, :] <= position[:, None]) & (position[None, :] < row_length[:, None])
    visible_rep = jnp.repeat(visible, query_group_width, axis=0)
    query_head_rows = queries.reshape(SUFFIX_ROWS, KEY_VALUE_HEADS, query_group_width, HEAD_SIZE).transpose(1, 0, 2, 3).reshape(KEY_VALUE_HEADS, SUFFIX_ROWS * query_group_width, HEAD_SIZE)
    prefix_key_block = prefix_cached_keys.reshape(N_SEQ, PREFIX_PER_INDEX, KEY_VALUE_HEADS, HEAD_SIZE).transpose(2, 0, 1, 3)
    prefix_value_block = prefix_cached_values.reshape(N_SEQ, PREFIX_PER_INDEX, KEY_VALUE_HEADS, HEAD_SIZE).transpose(2, 0, 1, 3)
    suffix_key_block = suffix_row_keys.reshape(SUFFIX_ROWS, KEY_VALUE_HEADS, HEAD_SIZE).transpose(1, 0, 2)
    suffix_value_block = suffix_row_values.reshape(SUFFIX_ROWS, KEY_VALUE_HEADS, HEAD_SIZE).transpose(1, 0, 2)

    def one_head(head_args):
        query_rows, shard_keys, shard_values, own_keys, own_values = head_args

        def one_shard(shard_pair):
            return shard_partial(query_rows, shard_pair[0], shard_pair[1])
        peak_list, mass_list, accum_list = lax.map(one_shard, (shard_keys, shard_values))
        scores = jnp.dot(query_rows, own_keys.T, preferred_element_type=jnp.float32) * HEAD_SIZE ** (-0.5)
        scores = jnp.where(visible_rep, scores, -1e+30)
        suffix_peak = lax.optimization_barrier(jnp.max(scores, axis=1))
        suffix_weights = jnp.where(visible_rep, jnp.exp(scores - suffix_peak[:, None]), 0.0)
        suffix_mass = lax.optimization_barrier(jnp.sum(suffix_weights, axis=1))
        suffix_accum = jnp.dot(suffix_weights.astype(jnp.bfloat16), own_values, preferred_element_type=jnp.float32)
        overall = jnp.maximum(lax.optimization_barrier(jnp.max(peak_list, axis=0)), suffix_peak)
        factor = jnp.exp(peak_list - overall[None, :])
        suffix_factor = jnp.exp(suffix_peak - overall)
        mass = lax.optimization_barrier(jnp.sum(factor * mass_list, axis=0)) + suffix_factor * suffix_mass
        accum = lax.optimization_barrier(jnp.sum(factor[:, :, None] * accum_list, axis=0)) + suffix_factor[:, None] * suffix_accum
        return accum / mass[:, None]
    head_output = lax.map(one_head, (query_head_rows, prefix_key_block, prefix_value_block, suffix_key_block, suffix_value_block))
    prefix_attention = head_output.reshape(KEY_VALUE_HEADS, SUFFIX_ROWS, query_group_width, HEAD_SIZE).transpose(1, 0, 2, 3).reshape(SUFFIX_ROWS, MODEL_WIDTH)
    residual = (hidden.astype(jnp.float32) + prefix_attention).astype(jnp.bfloat16)
    resid_f = residual.astype(jnp.float32)
    mean_square = lax.optimization_barrier(jnp.mean(resid_f * resid_f, axis=1))
    normed = (resid_f * lax.rsqrt(mean_square + NORM_EPS)[:, None] * expert_norm_gain.astype(jnp.float32)[None, :]).astype(jnp.bfloat16)
    logits = jnp.dot(normed, router, preferred_element_type=jnp.float32)
    picked = jnp.take_along_axis(logits, routes, axis=1)
    share_first = jax.nn.sigmoid(picked[:, 0] - picked[:, 1])
    share_second = jax.nn.sigmoid(picked[:, 1] - picked[:, 0])
    tenant_hot = tenants[:, None] == jnp.arange(TENANT_COUNT)[None, :]
    tenant_f = tenant_hot.astype(jnp.float32)
    mixture = jnp.zeros((SUFFIX_ROWS, MODEL_WIDTH), jnp.float32)
    for expert_index in range(EXPERT_COUNT):
        gate_proj = jnp.dot(normed, gate_weight[expert_index], preferred_element_type=jnp.float32)
        up_proj = jnp.dot(normed, up_weight[expert_index], preferred_element_type=jnp.float32)
        hidden_activations = (jax.nn.silu(gate_proj) * up_proj).astype(jnp.bfloat16)
        down_proj = jnp.dot(hidden_activations, down_weight[expert_index], preferred_element_type=jnp.float32)
        lowrank_gathered = jnp.dot(hidden_activations, adapter_down_maps[:, expert_index].reshape(TENANT_COUNT * ADAPTER_RANK, HIDDEN_UNITS).T, preferred_element_type=jnp.float32)
        low_rank = lax.optimization_barrier(jnp.sum(lowrank_gathered.reshape(SUFFIX_ROWS, TENANT_COUNT, ADAPTER_RANK) * tenant_f[:, :, None], axis=1)).astype(jnp.bfloat16)
        lowrank_padded = (tenant_hot[:, :, None].astype(jnp.bfloat16) * low_rank[:, None, :]).reshape(SUFFIX_ROWS, TENANT_COUNT * ADAPTER_RANK)
        tenant_adapter = jnp.dot(lowrank_padded, adapter_up_maps[:, expert_index].reshape(TENANT_COUNT * ADAPTER_RANK, MODEL_WIDTH), preferred_element_type=jnp.float32)
        route_weight = share_first * (routes[:, 0] == expert_index).astype(jnp.float32) + share_second * (routes[:, 1] == expert_index).astype(jnp.float32)
        mixture = mixture + route_weight[:, None] * (down_proj + tenant_adapter)
    return (resid_f + mixture).astype(jnp.bfloat16)
```

```python
import functools

import jax
import jax.numpy as jnp
from jax import lax
from jax.experimental import pallas as pl
from jax.experimental.pallas import tpu as pltpu
from jax.sharding import PartitionSpec as P

MESH = pl.DeviceIdType.MESH
F32 = jnp.float32
BF16 = jnp.bfloat16

HEAD = 128
GROUP = 6
KV = 2
HEADS = KV * GROUP
ROWS = 8
SEQ = 32
EXP = 4
CHIPS = SEQ // 2
PAIR = 2 * ROWS
TOTAL = SEQ * ROWS
WIDTH = 6144
HALF = WIDTH // 2
QUARTER = WIDTH // EXP
PREFIX = 2048
UNITS = 256
QB = GROUP * ROWS
BLK = KV * QB
MSG = BLK + 16
EXT = HALF + 128
CUT = 1536
NORM_EPS = 1e-05
LOG2E = 1.4426950408889634
SCALE2 = HEAD**-0.5 * LOG2E


def dot(a, b):
    return jnp.dot(a, b, preferred_element_type=F32)


def dot_t(a, b):
    return lax.dot_general(a, b, (((1,), (1,)), ((), ())), preferred_element_type=F32)


def iota(shape, dim):
    return lax.broadcasted_iota(jnp.int32, shape, dim)


def three_parts(v):
    high = v.astype(BF16).astype(F32)
    rest = v - high
    mid = rest.astype(BF16).astype(F32)
    low = rest - mid
    ax = v.ndim - 1
    return high + pltpu.roll(mid, 16, ax) + pltpu.roll(low, 32, ax)


def whole_of(p):
    ax = p.ndim - 1
    return p + pltpu.roll(p, 128 - 16, ax) + pltpu.roll(p, 128 - 32, ax)


def kernel(
    hid, qry, skey, sval, pk, pv, gain, rout, wg, wu, wd, adn, aup, routes, tenants, lengths,
    out,
    qall, kbuf, vext, sbuf, pbuf, suf_o, suf_l, rsnd, rbuf, xbuf, wgb, wub, wdb, adnb, upb,
    accg, accu, s1snd, s1rcv, own, p2, r2a, r2b, p3a, p3b, r3a, r3b, fsnd, fbuf, resid_ref,
    lsem, qs, qf, qr, ps, pr, rs, rr, xs, xf, xr, ups, upr, s1s, s1r, as2, ar2, bs2, br2,
    as3, ar3, bs3, br3, fs, fr,
):
    s = lax.axis_index("seq")
    z = lax.axis_index("exp")
    k = lax.rem(s, 2)
    c = lax.div(s, 2)
    x = lax.rem(c, 4)
    y = lax.div(c, 4)
    sib = s + 1 - 2 * k

    def remote(src, dst, ssem, rsem, seq, exp):
        return pltpu.make_async_remote_copy(
            src_ref=src, dst_ref=dst, send_sem=ssem, recv_sem=rsem,
            device_id=(seq, exp), device_id_type=MESH,
        )

    def each(n, body, first=0):
        def step(i, carry):
            body(i)
            return carry

        lax.fori_loop(first, n, step, 0)

    k_half = pl.multiple_of(k * HALF, HALF)
    up_row = pl.multiple_of(64 * lax.rem(c, 2) + 32 * k, 32)
    loads = [
        (pk, kbuf),
        (pv.at[:, pl.ds(0, HEAD)], vext.at[0, :, pl.ds(0, HEAD)]),
        (pv.at[:, pl.ds(HEAD, HEAD)], vext.at[1, :, pl.ds(0, HEAD)]),
        (wg, wgb),
        (wu, wub),
        (wd, wdb),
        (adn, adnb),
        (aup.at[:, pl.ds(k_half, HALF)], upb.at[pl.ds(up_row, 32), :]),
    ]
    loads = [pltpu.make_async_copy(a, b, lsem.at[i]) for i, (a, b) in enumerate(loads)]
    for cp in loads:
        cp.start()

    q = qry[...].astype(F32)
    for g in range(KV):
        heads = [q[:, (g * GROUP + j) * HEAD : (g * GROUP + j + 1) * HEAD] for j in range(GROUP)]
        qall[g, s] = jnp.concatenate(heads, axis=0).astype(BF16)

    barrier = pltpu.get_barrier_semaphore()

    def greet_plane(i):
        pl.semaphore_signal(barrier, inc=1, device_id=(lax.rem(s + i, SEQ), z), device_id_type=MESH)

    each(SEQ, greet_plane, 1)
    for d in range(1, EXP):
        for other in (s, sib):
            pl.semaphore_signal(
                barrier, inc=1, device_id=(other, lax.rem(z + d, EXP)), device_id_type=MESH
            )
    vext[:, :, HEAD:] = jnp.ones((KV, PREFIX, HEAD), BF16)
    other_rows = pl.multiple_of(64 - 64 * lax.rem(c, 2), 64)
    upb[pl.ds(other_rows, 64), :] = jnp.zeros((64, HALF), BF16)
    pl.semaphore_wait(barrier, SEQ - 1 + 2 * (EXP - 1))

    def chip_at(i):
        return lax.rem(y + 4 - i // 4, 4) * 4 + lax.rem(x + i % 4, 4)

    def q_copy(block, to, ssem):
        return remote(qall.at[:, block], qall.at[:, block], ssem, qr.at[block], to, z)

    def q_send(i):
        return q_copy(s, chip_at(i) * 2 + k, qs.at[i])

    def q_sib():
        return q_copy(s, sib, qs.at[0])

    q_sib().start()
    each(CHIPS, lambda i: q_send(i).start(), 1)
    up_other = pl.multiple_of(HALF - k * HALF, HALF)

    def up_copy():
        return remote(
            aup.at[:, pl.ds(up_other, HALF)], upb.at[pl.ds(up_row, 32), :], ups.at[0], upr.at[0], sib, z
        )

    up_copy().start()

    row8 = iota((ROWS, 128), 0)
    lane8 = iota((ROWS, 128), 1)
    ten = [tenants[s * ROWS + i] for i in range(ROWS)]
    pos = []
    for i in range(ROWS):
        p = jnp.int32(0)
        for j in range(i):
            p = p + (ten[i] == ten[j]).astype(jnp.int32)
        pos.append(p)
    lens = [lengths[ten[i]] for i in range(ROWS)]

    def spread(values, at):
        got = jnp.full((ROWS, 128), -1, jnp.int32)
        for i, v in enumerate(values):
            got = jnp.where(at == i, v, got)
        return got

    ten_r, ten_c = spread(ten, row8), spread(ten, lane8)
    pos_r, pos_c = spread(pos, row8), spread(pos, lane8)
    len_r = spread(lens, row8)
    visible = (lane8 < ROWS) & (ten_r == ten_c) & (pos_c <= pos_r) & (pos_c < len_r)
    visible = jnp.broadcast_to(visible[None], (GROUP, ROWS, 128))
    sk = skey[...].astype(F32)
    sv = sval[...].astype(F32)
    fill = jnp.zeros((128 - ROWS, HEAD), F32)
    stat = jnp.zeros((ROWS, 128), F32)
    for g in range(KV):
        kg = jnp.concatenate([sk[:, g * HEAD : (g + 1) * HEAD], fill], axis=0).astype(BF16)
        vg = jnp.concatenate([sv[:, g * HEAD : (g + 1) * HEAD], fill], axis=0).astype(BF16)
        sc = dot_t(qall[g, s], kg).reshape(GROUP, ROWS, 128)
        sc = jnp.where(visible, sc, -1e30)
        m = jnp.max(sc, axis=2, keepdims=True)
        w = jnp.where(visible, jnp.exp2((sc - m) * SCALE2), 0.0)
        mass = jnp.sum(w, axis=2, keepdims=True)
        acc = dot(w.reshape(QB, 128).astype(BF16), vg).reshape(GROUP, ROWS, HEAD)
        suf_o[g * GROUP : (g + 1) * GROUP] = acc / mass
        lse = jnp.broadcast_to(m * SCALE2 + jnp.log2(mass), (GROUP, ROWS, 128))
        for j in range(GROUP):
            stat = jnp.where(lane8 == g * GROUP + j, lse[j], stat)
    suf_l[...] = stat

    for cp in loads[:3]:
        cp.wait()

    def q_forward(yy):
        def one(i):
            chip = yy * 4 + lax.rem(x + i, 4)

            @pl.when(chip != c)
            def _():
                block = chip * 2 + k
                q_copy(block, sib, qf.at[chip]).wait_recv()
                q_copy(block, sib, qf.at[chip]).start()

        each(4, one)

    def p_copy(block, to):
        return remote(sbuf.at[block], pbuf.at[s], ps.at[block], pr.at[s], to, z)

    def attend(dy):
        yy = lax.rem(y + dy, 4)

        @pl.when(dy == 0)
        def _():
            q_forward(y)

        @pl.when(dy == 1)
        def _():
            for d in range(1, 4):
                q_forward(lax.rem(y + d, 4))

        def from_sib(i):
            block = (yy * 4 + i) * 2 + 1 - k
            q_copy(block, sib, qf.at[0]).wait_recv()

        each(4, from_sib)
        lane = iota((8, ROWS, 128), 2)
        stat = jnp.zeros((8, ROWS, 128), F32)
        for g in range(KV):
            qg = qall[g, pl.ds(yy * 8, 8)].reshape(8 * QB, HEAD)
            sc = dot_t(qg, kbuf[:, g * HEAD : (g + 1) * HEAD])
            m = jnp.max(sc, axis=1, keepdims=True) * SCALE2
            w = jnp.exp2(sc * SCALE2 - m).astype(BF16)
            acc = dot(w, vext[g])
            mass = acc[:, HEAD:]
            o = acc[:, :HEAD] / mass
            sbuf[pl.ds(yy * 8, 8), g * QB : (g + 1) * QB, :] = o.astype(BF16).reshape(8, QB, HEAD)
            lse = (m + jnp.log2(mass)).reshape(8, GROUP, ROWS, 128)
            for j in range(GROUP):
                stat = jnp.where(lane == g * GROUP + j, lse[:, j], stat)
        parts = three_parts(stat)
        parts = jnp.concatenate([parts, jnp.zeros_like(parts)], axis=1).astype(BF16)
        sbuf[pl.ds(yy * 8, 8), BLK:, :] = parts

        def p_send(i):
            block = yy * 8 + lax.rem(lax.rem(s, 8) + i, 8)

            @pl.when(block != s)
            def _():
                p_copy(block, block).start()

        each(8, p_send)

    each(4, attend)
    keep = pltpu.make_async_copy(sbuf.at[s], pbuf.at[s], lsem.at[8])
    keep.start()
    keep.wait()

    def p_wait(i):
        @pl.when(i != s)
        def _():
            remote(sbuf.at[i], pbuf.at[i], ps.at[i], pr.at[i], i, z).wait_recv()

    each(SEQ, p_wait)
    lses = whole_of(pbuf[:, BLK:, :].astype(F32)[:, :ROWS])
    top = jnp.maximum(jnp.max(lses, axis=0), suf_l[...])
    shares = jnp.exp2(lses - top[None])
    suf_share = jnp.exp2(suf_l[...] - top)
    inverse = 1.0 / (jnp.sum(shares, axis=0) + suf_share)
    suf_share = suf_share * inverse
    att = [suf_share[:, h : h + 1] * suf_o[h] for h in range(HEADS)]
    for i in range(SEQ):
        part = pbuf[i, 0:BLK, :].astype(F32)
        share = shares[i] * inverse
        for h in range(HEADS):
            att[h] = att[h] + share[:, h : h + 1] * part[h * ROWS : (h + 1) * ROWS]
    resid = hid[...].astype(F32) + jnp.concatenate(att, axis=1)
    resid = resid.astype(BF16).astype(F32)
    resid_ref[...] = resid
    cols = QUARTER // 2
    rsnd[...] = jnp.concatenate([resid[:, :cols], resid[:, cols:]], axis=0).astype(BF16)

    to_core = lax.div(z, 2)
    r_slot = k * 2 + lax.rem(z, 2)

    def r_copy(d):
        return remote(
            rsnd, rbuf.at[r_slot], rs.at[d], rr.at[r_slot], c * 2 + to_core, lax.rem(z + d, EXP)
        )

    for d in range(1, EXP):
        r_copy(d).start()

    @pl.when(to_core != k)
    def _():
        r_copy(0).start()

    @pl.when(to_core == k)
    def _():
        rbuf[r_slot] = rsnd[...]

    for kk in range(2):
        for j in range(2):

            @pl.when(~((kk == k) & (2 * k + j == z)))
            def _():
                slot = kk * 2 + j
                remote(
                    rsnd, rbuf.at[slot], rs.at[0], rr.at[slot], c * 2 + kk, 2 * k + j
                ).wait_recv()

    halves = []
    for kk in range(2):
        got = [rbuf[kk * 2 + j].astype(F32) for j in range(2)]
        halves.append(
            jnp.concatenate([got[0][:ROWS], got[0][ROWS:], got[1][:ROWS], got[1][ROWS:]], axis=1)
        )
    both = jnp.concatenate(halves, axis=0)
    squares = jnp.sum(both * both, axis=1, keepdims=True)
    gains = gain[...].astype(F32)
    gains = jnp.where(k == 0, gains[:, :HALF], gains[:, HALF:])
    own_rows = pl.multiple_of(c * PAIR, PAIR)
    xbuf[k, pl.ds(own_rows, PAIR), 0:HALF] = (both * gains).astype(BF16)
    squares = jnp.where(iota((PAIR, 128), 1) == 0, squares, 0.0)
    xbuf[k, pl.ds(own_rows, PAIR), HALF:] = three_parts(squares).astype(BF16)

    def x_copy(half, chip, to, ssem):
        at = pl.ds(pl.multiple_of(chip * PAIR, PAIR), PAIR)
        return remote(xbuf.at[half, at, :], xbuf.at[half, at, :], ssem, xr.at[half, chip], to, z)

    x_copy(k, c, sib, xs.at[0]).start()
    each(CHIPS, lambda i: x_copy(k, c, chip_at(i) * 2 + k, xs.at[i]).start(), 1)

    def x_forward(i):
        chip = lax.rem(y + i // 4, 4) * 4 + lax.rem(x + i % 4, 4)
        x_copy(k, chip, sib, xf.at[chip]).wait_recv()
        x_copy(k, chip, sib, xf.at[chip]).start()

    each(CHIPS, x_forward, 1)

    for cp in loads[3:5]:
        cp.wait()
    step_cols = 1024

    def project(half, first):
        def one(i):
            at = pl.multiple_of(i * step_cols, step_cols)
            rows = pl.ds(pl.multiple_of(half * HALF + at, step_cols), step_cols)
            xs_ = xbuf[half, :, pl.ds(at, step_cols)]
            g_ = dot(xs_, wgb[rows, :])
            u_ = dot(xs_, wub[rows, :])
            accg[...] = accg[...] + g_
            accu[...] = accu[...] + u_

        if first:
            accg[...] = jnp.zeros_like(accg)
            accu[...] = jnp.zeros_like(accu)
        each(HALF // step_cols, one)

    project(k, True)
    each(CHIPS, lambda i: x_copy(1 - k, i, sib, xf.at[0]).wait_recv())
    project(1 - k, False)

    def inverse_norm(parts):
        total = jnp.sum(parts, axis=1, keepdims=True)
        return lax.rsqrt(total / WIDTH + NORM_EPS)

    scale = inverse_norm(xbuf[0, :, HALF:].astype(F32) + xbuf[1, :, HALF:].astype(F32))
    gate = accg[...] * scale
    units = (gate / (1.0 + jnp.exp(-gate)) * (accu[...] * scale)).astype(BF16)

    for cp in loads[5:]:
        cp.wait()
    low = [
        dot_t(units[i * 32 : (i + 1) * 32], adnb[i * 128 : (i + 1) * 128, :])
        for i in range(CHIPS // 2)
    ]
    low = jnp.concatenate(low, axis=0)
    s1snd[:, HALF:] = low.astype(BF16)
    own[:, HALF:] = low

    part = 768
    n_parts = HALF // part
    widths = [part] * (n_parts - 1) + [part + 128]

    def s1_copy(i):
        at = pl.ds(i * part, widths[i])
        return remote(s1snd.at[:, at], s1rcv.at[:, at], s1s.at[i], s1r.at[i], sib, z)

    def down(half, i):
        at = pl.multiple_of(half * HALF + i * part, 128)
        return dot(units, wdb[:, pl.ds(at, part)])

    for i in range(n_parts):
        s1snd[:, i * part : (i + 1) * part] = down(1 - k, i).astype(BF16)
        s1_copy(i).start()
    for i in range(n_parts):
        own[:, i * part : (i + 1) * part] = down(k, i)

    def a2_copy(d):
        xx = lax.rem(x + d, 4)
        return remote(
            p2.at[:, xx, :, pl.ds(0, CUT)], r2a.at[x], as2.at[d], ar2.at[x], (y * 4 + xx) * 2 + k, z
        )

    def b2_copy(d):
        yy = lax.rem(y + d, 4)
        return remote(
            p2.at[yy, :, :, pl.ds(CUT, EXT - CUT)], r2b.at[y], bs2.at[d], br2.at[y],
            (yy * 4 + x) * 2 + k, z,
        )

    for i in range(n_parts):
        s1_copy(i).wait_recv()
        at = slice(i * part, i * part + widths[i])
        both = own[:, at] + s1rcv[:, at].astype(F32)
        p2[:, :, :, at] = both.astype(BF16).reshape(4, 4, PAIR, widths[i])
        if (i + 1) * part == CUT:
            for d in (2, 1, 3):
                a2_copy(d).start()
    for d in (2, 1, 3):
        b2_copy(d).start()

    row16 = iota((PAIR, 128), 0)

    def column(load):
        got = jnp.zeros((PAIR, 128), jnp.int32)
        for i in range(PAIR):
            got = jnp.where(row16 == i, load(c * PAIR + i), got)
        return got

    first = column(lambda i: routes[0, i])
    second = column(lambda i: routes[1, i])
    ten_rows = column(lambda i: tenants[i])
    xa = xbuf[0, pl.ds(own_rows, PAIR), :].astype(F32)
    xb = xbuf[1, pl.ds(own_rows, PAIR), :].astype(F32)
    own_scale = inverse_norm(xa[:, HALF:] + xb[:, HALF:])
    rt = rout[...].astype(F32)
    other = first + second - z
    mine = jnp.zeros((PAIR, 128), F32)
    theirs = jnp.zeros((PAIR, 128), F32)
    for e in range(EXP):
        logit = jnp.sum(xa[:, :HALF] * rt[e : e + 1, :HALF], axis=1, keepdims=True)
        logit = logit + jnp.sum(xb[:, :HALF] * rt[e : e + 1, HALF:], axis=1, keepdims=True)
        logit = logit * own_scale
        mine = jnp.where(z == e, logit, mine)
        theirs = jnp.where(other == e, logit, theirs)
    share = 1.0 / (1.0 + jnp.exp(theirs - mine))
    share = jnp.where((first == z) | (second == z), share, 0.0)[:, 0:1]

    def a2_wait(d):
        xx = lax.rem(x + d, 4)
        remote(
            p2.at[:, x, :, pl.ds(0, CUT)], r2a.at[xx], as2.at[0], ar2.at[xx],
            (y * 4 + xx) * 2 + k, z,
        ).wait_recv()
        return xx

    def b2_wait(d):
        yy = lax.rem(y + d, 4)
        remote(
            p2.at[y, :, :, pl.ds(CUT, EXT - CUT)], r2b.at[yy], bs2.at[0], br2.at[yy],
            (yy * 4 + x) * 2 + k, z,
        ).wait_recv()
        return yy

    total = p2[:, x, :, 0:CUT].astype(F32)
    for d in (1, 3, 2):
        total = total + r2a[a2_wait(d)].astype(F32)
    p3a[...] = total.astype(BF16)

    def a3_copy(d):
        yy = lax.rem(y + d, 4)
        return remote(p3a.at[yy], r3a.at[y], as3.at[d], ar3.at[y], (yy * 4 + x) * 2 + k, z)

    for d in (2, 1, 3):
        a3_copy(d).start()
    total = p2[y, :, :, CUT:].astype(F32)
    for d in (1, 3, 2):
        total = total + r2b[b2_wait(d)].astype(F32)
    p3b[...] = total.astype(BF16)

    def b3_copy(d):
        xx = lax.rem(x + d, 4)
        return remote(p3b.at[xx], r3b.at[x], bs3.at[d], br3.at[x], (y * 4 + xx) * 2 + k, z)

    for d in (2, 1, 3):
        b3_copy(d).start()

    sum_a = p3a[y].astype(F32)
    for d in (1, 3, 2):
        yy = lax.rem(y + d, 4)
        remote(p3a.at[y], r3a.at[yy], as3.at[0], ar3.at[yy], (yy * 4 + x) * 2 + k, z).wait_recv()
        sum_a = sum_a + r3a[yy].astype(F32)
    sum_b = p3b[x].astype(F32)
    for d in (1, 3, 2):
        xx = lax.rem(x + d, 4)
        remote(p3b.at[x], r3b.at[xx], bs3.at[0], br3.at[xx], (y * 4 + xx) * 2 + k, z).wait_recv()
        sum_b = sum_b + r3b[xx].astype(F32)

    up_copy().wait_recv()
    low = sum_b[:, HALF - CUT :]
    low = jnp.where(lax.div(iota((PAIR, 128), 1), 16) == lax.rem(ten_rows, 8), low, 0.0)
    adapter = dot(low.astype(BF16), upb[...])
    contrib = (jnp.concatenate([sum_a, sum_b[:, : HALF - CUT]], axis=1) + adapter) * share

    def f_copy(kk, j):
        slot = kk * 2 + j
        return remote(fsnd.at[slot], fbuf.at[z], fs.at[slot], fr.at[z], c * 2 + kk, 2 * k + j)

    for kk in range(2):
        for j in range(2):
            slot = kk * 2 + j
            rows = contrib[kk * ROWS : (kk + 1) * ROWS, j * QUARTER : (j + 1) * QUARTER]
            fsnd[slot] = jnp.concatenate([rows[:, :cols], rows[:, cols:]], axis=0).astype(BF16)
            is_self = (kk == k) & (2 * k + j == z)

            @pl.when(~is_self)
            def _():
                f_copy(kk, j).start()

            @pl.when(is_self)
            def _():
                fbuf[z] = fsnd[slot]

    for e in range(EXP):

        @pl.when(~((to_core == k) & (e == z)))
        def _():
            remote(fsnd.at[0], fbuf.at[e], fs.at[0], fr.at[e], c * 2 + to_core, e).wait_recv()

    got = fbuf[...].astype(F32)
    got = got[0] + got[1] + got[2] + got[3]
    got = jnp.concatenate([got[:ROWS], got[ROWS:]], axis=1)
    out[...] = (resid_ref[...] + got).astype(BF16)

    q_sib().wait_send()
    each(CHIPS, lambda i: q_send(i).wait_send(), 1)
    up_copy().wait_send()

    def sends_of_chip(i):
        @pl.when(i != c)
        def _():
            q_copy(i * 2 + k, sib, qf.at[i]).wait_send()
            x_copy(k, i, sib, xf.at[i]).wait_send()

    each(CHIPS, sends_of_chip)

    def sends_of_block(i):
        @pl.when(i != s)
        def _():
            p_copy(i, i).wait_send()

    each(SEQ, sends_of_block)
    for d in range(1, EXP):
        r_copy(d).wait_send()

    @pl.when(to_core != k)
    def _():
        r_copy(0).wait_send()

    x_copy(k, c, sib, xs.at[0]).wait_send()
    each(CHIPS, lambda i: x_copy(k, c, chip_at(i) * 2 + k, xs.at[i]).wait_send(), 1)
    for i in range(n_parts):
        s1_copy(i).wait_send()
    for d in (2, 1, 3):
        a2_copy(d).wait_send()
        b2_copy(d).wait_send()
        a3_copy(d).wait_send()
        b3_copy(d).wait_send()
    for kk in range(2):
        for j in range(2):

            @pl.when(~((kk == k) & (2 * k + j == z)))
            def _():
                f_copy(kk, j).wait_send()


def on_device(
    hidden, queries, suffix_row_keys, suffix_row_values, prefix_cached_keys, prefix_cached_values,
    expert_norm_gain, router, gate_weight, up_weight, down_weight, adapter_down_maps,
    adapter_up_maps, routes, tenants, lengths,
):
    vmem = pl.BlockSpec(memory_space=pltpu.VMEM)
    smem = pl.BlockSpec(memory_space=pltpu.SMEM)
    hbm = pl.BlockSpec(memory_space=pl.ANY)
    dma = pltpu.SemaphoreType.DMA
    scratch = [
        pltpu.VMEM((KV, SEQ, QB, HEAD), BF16),
        pltpu.VMEM((PREFIX, KV * HEAD), BF16),
        pltpu.VMEM((KV, PREFIX, 2 * HEAD), BF16),
        pltpu.VMEM((SEQ, MSG, HEAD), BF16),
        pltpu.VMEM((SEQ, MSG, HEAD), BF16),
        pltpu.VMEM((HEADS, ROWS, HEAD), F32),
        pltpu.VMEM((ROWS, 128), F32),
        pltpu.VMEM((PAIR, QUARTER // 2), BF16),
        pltpu.VMEM((4, PAIR, QUARTER // 2), BF16),
        pltpu.VMEM((2, TOTAL, EXT), BF16),
        pltpu.VMEM((WIDTH, UNITS), BF16),
        pltpu.VMEM((WIDTH, UNITS), BF16),
        pltpu.VMEM((UNITS, WIDTH), BF16),
        pltpu.VMEM((1024, UNITS), BF16),
        pltpu.VMEM((128, HALF), BF16),
        pltpu.VMEM((TOTAL, UNITS), F32),
        pltpu.VMEM((TOTAL, UNITS), F32),
        pltpu.VMEM((TOTAL, EXT), BF16),
        pltpu.VMEM((TOTAL, EXT), BF16),
        pltpu.VMEM((TOTAL, EXT), F32),
        pltpu.VMEM((4, 4, PAIR, EXT), BF16),
        pltpu.VMEM((4, 4, PAIR, CUT), BF16),
        pltpu.VMEM((4, 4, PAIR, EXT - CUT), BF16),
        pltpu.VMEM((4, PAIR, CUT), BF16),
        pltpu.VMEM((4, PAIR, EXT - CUT), BF16),
        pltpu.VMEM((4, PAIR, CUT), BF16),
        pltpu.VMEM((4, PAIR, EXT - CUT), BF16),
        pltpu.VMEM((4, PAIR, QUARTER // 2), BF16),
        pltpu.VMEM((EXP, PAIR, QUARTER // 2), BF16),
        pltpu.VMEM((ROWS, QUARTER), F32),
        dma((9,)),
        dma((CHIPS,)),
        dma((CHIPS,)),
        dma((SEQ,)),
        dma((SEQ,)),
        dma((SEQ,)),
        dma((EXP,)),
        dma((4,)),
        dma((CHIPS,)),
        dma((CHIPS,)),
        dma((2, CHIPS)),
        dma((1,)),
        dma((1,)),
        dma((4,)),
        dma((4,)),
    ] + [dma((4,)) for _ in range(10)]
    return pl.pallas_call(
        kernel,
        out_shape=jax.ShapeDtypeStruct((ROWS, QUARTER), BF16),
        in_specs=[vmem, vmem, vmem, vmem, hbm, hbm, vmem, vmem, hbm, hbm, hbm, hbm, hbm, smem, smem, smem],
        out_specs=vmem,
        scratch_shapes=scratch,
        compiler_params=pltpu.CompilerParams(
            collective_id=0, has_side_effects=True, vmem_limit_bytes=58 * 1024 * 1024
        ),
        cost_estimate=pl.CostEstimate(flops=5 * 10**9, bytes_accessed=13 * 2**20, transcendentals=7 * 10**6),
        name="layer",
    )(
        hidden, queries, suffix_row_keys, suffix_row_values, prefix_cached_keys,
        prefix_cached_values, expert_norm_gain.reshape(1, WIDTH), router.T,
        gate_weight.reshape(WIDTH, UNITS), up_weight.reshape(WIDTH, UNITS),
        down_weight.reshape(UNITS, WIDTH), adapter_down_maps.reshape(-1, UNITS),
        adapter_up_maps.reshape(-1, WIDTH), routes.T, tenants, lengths,
    )


def solution(mesh):
    in_specs = (
        P("seq", "exp"),
        P("seq", "exp"),
        P("seq", "exp"),
        P("seq", "exp"),
        P("seq", "exp"),
        P("seq", "exp"),
        P(),
        P(),
        P("exp", None, "seq"),
        P("exp", None, "seq"),
        P("exp", "seq", None),
        P(None, "exp", None, "seq"),
        P("seq", "exp", None, None),
        P(),
        P(),
        P(),
    )
    return jax.shard_map(
        on_device, mesh=mesh, in_specs=in_specs, out_specs=P("seq", "exp"), check_vma=False
    )
```

```python
import functools

import jax
import jax.numpy as jnp
from jax import lax
from jax.experimental import pallas as pl
from jax.experimental.pallas import tpu as pltpu
from jax.sharding import PartitionSpec as P

MESH = pl.DeviceIdType.MESH
F32 = jnp.float32
BF16 = jnp.bfloat16

HEAD = 128
GROUP = 6
KV = 2
HEADS = KV * GROUP
ROWS = 8
SEQ = 32
EXP = 4
CHIPS = SEQ // 2
PAIR = 2 * ROWS
TOTAL = SEQ * ROWS
WIDTH = 6144
HALF = WIDTH // 2
QUARTER = WIDTH // EXP
PREFIX = 2048
UNITS = 256
QB = GROUP * ROWS
BLK = 2 * QB
MSG = BLK + 16
PART = GROUP * HEAD
THIRD = PART // 3
KEYS = 512
EXT = HALF + 128
CUT = 1536
NORM_EPS = 1e-05
LOG2E = 1.4426950408889634
SCALE2 = HEAD**-0.5 * LOG2E


def dot(a, b):
    return jnp.dot(a, b, preferred_element_type=F32)


def dot_t(a, b):
    return lax.dot_general(a, b, (((1,), (1,)), ((), ())), preferred_element_type=F32)


def iota(shape, dim):
    return lax.broadcasted_iota(jnp.int32, shape, dim)


def three_parts(v):
    high = v.astype(BF16).astype(F32)
    rest = v - high
    mid = rest.astype(BF16).astype(F32)
    low = rest - mid
    ax = v.ndim - 1
    return high + pltpu.roll(mid, 16, ax) + pltpu.roll(low, 32, ax)


def whole_of(p):
    ax = p.ndim - 1
    return p + pltpu.roll(p, 128 - 16, ax) + pltpu.roll(p, 128 - 32, ax)


N_SMALL = 6


def kernel(
    hid, qry, skey, sval, pk, pv, gain, rout, wg, wu, wd, adn, aup, routes, tenants, lengths,
    out,
    hid_v, qry_v, skey_v, sval_v, rout_v, gain_v, gainf, msnd, pairb, qall, kbuf, vext, sbuf, pbuf,
    suf_o, suf_l, xb, wgb, wub, wdb, adnb, upb,
    accg, accu, accs, s1snd, s1rcv, own, p2, r2a, r2b, p3a, p3b, r3a, r3b, fsnd, fbuf,
    lsem, ms, mr, ks, kr, qs, qr, ps, pr, gs, gr, hs, hr, ups, upr, s1s, s1r,
    as2, ar2, bs2, br2, as3, ar3, bs3, br3, fs, fr,
):
    s = lax.axis_index("seq")
    z = lax.axis_index("exp")
    k = lax.rem(s, 2)
    c = lax.div(s, 2)
    x = lax.rem(c, 4)
    y = lax.div(c, 4)
    sib = s + 1 - 2 * k
    sent = []

    def remote(src, dst, ssem, rsem, seq, exp):
        return pltpu.make_async_remote_copy(
            src_ref=src, dst_ref=dst, send_sem=ssem, recv_sem=rsem,
            device_id=(seq, exp), device_id_type=MESH,
        )

    def each(n, body, first=0):
        def step(i, carry):
            body(i)
            return carry

        lax.fori_loop(first, n, step, 0)

    def chip_at(i):
        return lax.rem(y + 4 - i // 4, 4) * 4 + lax.rem(x + i % 4, 4)

    barrier = pltpu.get_barrier_semaphore()

    def greet(seq, exp):
        pl.semaphore_signal(barrier, inc=1, device_id=(seq, exp), device_id_type=MESH)

    greet(sib, z)
    each(CHIPS, lambda i: greet(chip_at(i) * 2 + k, z), 1)
    for d in range(1, EXP):
        for seq in (s, sib):
            greet(seq, lax.rem(z + d, EXP))

    k_half = pl.multiple_of(k * HALF, HALF)
    own_head = pl.ds(pl.multiple_of(k * HEAD, HEAD), HEAD)
    sib_head = pl.ds(pl.multiple_of(HEAD - k * HEAD, HEAD), HEAD)
    up_row = pl.multiple_of(64 * lax.rem(c, 2) + 32 * k, 32)
    loads = [
        (qry, qry_v),
        (hid, hid_v),
        (skey, skey_v),
        (sval, sval_v),
        (gain, gain_v),
        (rout, rout_v),
        (pk.at[:, own_head], kbuf.at[pl.ds(0, PREFIX), :]),
        (pv.at[:, own_head], vext.at[pl.ds(0, PREFIX), pl.ds(0, HEAD)]),
        (wg, wgb),
        (wu, wub),
        (wd, wdb),
        (adn, adnb),
        (aup.at[:, pl.ds(k_half, HALF)], upb.at[pl.ds(up_row, 32), :]),
    ]
    loads = [pltpu.make_async_copy(a, b, lsem.at[i]) for i, (a, b) in enumerate(loads)]
    for cp in loads:
        cp.start()
    vext[:, HEAD:] = jnp.ones((2 * PREFIX, HEAD), BF16)
    other_rows = pl.multiple_of(64 - 64 * lax.rem(c, 2), 64)
    upb[pl.ds(other_rows, 64), :] = jnp.zeros((64, HALF), BF16)
    for cp in loads[:N_SMALL]:
        cp.wait()
    gainf[...] = gain_v[...].astype(F32).reshape(1, WIDTH)

    q, h = qry_v[...].astype(F32), hid_v[...].astype(F32)
    kv = [skey_v[...].astype(F32), sval_v[...].astype(F32)]
    by_head = []
    for g in range(KV):
        tiles = [a[:, (g * GROUP + j) * HEAD : (g * GROUP + j + 1) * HEAD] for a in (q, h) for j in range(GROUP)]
        tiles = tiles + [a[:, g * HEAD : (g + 1) * HEAD] for a in kv]
        by_head.append(jnp.concatenate(tiles, axis=0))
    pairb[k] = jnp.where(k == 0, by_head[0], by_head[1]).astype(BF16)
    msnd[...] = jnp.where(k == 0, by_head[1], by_head[0]).astype(BF16)
    pl.semaphore_wait(barrier, CHIPS + 2 * (EXP - 1))

    m_copy = remote(msnd, pairb.at[k], ms.at[0], mr.at[0], sib, z)
    m_copy.start()
    kv_copies = [
        remote(pk.at[:, sib_head], kbuf.at[pl.ds(PREFIX, PREFIX), :], ks.at[0], kr.at[0], sib, z),
        remote(pv.at[:, sib_head], vext.at[pl.ds(PREFIX, PREFIX), pl.ds(0, HEAD)], ks.at[1], kr.at[1], sib, z),
    ]
    for cp in kv_copies:
        cp.start()
    sent.append(lambda: [cp.wait_send() for cp in (m_copy, *kv_copies)])
    remote(msnd, pairb.at[1 - k], ms.at[0], mr.at[0], sib, z).wait_recv()

    for kk in range(2):
        qall[c, kk * QB : (kk + 1) * QB, :] = pairb[kk, 0:QB, :]

    def q_send(i):
        return remote(qall.at[c], qall.at[c], qs.at[i], qr.at[c], chip_at(i) * 2 + k, z)

    each(CHIPS, lambda i: q_send(i).start(), 1)
    sent.append(lambda: each(CHIPS, lambda i: q_send(i).wait_send(), 1))
    up_other = pl.multiple_of(HALF - k * HALF, HALF)

    def up_copy():
        return remote(
            aup.at[:, pl.ds(up_other, HALF)], upb.at[pl.ds(up_row, 32), :], ups.at[0], upr.at[0], sib, z
        )

    up_copy().start()
    sent.append(lambda: up_copy().wait_send())

    row16 = iota((PAIR, 128), 0)
    lane16 = iota((PAIR, 128), 1)
    ten = [tenants[c * PAIR + i] for i in range(PAIR)]
    pos = []
    for i in range(PAIR):
        p = jnp.int32(0)
        for j in range(i // ROWS * ROWS, i):
            p = p + (ten[i] == ten[j]).astype(jnp.int32)
        pos.append(p)
    lens = [lengths[t] for t in ten]

    def spread(values, at):
        got = jnp.full((PAIR, 128), -1, jnp.int32)
        for i, v in enumerate(values):
            got = jnp.where(at == i, v, got)
        return got

    ten_rows = spread(ten, row16)
    pos_c = spread(pos, lane16)
    visible = (lane16 < PAIR) & (ten_rows == spread(ten, lane16))
    visible = visible & (pos_c <= spread(pos, row16)) & (pos_c < spread(lens, row16))
    pairs = [pairb[kk, BLK:, :].astype(F32) for kk in range(2)]
    fill = jnp.zeros((128 - PAIR, HEAD), F32)
    keys = jnp.concatenate([pairs[0][:ROWS], pairs[1][:ROWS], fill], axis=0).astype(BF16)
    values = jnp.concatenate([pairs[0][ROWS:], pairs[1][ROWS:], fill], axis=0).astype(BF16)
    for kk in range(2):
        seen = visible[kk * ROWS : (kk + 1) * ROWS]
        seen = jnp.broadcast_to(seen[None], (GROUP, ROWS, 128))
        sc = dot_t(pairb[kk, 0:QB, :], keys).reshape(GROUP, ROWS, 128)
        sc = jnp.where(seen, sc, -1e30)
        m = jnp.max(sc, axis=2, keepdims=True)
        w = jnp.where(seen, jnp.exp2((sc - m) * SCALE2), 0.0)
        mass = jnp.sum(w, axis=2, keepdims=True)
        acc = dot(w.reshape(QB, 128).astype(BF16), values).reshape(GROUP, ROWS, HEAD)
        suf_o[kk] = acc / mass
        lse = jnp.broadcast_to(m * SCALE2 + jnp.log2(mass), (GROUP, ROWS, 128))
        stat = jnp.zeros((ROWS, 128), F32)
        for j in range(GROUP):
            stat = jnp.where(lane16[:ROWS] == j, lse[j], stat)
        suf_l[kk * ROWS : (kk + 1) * ROWS, :] = stat

    for cp in loads[N_SMALL : N_SMALL + 2]:
        cp.wait()
    for cp in kv_copies:
        cp.wait_recv()

    def p_copy(chip):
        return remote(sbuf.at[chip], pbuf.at[c], ps.at[chip], pr.at[c], chip * 2 + k, z)

    def attend(dy):
        yy = lax.rem(y + dy, 4)

        def q_wait(i):
            chip = yy * 4 + i

            @pl.when(chip != c)
            def _():
                remote(qall.at[c], qall.at[chip], qs.at[0], qr.at[chip], chip * 2 + k, z).wait_recv()

        each(4, q_wait)
        qs_ = qall[pl.ds(yy * 4, 4)].reshape(4 * BLK, HEAD)
        coming = dot_t(qs_, kbuf[0:KEYS, :])
        m = acc = None
        for at in range(0, 2 * PREFIX, KEYS):
            sc = coming * SCALE2
            if at + KEYS < 2 * PREFIX:
                coming = dot_t(qs_, kbuf[at + KEYS : at + 2 * KEYS, :])
            top = jnp.max(sc, axis=1, keepdims=True)
            top = top if m is None else jnp.maximum(m, top)
            got = dot(jnp.exp2(sc - top).astype(BF16), vext[at : at + KEYS, :])
            acc = got if m is None else acc * jnp.exp2(m - top) + got
            m = top
        mass = acc[:, HEAD:]
        o = acc[:, :HEAD] / mass
        sbuf[pl.ds(yy * 4, 4), 0:BLK, :] = o.astype(BF16).reshape(4, BLK, HEAD)
        lse = (m + jnp.log2(mass)).reshape(8, GROUP, ROWS, 128)
        lane = iota((8, ROWS, 128), 2)
        stat = jnp.zeros((8, ROWS, 128), F32)
        for j in range(GROUP):
            stat = jnp.where(lane == j, lse[:, j], stat)
        sbuf[pl.ds(yy * 4, 4), BLK:, :] = three_parts(stat).reshape(4, PAIR, 128).astype(BF16)

        def p_send(i):
            chip = yy * 4 + lax.rem(x + i, 4)

            @pl.when(chip != c)
            def _():
                p_copy(chip).start()

        each(4, p_send)

    each(4, attend)

    def partials_sent():
        def one(i):
            @pl.when(i != c)
            def _():
                p_copy(i).wait_send()

        each(CHIPS, one)

    sent.append(partials_sent)
    pbuf[c] = sbuf[c]

    def p_wait(i):
        @pl.when(i != c)
        def _():
            remote(sbuf.at[i], pbuf.at[i], ps.at[i], pr.at[i], i * 2 + k, z).wait_recv()

    each(CHIPS, p_wait)
    lses = whole_of(pbuf[:, BLK:, :].astype(F32))
    top = jnp.maximum(jnp.max(lses, axis=0), suf_l[...])
    shares = jnp.exp2(lses - top[None])
    suf_share = jnp.exp2(suf_l[...] - top)
    inverse = 1.0 / (jnp.sum(shares, axis=0) + suf_share)
    suf_share = suf_share * inverse
    att = {}
    for kk in range(2):
        rows = slice(kk * ROWS, (kk + 1) * ROWS)
        hidden = pairb[kk, QB : 2 * QB, :].astype(F32)
        for j in range(GROUP):
            att[kk, j] = hidden[j * ROWS : (j + 1) * ROWS] + suf_share[rows, j : j + 1] * suf_o[kk, j]
    for i in range(CHIPS):
        part = pbuf[i, 0:BLK, :].astype(F32)
        share = shares[i] * inverse
        for kk in range(2):
            rows = slice(kk * ROWS, (kk + 1) * ROWS)
            for j in range(GROUP):
                at = (kk * GROUP + j) * ROWS
                att[kk, j] = att[kk, j] + share[rows, j : j + 1] * part[at : at + ROWS]
    resid = [jnp.concatenate([att[kk, j] for j in range(GROUP)], axis=1) for kk in range(2)]
    xb[k, z, y, x] = jnp.concatenate(resid, axis=0).astype(BF16)

    here = {"x": x, "y": y, "z": z}
    orders = ("xyz", "yzx", "zxy")

    def region(t, step, **at):
        at = {**here, **at}
        index = [pl.ds(0, 4) if a in orders[t][:step] else at[a] for a in "zyx"]
        return xb.at[(k, *index, slice(None), pl.ds(t * THIRD, THIRD))]

    def peer(axis, d):
        at = {**here, axis: lax.rem(here[axis] + d, 4)}
        return at[axis], (at["y"] * 4 + at["x"]) * 2 + k, at["z"]

    def g_send(t, step, d):
        axis = orders[t][step]
        _, seq, exp = peer(axis, d)
        block = region(t, step)
        return remote(block, block, gs.at[t, step, d], gr.at[t, step, here[axis]], seq, exp)

    def g_wait(t, step, d):
        axis = orders[t][step]
        there, seq, exp = peer(axis, d)
        block = region(t, step, **{axis: there})
        remote(block, block, gs.at[t, step, 0], gr.at[t, step, there], seq, exp).wait_recv()

    def h_copy(t, there):
        block = region(t, 2, **{orders[t][2]: there})
        return remote(block, block, hs.at[t, there], hr.at[t, there], sib, z)

    for step in range(3):
        for t in range(3):
            if step:
                for d in (1, 3, 2):
                    g_wait(t, step - 1, d)
            for d in (2, 1, 3):
                g_send(t, step, d).start()
    for t in range(3):
        h_copy(t, here[orders[t][2]]).start()
    for d in (1, 3, 2):
        for t in range(3):
            g_wait(t, 2, d)
            h_copy(t, peer(orders[t][2], d)[0]).start()

    def rows_sent():
        for t in range(3):
            for step in range(3):
                for d in (1, 2, 3):
                    g_send(t, step, d).wait_send()
            for there in range(4):
                h_copy(t, there).wait_send()

    sent.append(rows_sent)

    for cp in loads[N_SMALL + 2 : N_SMALL + 4]:
        cp.wait()
    accg[...] = jnp.zeros_like(accg)
    accu[...] = jnp.zeros_like(accu)
    accs[...] = jnp.zeros_like(accs)

    def project(core):
        def one(zz):
            at = pl.multiple_of(zz * QUARTER + core * PART, PART)
            rows = xb[core, zz].reshape(TOTAL, PART).astype(F32)
            squares = rows * rows
            total = squares[:, 0:128]
            for i in range(1, PART // 128):
                total = total + squares[:, i * 128 : (i + 1) * 128]
            accs[...] = accs[...] + total
            rows = (rows * gainf[:, pl.ds(at, PART)]).astype(BF16)
            accg[...] = accg[...] + dot(rows, wgb[pl.ds(at, PART), :])
            accu[...] = accu[...] + dot(rows, wub[pl.ds(at, PART), :])

        each(EXP, one)

    project(k)
    for t in range(3):
        for there in range(4):
            block = xb.at[(1 - k, *[there if a == orders[t][2] else pl.ds(0, 4) for a in "zyx"], slice(None), pl.ds(t * THIRD, THIRD))]
            remote(block, block, hs.at[t, there], hr.at[t, there], sib, z).wait_recv()
    project(1 - k)
    scale = lax.rsqrt(jnp.sum(accs[...], axis=1, keepdims=True) / WIDTH + NORM_EPS)
    gate = accg[...] * scale
    units = (gate / (1.0 + jnp.exp(-gate)) * (accu[...] * scale)).astype(BF16)

    for cp in loads[N_SMALL + 4 :]:
        cp.wait()
    low = [
        dot_t(units[i * 32 : (i + 1) * 32], adnb[i * 128 : (i + 1) * 128, :])
        for i in range(CHIPS // 2)
    ]
    low = jnp.concatenate(low, axis=0)
    s1snd[:, HALF:] = low.astype(BF16)
    own[:, HALF:] = low

    part = 768
    n_parts = HALF // part
    widths = [part] * (n_parts - 1) + [part + 128]

    def s1_copy(i):
        at = pl.ds(i * part, widths[i])
        return remote(s1snd.at[:, at], s1rcv.at[:, at], s1s.at[i], s1r.at[i], sib, z)

    def down(half, i):
        at = pl.multiple_of(half * HALF + i * part, 128)
        return dot(units, wdb[:, pl.ds(at, part)])

    for i in range(n_parts):
        s1snd[:, i * part : (i + 1) * part] = down(1 - k, i).astype(BF16)
        s1_copy(i).start()
    for i in range(n_parts):
        own[:, i * part : (i + 1) * part] = down(k, i)
    sent.append(lambda: [s1_copy(i).wait_send() for i in range(n_parts)])

    def a2_copy(d):
        xx = lax.rem(x + d, 4)
        return remote(
            p2.at[:, xx, :, pl.ds(0, CUT)], r2a.at[x], as2.at[d], ar2.at[x], (y * 4 + xx) * 2 + k, z
        )

    def b2_copy(d):
        yy = lax.rem(y + d, 4)
        return remote(
            p2.at[yy, :, :, pl.ds(CUT, EXT - CUT)], r2b.at[y], bs2.at[d], br2.at[y],
            (yy * 4 + x) * 2 + k, z,
        )

    for i in range(n_parts):
        s1_copy(i).wait_recv()
        at = slice(i * part, i * part + widths[i])
        both = own[:, at] + s1rcv[:, at].astype(F32)
        p2[:, :, :, at] = both.astype(BF16).reshape(4, 4, PAIR, widths[i])
        if (i + 1) * part == CUT:
            for d in (2, 1, 3):
                a2_copy(d).start()
    for d in (2, 1, 3):
        b2_copy(d).start()
    sent.append(lambda: [copy(d).wait_send() for copy in (a2_copy, b2_copy) for d in (2, 1, 3)])

    def column(load):
        got = jnp.zeros((PAIR, 128), jnp.int32)
        for i in range(PAIR):
            got = jnp.where(row16 == i, load(c * PAIR + i), got)
        return got

    first = column(lambda i: routes[0, i])
    second = column(lambda i: routes[1, i])
    other = first + second - z
    logits = [jnp.zeros((PAIR, 1), F32)] * EXP
    squares = jnp.zeros((PAIR, 1), F32)
    for kk in range(2):
        for zz in range(EXP):
            at = slice(zz * QUARTER + kk * PART, zz * QUARTER + (kk + 1) * PART)
            rows = xb[kk, zz, y, x].astype(F32)
            squares = squares + jnp.sum(rows * rows, axis=1, keepdims=True)
            rows = (rows * gainf[:, at]).astype(BF16).astype(F32)
            for e in range(EXP):
                by = rout_v[e : e + 1, at].astype(F32)
                logits[e] = logits[e] + jnp.sum(rows * by, axis=1, keepdims=True)
    own_scale = lax.rsqrt(squares / WIDTH + NORM_EPS)
    mine = jnp.zeros((PAIR, 128), F32)
    theirs = jnp.zeros((PAIR, 128), F32)
    for e in range(EXP):
        logit = logits[e] * own_scale
        mine = jnp.where(z == e, logit, mine)
        theirs = jnp.where(other == e, logit, theirs)
    share = 1.0 / (1.0 + jnp.exp(theirs - mine))
    share = jnp.where((first == z) | (second == z), share, 0.0)[:, 0:1]

    def a2_wait(d):
        xx = lax.rem(x + d, 4)
        remote(
            p2.at[:, x, :, pl.ds(0, CUT)], r2a.at[xx], as2.at[0], ar2.at[xx],
            (y * 4 + xx) * 2 + k, z,
        ).wait_recv()
        return xx

    def b2_wait(d):
        yy = lax.rem(y + d, 4)
        remote(
            p2.at[y, :, :, pl.ds(CUT, EXT - CUT)], r2b.at[yy], bs2.at[0], br2.at[yy],
            (yy * 4 + x) * 2 + k, z,
        ).wait_recv()
        return yy

    total = p2[:, x, :, 0:CUT].astype(F32)
    for d in (1, 3, 2):
        total = total + r2a[a2_wait(d)].astype(F32)
    p3a[...] = total.astype(BF16)

    def a3_copy(d):
        yy = lax.rem(y + d, 4)
        return remote(p3a.at[yy], r3a.at[y], as3.at[d], ar3.at[y], (yy * 4 + x) * 2 + k, z)

    for d in (2, 1, 3):
        a3_copy(d).start()
    total = p2[y, :, :, CUT:].astype(F32)
    for d in (1, 3, 2):
        total = total + r2b[b2_wait(d)].astype(F32)
    p3b[...] = total.astype(BF16)

    def b3_copy(d):
        xx = lax.rem(x + d, 4)
        return remote(p3b.at[xx], r3b.at[x], bs3.at[d], br3.at[x], (y * 4 + xx) * 2 + k, z)

    for d in (2, 1, 3):
        b3_copy(d).start()
    sent.append(lambda: [copy(d).wait_send() for copy in (a3_copy, b3_copy) for d in (2, 1, 3)])

    sum_a = p3a[y].astype(F32)
    for d in (1, 3, 2):
        yy = lax.rem(y + d, 4)
        remote(p3a.at[y], r3a.at[yy], as3.at[0], ar3.at[yy], (yy * 4 + x) * 2 + k, z).wait_recv()
        sum_a = sum_a + r3a[yy].astype(F32)
    sum_b = p3b[x].astype(F32)
    for d in (1, 3, 2):
        xx = lax.rem(x + d, 4)
        remote(p3b.at[x], r3b.at[xx], bs3.at[0], br3.at[xx], (y * 4 + xx) * 2 + k, z).wait_recv()
        sum_b = sum_b + r3b[xx].astype(F32)

    up_copy().wait_recv()
    low = sum_b[:, HALF - CUT :]
    low = jnp.where(lax.div(iota((PAIR, 128), 1), 16) == lax.rem(ten_rows, 8), low, 0.0)
    adapter = dot(low.astype(BF16), upb[...])
    contrib = (jnp.concatenate([sum_a, sum_b[:, : HALF - CUT]], axis=1) + adapter) * share

    def f_copy(kk, j):
        slot = kk * 2 + j
        return remote(fsnd.at[slot], fbuf.at[z], fs.at[slot], fr.at[z], c * 2 + kk, 2 * k + j)

    for kk in range(2):
        for j in range(2):
            slot = kk * 2 + j
            rows = contrib[kk * ROWS : (kk + 1) * ROWS, j * QUARTER : (j + 1) * QUARTER]
            fsnd[slot] = jnp.concatenate([rows[:, :PART], rows[:, PART:]], axis=0).astype(BF16)
            is_self = (kk == k) & (2 * k + j == z)

            @pl.when(~is_self)
            def _():
                f_copy(kk, j).start()

            @pl.when(is_self)
            def _():
                fbuf[z] = fsnd[slot]

    to_core = lax.div(z, 2)
    for e in range(EXP):

        @pl.when(~((to_core == k) & (e == z)))
        def _():
            remote(fsnd.at[0], fbuf.at[e], fs.at[0], fr.at[e], c * 2 + to_core, e).wait_recv()

    def final_sent():
        for kk in range(2):
            for j in range(2):

                @pl.when(~((kk == k) & (2 * k + j == z)))
                def _():
                    f_copy(kk, j).wait_send()

    sent.append(final_sent)
    got = fbuf[...].astype(F32)
    got = got[0] + got[1] + got[2] + got[3]
    got = jnp.concatenate([got[:ROWS], got[ROWS:]], axis=1)
    resid = [xb[kk, z, y, x].astype(F32) for kk in range(2)]
    resid = [jnp.where(k == 0, r[:ROWS], r[ROWS:]) for r in resid]
    out[...] = (jnp.concatenate(resid, axis=1) + got).astype(BF16)

    for wait in sent:
        wait()


def on_device(
    hidden, queries, suffix_row_keys, suffix_row_values, prefix_cached_keys, prefix_cached_values,
    expert_norm_gain, router, gate_weight, up_weight, down_weight, adapter_down_maps,
    adapter_up_maps, routes, tenants, lengths,
):
    vmem = pl.BlockSpec(memory_space=pltpu.VMEM)
    smem = pl.BlockSpec(memory_space=pltpu.SMEM)
    hbm = pl.BlockSpec(memory_space=pl.ANY)
    dma = pltpu.SemaphoreType.DMA
    scratch = [
        pltpu.VMEM((ROWS, QUARTER), BF16),
        pltpu.VMEM((ROWS, QUARTER), BF16),
        pltpu.VMEM((ROWS, KV * HEAD), BF16),
        pltpu.VMEM((ROWS, KV * HEAD), BF16),
        pltpu.VMEM((EXP, WIDTH), BF16),
        pltpu.VMEM((WIDTH,), BF16),
        pltpu.VMEM((1, WIDTH), F32),
        pltpu.VMEM((MSG, HEAD), BF16),
        pltpu.VMEM((2, MSG, HEAD), BF16),
        pltpu.VMEM((CHIPS, BLK, HEAD), BF16),
        pltpu.VMEM((2 * PREFIX, HEAD), BF16),
        pltpu.VMEM((2 * PREFIX, 2 * HEAD), BF16),
        pltpu.VMEM((CHIPS, MSG, HEAD), BF16),
        pltpu.VMEM((CHIPS, MSG, HEAD), BF16),
        pltpu.VMEM((2, GROUP, ROWS, HEAD), F32),
        pltpu.VMEM((PAIR, 128), F32),
        pltpu.VMEM((2, EXP, 4, 4, PAIR, PART), BF16),
        pltpu.VMEM((WIDTH, UNITS), BF16),
        pltpu.VMEM((WIDTH, UNITS), BF16),
        pltpu.VMEM((UNITS, WIDTH), BF16),
        pltpu.VMEM((1024, UNITS), BF16),
        pltpu.VMEM((128, HALF), BF16),
        pltpu.VMEM((TOTAL, UNITS), F32),
        pltpu.VMEM((TOTAL, UNITS), F32),
        pltpu.VMEM((TOTAL, 128), F32),
        pltpu.VMEM((TOTAL, EXT), BF16),
        pltpu.VMEM((TOTAL, EXT), BF16),
        pltpu.VMEM((TOTAL, EXT), F32),
        pltpu.VMEM((4, 4, PAIR, EXT), BF16),
        pltpu.VMEM((4, 4, PAIR, CUT), BF16),
        pltpu.VMEM((4, 4, PAIR, EXT - CUT), BF16),
        pltpu.VMEM((4, PAIR, CUT), BF16),
        pltpu.VMEM((4, PAIR, EXT - CUT), BF16),
        pltpu.VMEM((4, PAIR, CUT), BF16),
        pltpu.VMEM((4, PAIR, EXT - CUT), BF16),
        pltpu.VMEM((4, PAIR, PART), BF16),
        pltpu.VMEM((EXP, PAIR, PART), BF16),
        dma((13,)),
        dma((1,)),
        dma((1,)),
        dma((2,)),
        dma((2,)),
        dma((CHIPS,)),
        dma((CHIPS,)),
        dma((CHIPS,)),
        dma((CHIPS,)),
        dma((3, 3, 4)),
        dma((3, 3, 4)),
        dma((3, 4)),
        dma((3, 4)),
        dma((1,)),
        dma((1,)),
        dma((4,)),
        dma((4,)),
    ] + [dma((4,)) for _ in range(10)]
    return pl.pallas_call(
        kernel,
        out_shape=jax.ShapeDtypeStruct((ROWS, QUARTER), BF16),
        in_specs=[hbm] * 13 + [smem] * 3,
        out_specs=vmem,
        scratch_shapes=scratch,
        compiler_params=pltpu.CompilerParams(
            collective_id=0, has_side_effects=True, vmem_limit_bytes=58 * 1024 * 1024
        ),
        cost_estimate=pl.CostEstimate(flops=5 * 10**9, bytes_accessed=13 * 2**20, transcendentals=7 * 10**6),
        name="layer",
    )(
        hidden, queries, suffix_row_keys, suffix_row_values, prefix_cached_keys,
        prefix_cached_values, expert_norm_gain, router.T,
        gate_weight.reshape(WIDTH, UNITS), up_weight.reshape(WIDTH, UNITS),
        down_weight.reshape(UNITS, WIDTH), adapter_down_maps.reshape(-1, UNITS),
        adapter_up_maps.reshape(-1, WIDTH), routes.T, tenants, lengths,
    )


def solution(mesh):
    in_specs = (
        P("seq", "exp"),
        P("seq", "exp"),
        P("seq", "exp"),
        P("seq", "exp"),
        P("seq", "exp"),
        P("seq", "exp"),
        P(),
        P(),
        P("exp", None, "seq"),
        P("exp", None, "seq"),
        P("exp", "seq", None),
        P(None, "exp", None, "seq"),
        P("seq", "exp", None, None),
        P(),
        P(),
        P(),
    )
    return jax.shard_map(
        on_device, mesh=mesh, in_specs=in_specs, out_specs=P("seq", "exp"), check_vma=False
    )
```

```python
import functools

import jax
import jax.numpy as jnp
from jax import lax
from jax.experimental import pallas as pl
from jax.experimental.pallas import tpu as pltpu
from jax.sharding import PartitionSpec as P

MESH = pl.DeviceIdType.MESH
F32 = jnp.float32
BF16 = jnp.bfloat16

HEAD = 128
GROUP = 6
KV = 2
HEADS = KV * GROUP
ROWS = 8
SEQ = 32
EXP = 4
CHIPS = SEQ // 2
PAIR = 2 * ROWS
TOTAL = SEQ * ROWS
WIDTH = 6144
HALF = WIDTH // 2
QUARTER = WIDTH // EXP
PREFIX = 2048
UNITS = 256
QB = GROUP * ROWS
BLK = 2 * QB
MSG = BLK + 16
PART = GROUP * HEAD
THIRD = PART // 3
KEYS = 512
NORM_EPS = 1e-05
LOG2E = 1.4426950408889634
SCALE2 = HEAD**-0.5 * LOG2E


def dot(a, b):
    return jnp.dot(a, b, preferred_element_type=F32)


def dot_t(a, b):
    return lax.dot_general(a, b, (((1,), (1,)), ((), ())), preferred_element_type=F32)


def iota(shape, dim):
    return lax.broadcasted_iota(jnp.int32, shape, dim)


def three_parts(v):
    high = v.astype(BF16).astype(F32)
    rest = v - high
    mid = rest.astype(BF16).astype(F32)
    low = rest - mid
    ax = v.ndim - 1
    return high + pltpu.roll(mid, 16, ax) + pltpu.roll(low, 32, ax)


def whole_of(p):
    ax = p.ndim - 1
    return p + pltpu.roll(p, 128 - 16, ax) + pltpu.roll(p, 128 - 32, ax)


N_SMALL = 9


def kernel(
    hid, qry, skey, sval, pk, pv, gain, rout, wg, wu, wd, adn, aup, routes, tenants_h, lengths_h,
    out,
    tenants, lengths,
    hid_v, qry_v, skey_v, sval_v, rout_v, routes_v, gain_v, gainf, msnd, pairb, qall, kbuf, vbuf, sbuf, pbuf,
    suf_o, suf_l, ksnd, vsnd, xb, wgb, wub, wdb, adnb, upb,
    accg, accu, accs, accl, rpad, rcol, lsnd, lrcv, lpair, asnd, arcv, usnd, urcv,
    p2, r2, p3, r3, p4, r4, fpair,
    lsem, ms, mr, ks, kr, qs, qr, ps, pr, gs, gr, hs, hr, ups, upr, ls, lr, lps, lpr, as_, ar,
    ds, dr, us, ur, ss, sr, fs, fr,
):
    s = lax.axis_index("seq")
    z = lax.axis_index("exp")
    k = lax.rem(s, 2)
    c = lax.div(s, 2)
    x = lax.rem(c, 4)
    y = lax.div(c, 4)
    sib = s + 1 - 2 * k
    sent = []

    def remote(src, dst, ssem, rsem, seq, exp):
        return pltpu.make_async_remote_copy(
            src_ref=src, dst_ref=dst, send_sem=ssem, recv_sem=rsem,
            device_id=(seq, exp), device_id_type=MESH,
        )

    def each(n, body, first=0):
        def step(i, carry):
            body(i)
            return carry

        lax.fori_loop(first, n, step, 0)

    def chip_at(i):
        return lax.rem(y + i // 4, 4) * 4 + lax.rem(x + i % 4, 4)

    barrier = pltpu.get_barrier_semaphore()

    def greet(seq, exp):
        pl.semaphore_signal(barrier, inc=1, device_id=(seq, exp), device_id_type=MESH)

    greet(sib, z)
    for i in range(1, CHIPS):
        greet(chip_at(i) * 2 + k, z)
    for d in range(1, EXP):
        greet(s, lax.rem(z + d, EXP))

    own_head = pl.ds(pl.multiple_of(k * HEAD, HEAD), HEAD)
    sib_head = pl.ds(pl.multiple_of(HEAD - k * HEAD, HEAD), HEAD)
    up_row = pl.multiple_of(64 * lax.rem(c, 2) + 32 * k, 32)
    def up_part(zz, core):
        at = pl.multiple_of(zz * QUARTER + core * PART, PART)
        return aup.at[:, pl.ds(at, PART)], upb.at[pl.ds(up_row, 32), pl.ds(zz * PART, PART)]

    def down_part(zz, core):
        at = pl.multiple_of(zz * QUARTER + core * PART, PART)
        rows = 0 if core is k else UNITS
        return wd.at[:, pl.ds(at, PART)], wdb.at[pl.ds(rows, UNITS), pl.ds(zz * PART, PART)]

    loads = [
        (qry, qry_v),
        (hid, hid_v),
        (skey, skey_v),
        (sval, sval_v),
        (gain, gain_v),
        (rout, rout_v),
        (routes, routes_v),
        (tenants_h, tenants),
        (lengths_h, lengths),
        (pk.at[:, own_head], kbuf.at[pl.ds(0, PREFIX), :]),
        (pv.at[:, own_head], vbuf.at[pl.ds(0, PREFIX), :]),
        (pk.at[:, sib_head], ksnd),
        (pv.at[:, sib_head], vsnd),
        (wg, wgb),
        (wu, wub),
        (adn, adnb),
    ] + [part(zz, k) for part in (up_part, down_part) for zz in range(EXP)]
    loads = [pltpu.make_async_copy(a, b, lsem.at[i]) for i, (a, b) in enumerate(loads)]
    for cp in loads:
        cp.start()
    other_rows = pl.multiple_of(64 - 64 * lax.rem(c, 2), 64)
    upb[pl.ds(other_rows, 64), :] = jnp.zeros((64, HALF), BF16)
    for cp in loads[:N_SMALL]:
        cp.wait()
    gainf[...] = gain_v[...].astype(F32).reshape(1, WIDTH)

    q, h = qry_v[...].astype(F32), hid_v[...].astype(F32)
    kv = [skey_v[...].astype(F32), sval_v[...].astype(F32)]
    by_head = []
    for g in range(KV):
        tiles = [a[:, (g * GROUP + j) * HEAD : (g * GROUP + j + 1) * HEAD] for a in (q, h) for j in range(GROUP)]
        tiles = tiles + [a[:, g * HEAD : (g + 1) * HEAD] for a in kv]
        by_head.append(jnp.concatenate(tiles, axis=0))
    pairb[k] = jnp.where(k == 0, by_head[0], by_head[1]).astype(BF16)
    msnd[...] = jnp.where(k == 0, by_head[1], by_head[0]).astype(BF16)
    pl.semaphore_wait(barrier, CHIPS + EXP - 1)

    m_copy = remote(msnd, pairb.at[k], ms.at[0], mr.at[0], sib, z)
    m_copy.start()
    kv_copies = [
        remote(ksnd, kbuf.at[pl.ds(PREFIX, PREFIX), :], ks.at[0], kr.at[0], sib, z),
        remote(vsnd, vbuf.at[pl.ds(PREFIX, PREFIX), :], ks.at[1], kr.at[1], sib, z),
    ]
    for cp in loads[N_SMALL + 2 : N_SMALL + 4]:
        cp.wait()
    sent.append(lambda: [cp.wait_send() for cp in (m_copy, *kv_copies)])
    remote(msnd, pairb.at[1 - k], ms.at[0], mr.at[0], sib, z).wait_recv()

    own = [pairb[kk, 0:QB, :] for kk in range(2)]
    qall[c] = jnp.concatenate(own, axis=0)
    order = (1, 2, 3, 12, 13, 14, 15, 8, 9, 10, 11, 4, 5, 6, 7)

    def q_send(i):
        return remote(qall.at[c], qall.at[c], qs.at[i], qr.at[c], chip_at(i) * 2 + k, z)

    for i in order[:3]:
        q_send(i).start()
    kv_copies[0].start()
    for i in order[3:]:
        q_send(i).start()
    kv_copies[1].start()
    sent.append(lambda: [q_send(i).wait_send() for i in order])
    up_copies = []
    for zz in range(EXP):
        src, dst = up_part(zz, 1 - k)
        up_copies.append(remote(src, dst, ups.at[zz], upr.at[zz], sib, z))
    down_copies = []
    for zz in range(EXP):
        src, dst = down_part(zz, 1 - k)
        down_copies.append(remote(src, dst, ds.at[zz], dr.at[zz], sib, z))
    for cp in up_copies + down_copies:
        cp.start()
    sent.append(lambda: [cp.wait_send() for cp in up_copies + down_copies])

    def stacked(rows):
        index = iota((PAIR, rows.shape[1]), 0)
        got = jnp.zeros(index.shape, F32)
        for i in range(rows.shape[0]):
            got = jnp.where(index == i, rows[i : i + 1], got)
        return got.astype(BF16)

    rpad[...] = stacked(rout_v[...].astype(F32))
    eye = (iota((TOTAL, TOTAL), 0) == iota((TOTAL, TOTAL), 1)).astype(F32).astype(BF16)
    rcol[...] = dot_t(eye, stacked(routes_v[...].astype(F32)))

    row16 = iota((PAIR, 128), 0)
    lane16 = iota((PAIR, 128), 1)
    ten = [tenants[c * PAIR + i] for i in range(PAIR)]
    pos = []
    for i in range(PAIR):
        p = jnp.int32(0)
        for j in range(i // ROWS * ROWS, i):
            p = p + (ten[i] == ten[j]).astype(jnp.int32)
        pos.append(p)
    lens = [lengths[t] for t in ten]

    def spread(values, at):
        got = jnp.full((PAIR, 128), -1, jnp.int32)
        for i, v in enumerate(values):
            got = jnp.where(at == i, v, got)
        return got

    ten_rows = spread(ten, row16)
    pos_c = spread(pos, lane16)
    visible = (lane16 < PAIR) & (ten_rows == spread(ten, lane16))
    visible = visible & (pos_c <= spread(pos, row16)) & (pos_c < spread(lens, row16))
    pairs = [pairb[kk, BLK:, :].astype(F32) for kk in range(2)]
    fill = jnp.zeros((128 - PAIR, HEAD), F32)
    keys = jnp.concatenate([pairs[0][:ROWS], pairs[1][:ROWS], fill], axis=0).astype(BF16)
    values = jnp.concatenate([pairs[0][ROWS:], pairs[1][ROWS:], fill], axis=0).astype(BF16)
    for kk in range(2):
        seen = visible[kk * ROWS : (kk + 1) * ROWS]
        seen = jnp.broadcast_to(seen[None], (GROUP, ROWS, 128))
        sc = dot_t(pairb[kk, 0:QB, :], keys).reshape(GROUP, ROWS, 128)
        sc = jnp.where(seen, sc, -1e30)
        m = jnp.max(sc, axis=2, keepdims=True)
        w = jnp.where(seen, jnp.exp2((sc - m) * SCALE2), 0.0)
        mass = jnp.sum(w, axis=2, keepdims=True)
        acc = dot(w.reshape(QB, 128).astype(BF16), values).reshape(GROUP, ROWS, HEAD)
        suf_o[kk] = acc / mass
        lse = jnp.broadcast_to(m * SCALE2 + jnp.log2(mass), (GROUP, ROWS, 128))
        stat = jnp.zeros((ROWS, 128), F32)
        for j in range(GROUP):
            stat = jnp.where(lane16[:ROWS] == j, lse[j], stat)
        suf_l[kk * ROWS : (kk + 1) * ROWS, :] = stat

    for cp in loads[N_SMALL : N_SMALL + 2]:
        cp.wait()
    for cp in kv_copies:
        cp.wait_recv()

    def q_wait(i):
        chip = chip_at(i)
        remote(qall.at[c], qall.at[chip], qs.at[0], qr.at[chip], chip * 2 + k, z).wait_recv()

    tiles = [(u, at) for u in range(4) for at in range(0, 2 * PREFIX, KEYS)]
    queries = {}
    ones = jnp.ones((KEYS, HEAD), BF16)

    def scores(u, at):
        if at == 0:
            for i in range(4 * u, 4 * u + 4):
                if i:
                    q_wait(i)
            queries[u] = qall[pl.ds(lax.rem(y + u, 4) * 4, 4)].reshape(4 * BLK, HEAD)
        return dot_t(queries[u], kbuf[at : at + KEYS, :])

    def finish(u, m, acc):
        mass = acc[:, HEAD:]
        o = (acc[:, :HEAD] / mass).astype(BF16).reshape(4, BLK, HEAD)
        lse = (m + jnp.log2(mass)).reshape(8, GROUP, ROWS, 128)
        lane = iota((8, ROWS, 128), 2)
        stat = jnp.zeros((8, ROWS, 128), F32)
        for j in range(GROUP):
            stat = jnp.where(lane == j, lse[:, j], stat)
        at = pl.ds(lax.rem(y + u, 4) * 4, 4)
        sbuf[at, 0:BLK, :] = o
        sbuf[at, BLK:, :] = three_parts(stat).reshape(4, PAIR, 128).astype(BF16)
        for i in range(4 * u, 4 * u + 4):
            if i:
                p_copy(i).start()

    def p_copy(i):
        chip = chip_at(i)
        return remote(sbuf.at[chip], pbuf.at[c], ps.at[i], pr.at[c], chip * 2 + k, z)

    coming = scores(*tiles[0])
    m = acc = done = None
    for n, (u, at) in enumerate(tiles):
        sc = coming * SCALE2
        if n + 1 < len(tiles):
            coming = scores(*tiles[n + 1])
        if done is not None:
            finish(*done)
            done = None
        top = jnp.max(sc, axis=1, keepdims=True)
        top = top if at == 0 else jnp.maximum(m, top)
        got = dot(jnp.exp2(sc - top).astype(BF16), jnp.concatenate([vbuf[at : at + KEYS, :], ones], axis=1))
        acc = got if at == 0 else acc * jnp.exp2(m - top) + got
        m = top
        if at + KEYS == 2 * PREFIX:
            done = (u, m, acc)
    finish(*done)
    sent.append(lambda: [p_copy(i).wait_send() for i in range(1, CHIPS)])

    pbuf[c] = sbuf[c]
    for i in range(1, CHIPS):
        chip = chip_at(i)
        remote(sbuf.at[chip], pbuf.at[chip], ps.at[0], pr.at[chip], chip * 2 + k, z).wait_recv()
    lses = whole_of(pbuf[:, BLK:, :].astype(F32))
    top = jnp.maximum(jnp.max(lses, axis=0), suf_l[...])
    shares = jnp.exp2(lses - top[None])
    suf_share = jnp.exp2(suf_l[...] - top)
    inverse = 1.0 / (jnp.sum(shares, axis=0) + suf_share)
    suf_share = suf_share * inverse
    att = {}
    for kk in range(2):
        rows = slice(kk * ROWS, (kk + 1) * ROWS)
        hidden = pairb[kk, QB : 2 * QB, :].astype(F32)
        for j in range(GROUP):
            own = suf_share[rows, j : j + 1] * suf_o[kk, j]
            att[kk, j] = hidden[j * ROWS : (j + 1) * ROWS] + own
    for i in range(CHIPS):
        part = pbuf[i, 0:BLK, :].astype(F32)
        share = shares[i] * inverse
        for kk in range(2):
            rows = slice(kk * ROWS, (kk + 1) * ROWS)
            for j in range(GROUP):
                at = (kk * GROUP + j) * ROWS
                att[kk, j] = att[kk, j] + share[rows, j : j + 1] * part[at : at + ROWS]

    here = {"x": x, "y": y, "z": z}
    orders = ("xyz", "yzx", "zxy")

    def region(p, step, core=k, **at):
        at = {**here, **at}
        index = [at[a] for a in orders[p][: step - 1 if step else None : -1]]
        return xb.at[(core, p, *index)]

    def peer(axis, d):
        at = {**here, axis: lax.rem(here[axis] + d, 4)}
        return at[axis], (at["y"] * 4 + at["x"]) * 2 + k, at["z"]

    def g_send(p, step, d):
        axis = orders[p][step]
        _, seq, exp = peer(axis, d)
        block = region(p, step)
        return remote(block, block, gs.at[p, step, d], gr.at[p, step, here[axis]], seq, exp)

    def g_wait(p, step, d):
        axis = orders[p][step]
        there, seq, exp = peer(axis, d)
        block = region(p, step, **{axis: there})
        remote(block, block, gs.at[p, step, 0], gr.at[p, step, there], seq, exp).wait_recv()

    def h_copy(p, there, core):
        block = xb.at[core, p, there]
        return remote(block, block, hs.at[p, there], hr.at[p, there], sib, z)

    def own_block(p, core):
        return (core, p, *[here[a] for a in reversed(orders[p])])

    for p in range(3):
        rows = [jnp.concatenate([att[kk, j] for j in (2 * p, 2 * p + 1)], axis=1) for kk in range(2)]
        xb[own_block(p, k)] = jnp.concatenate(rows, axis=0).astype(BF16)
    for d in (2, 1, 3):
        for p in range(3):
            g_send(p, 0, d).start()
    for step in (1, 2):
        for p in range(3):
            for d in (1, 3, 2):
                g_wait(p, step - 1, d)
            for d in (2, 1, 3):
                g_send(p, step, d).start()
    for p in range(3):
        h_copy(p, here[orders[p][2]], k).start()
    for d in (1, 3, 2):
        for p in range(3):
            g_wait(p, 2, d)
            h_copy(p, peer(orders[p][2], d)[0], k).start()

    def rows_sent():
        for p in range(3):
            for step in range(3):
                for d in (1, 2, 3):
                    g_send(p, step, d).wait_send()
            for there in range(4):
                h_copy(p, there, k).wait_send()

    sent.append(rows_sent)

    for cp in loads[N_SMALL + 4 : N_SMALL + 6]:
        cp.wait()
    accg[...] = jnp.zeros_like(accg)
    accu[...] = jnp.zeros_like(accu)
    accs[...] = jnp.zeros_like(accs)
    accl[...] = jnp.zeros_like(accl)

    def project(core):
        def one(zz):
            at = pl.multiple_of(zz * QUARTER + core * PART, PART)
            turned = xb[core, 1, :, zz]
            turned = jnp.stack([turned[i, j] for j in range(4) for i in range(4)])
            rows = [xb[core, 0, zz], turned, xb[core, 2, :, :, zz]]
            rows = jnp.concatenate([r.reshape(TOTAL, THIRD) for r in rows], axis=1).astype(F32)
            squares = rows * rows
            total = squares[:, 0:128]
            for i in range(1, PART // 128):
                total = total + squares[:, i * 128 : (i + 1) * 128]
            accs[...] = accs[...] + total
            rows = (rows * gainf[:, pl.ds(at, PART)]).astype(BF16)
            accg[...] = accg[...] + dot(rows, wgb[pl.ds(at, PART), :])
            accu[...] = accu[...] + dot(rows, wub[pl.ds(at, PART), :])
            accl[...] = accl[...] + dot_t(rows, rpad[:, pl.ds(at, PART)])

        each(EXP, one)

    project(k)
    for p in range(3):
        for there in range(4):
            h_copy(p, there, 1 - k).wait_recv()
    project(1 - k)
    scale = lax.rsqrt(jnp.sum(accs[...], axis=1, keepdims=True) / WIDTH + NORM_EPS)
    gate = accg[...] * scale
    logits = accl[...] * scale
    first, second = rcol[:, 0:1], rcol[:, 1:2]
    expert = iota((TOTAL, PAIR), 1).astype(F32)
    here_e = z.astype(F32)
    mine = jnp.sum(jnp.where(expert == here_e, logits, 0.0), axis=1, keepdims=True)
    theirs = jnp.sum(jnp.where(expert == first + second - here_e, logits, 0.0), axis=1, keepdims=True)
    share = 1.0 / (1.0 + jnp.exp(theirs - mine))
    share = jnp.where((first == here_e) | (second == here_e), share, 0.0)
    units = (gate / (1.0 + jnp.exp(-gate)) * (accu[...] * scale) * share).astype(BF16)

    usnd[...] = units
    u_copy = remote(usnd, urcv, us.at[0], ur.at[0], sib, z)
    u_copy.start()
    sent.append(lambda: u_copy.wait_send())

    for cp in loads[N_SMALL + 6 :]:
        cp.wait()
    for i in range(CHIPS // 2):
        low = dot_t(units[i * 32 : (i + 1) * 32], adnb[i * 128 : (i + 1) * 128, :])
        lsnd[2 * i : 2 * i + 2] = low.astype(BF16).reshape(2, PAIR, 128)

    def low_copy(i):
        chip = chip_at(i)
        return remote(lsnd.at[chip], lrcv.at[c], ls.at[i], lr.at[c], chip * 2 + k, z)

    for i in range(1, CHIPS):
        low_copy(i).start()
    sent.append(lambda: [low_copy(i).wait_send() for i in range(1, CHIPS)])
    lrcv[c] = lsnd[c]

    sum_orders = ("zyx", "xzy", "yxz")

    def part_of(t, step, there):
        if step == 1 and t == 2:
            return p3.at[t, :, there]
        return (p2, p3, p4)[step].at[t, there]

    def s_send(t, step, d):
        axis = sum_orders[t][step]
        there, seq, exp = peer(axis, d)
        return remote(
            part_of(t, step, there), (r2, r3, r4)[step].at[t, here[axis]],
            ss.at[t, step, d], sr.at[t, step, here[axis]], seq, exp,
        )

    def s_sum(t, step):
        axis = sum_orders[t][step]
        into = (r2, r3, r4)[step]
        total = part_of(t, step, here[axis])[...].astype(F32)
        for d in (1, 3, 2):
            there, seq, exp = peer(axis, d)
            remote(
                part_of(t, step, here[axis]), into.at[t, there],
                ss.at[t, step, 0], sr.at[t, step, there], seq, exp,
            ).wait_recv()
            total = total + into[t, there].astype(F32)
        return total

    def s_start(t, step):
        for d in (2, 1, 3):
            s_send(t, step, d).start()

    u_copy.wait_recv()
    for cp in down_copies:
        cp.wait_recv()
    both_units = jnp.concatenate([units, urcv[...]], axis=1)
    for t in range(3):
        for zz in range(EXP):
            at = zz * PART + t * THIRD
            both = dot(both_units, wdb[:, at : at + THIRD]).astype(BF16).reshape(4, 4, PAIR, THIRD)
            if t == 0:
                p2[t, zz] = both
            elif t == 1:
                for i in range(4):
                    p2[t, i, zz] = both[:, i]
            else:
                p2[t, :, zz] = both
        s_start(t, 0)
    sent.append(
        lambda: [s_send(t, i, d).wait_send() for t in range(3) for i in range(3) for d in (1, 2, 3)]
    )

    for i in range(1, CHIPS):
        chip = chip_at(i)
        remote(lsnd.at[chip], lrcv.at[chip], ls.at[0], lr.at[chip], chip * 2 + k, z).wait_recv()
    low = jnp.sum(lrcv[...].astype(F32), axis=0)
    lpair[0] = low.astype(BF16)
    lp_copy = remote(lpair.at[0], lpair.at[1], lps.at[0], lpr.at[0], sib, z)
    lp_copy.start()
    sent.append(lambda: lp_copy.wait_send())
    for cp in up_copies:
        cp.wait_recv()
    lp_copy.wait_recv()
    low = low + lpair[1].astype(F32)
    low = jnp.where(lax.div(lane16, 16) == lax.rem(ten_rows, 8), low, 0.0).astype(BF16)
    for zz in range(EXP):
        asnd[zz] = dot(low, upb[:, zz * PART : (zz + 1) * PART]).astype(BF16)

    def a_copy(d):
        zz = lax.rem(z + d, EXP)
        return remote(asnd.at[zz], arcv.at[z], as_.at[d], ar.at[z], s, zz)

    for d in (2, 1, 3):
        a_copy(d).start()
    sent.append(lambda: [a_copy(d).wait_send() for d in (1, 2, 3)])

    for t in range(3):
        p3[t] = s_sum(t, 0).astype(BF16)
        s_start(t, 1)
    for t in range(3):
        p4[t] = s_sum(t, 1).astype(BF16)
        s_start(t, 2)
    adapter = asnd[z].astype(F32)
    for d in (1, 3, 2):
        zz = lax.rem(z + d, EXP)
        remote(asnd.at[z], arcv.at[zz], as_.at[0], ar.at[zz], s, zz).wait_recv()
        adapter = adapter + arcv[zz].astype(F32)
    total = jnp.concatenate([s_sum(t, 2) for t in range(3)], axis=1) + adapter

    theirs = jnp.where(k == 0, total[ROWS:], total[:ROWS])
    fpair[0] = jnp.concatenate([theirs[:, : PART // 2], theirs[:, PART // 2 :]], axis=0).astype(BF16)
    f_copy = remote(fpair.at[0], fpair.at[1], fs.at[0], fr.at[0], sib, z)
    f_copy.start()
    sent.append(lambda: f_copy.wait_send())
    mine = jnp.where(k == 0, total[:ROWS], total[ROWS:])
    resid = [[xb[own_block(p, kk)].astype(F32) for p in range(3)] for kk in range(2)]
    resid = [jnp.concatenate(r, axis=1) for r in resid]
    resid = [jnp.where(k == 0, r[:ROWS], r[ROWS:]) for r in resid]
    f_copy.wait_recv()
    got = fpair[1].astype(F32)
    got = jnp.concatenate([got[:ROWS], got[ROWS:]], axis=1)
    got = [jnp.where(k == kk, mine, got) for kk in range(2)]
    out[...] = jnp.concatenate([r + g for r, g in zip(resid, got)], axis=1).astype(BF16)

    for wait in sent:
        wait()


def on_device(
    hidden, queries, suffix_row_keys, suffix_row_values, prefix_cached_keys, prefix_cached_values,
    expert_norm_gain, router, gate_weight, up_weight, down_weight, adapter_down_maps,
    adapter_up_maps, routes, tenants, lengths,
):
    vmem = pl.BlockSpec(memory_space=pltpu.VMEM)
    hbm = pl.BlockSpec(memory_space=pl.ANY)
    dma = pltpu.SemaphoreType.DMA
    scratch = [
        pltpu.SMEM((TOTAL,), jnp.int32),
        pltpu.SMEM((64,), jnp.int32),
        pltpu.VMEM((ROWS, QUARTER), BF16),
        pltpu.VMEM((ROWS, QUARTER), BF16),
        pltpu.VMEM((ROWS, KV * HEAD), BF16),
        pltpu.VMEM((ROWS, KV * HEAD), BF16),
        pltpu.VMEM((EXP, WIDTH), BF16),
        pltpu.VMEM((2, TOTAL), jnp.int32),
        pltpu.VMEM((WIDTH,), BF16),
        pltpu.VMEM((1, WIDTH), F32),
        pltpu.VMEM((MSG, HEAD), BF16),
        pltpu.VMEM((2, MSG, HEAD), BF16),
        pltpu.VMEM((CHIPS, BLK, HEAD), BF16),
        pltpu.VMEM((2 * PREFIX, HEAD), BF16),
        pltpu.VMEM((2 * PREFIX, HEAD), BF16),
        pltpu.VMEM((CHIPS, MSG, HEAD), BF16),
        pltpu.VMEM((CHIPS, MSG, HEAD), BF16),
        pltpu.VMEM((2, GROUP, ROWS, HEAD), F32),
        pltpu.VMEM((PAIR, 128), F32),
        pltpu.VMEM((PREFIX, HEAD), BF16),
        pltpu.VMEM((PREFIX, HEAD), BF16),
        pltpu.VMEM((2, 3, 4, 4, 4, PAIR, THIRD), BF16),
        pltpu.VMEM((WIDTH, UNITS), BF16),
        pltpu.VMEM((WIDTH, UNITS), BF16),
        pltpu.VMEM((2 * UNITS, HALF), BF16),
        pltpu.VMEM((1024, UNITS), BF16),
        pltpu.VMEM((128, HALF), BF16),
        pltpu.VMEM((TOTAL, UNITS), F32),
        pltpu.VMEM((TOTAL, UNITS), F32),
        pltpu.VMEM((TOTAL, 128), F32),
        pltpu.VMEM((TOTAL, PAIR), F32),
        pltpu.VMEM((PAIR, WIDTH), BF16),
        pltpu.VMEM((TOTAL, PAIR), F32),
        pltpu.VMEM((CHIPS, PAIR, 128), BF16),
        pltpu.VMEM((CHIPS, PAIR, 128), BF16),
        pltpu.VMEM((2, PAIR, 128), BF16),
        pltpu.VMEM((EXP, PAIR, PART), BF16),
        pltpu.VMEM((EXP, PAIR, PART), BF16),
        pltpu.VMEM((TOTAL, UNITS), BF16),
        pltpu.VMEM((TOTAL, UNITS), BF16),
        pltpu.VMEM((3, 4, 4, 4, PAIR, THIRD), BF16),
        pltpu.VMEM((3, 4, 4, 4, PAIR, THIRD), BF16),
        pltpu.VMEM((3, 4, 4, PAIR, THIRD), BF16),
        pltpu.VMEM((3, 4, 4, PAIR, THIRD), BF16),
        pltpu.VMEM((3, 4, PAIR, THIRD), BF16),
        pltpu.VMEM((3, 4, PAIR, THIRD), BF16),
        pltpu.VMEM((2, PAIR, PART // 2), BF16),
        dma((24,)),
        dma((1,)),
        dma((1,)),
        dma((2,)),
        dma((2,)),
        dma((CHIPS,)),
        dma((CHIPS,)),
        dma((CHIPS,)),
        dma((CHIPS,)),
        dma((3, 3, 4)),
        dma((3, 3, 4)),
        dma((3, 4)),
        dma((3, 4)),
        dma((4,)),
        dma((4,)),
        dma((CHIPS,)),
        dma((CHIPS,)),
        dma((1,)),
        dma((1,)),
        dma((4,)),
        dma((4,)),
        dma((4,)),
        dma((4,)),
        dma((1,)),
        dma((1,)),
        dma((3, 3, 4)),
        dma((3, 3, 4)),
        dma((1,)),
        dma((1,)),
    ]
    return pl.pallas_call(
        kernel,
        out_shape=jax.ShapeDtypeStruct((ROWS, QUARTER), BF16),
        in_specs=[hbm] * 16,
        out_specs=vmem,
        scratch_shapes=scratch,
        compiler_params=pltpu.CompilerParams(
            collective_id=0, has_side_effects=True, vmem_limit_bytes=58 * 1024 * 1024
        ),
        cost_estimate=pl.CostEstimate(flops=5 * 10**9, bytes_accessed=13 * 2**20, transcendentals=7 * 10**6),
        name="layer",
    )(
        hidden, queries, suffix_row_keys, suffix_row_values, prefix_cached_keys,
        prefix_cached_values, expert_norm_gain, router.T,
        gate_weight.reshape(WIDTH, UNITS), up_weight.reshape(WIDTH, UNITS),
        down_weight.reshape(UNITS, WIDTH), adapter_down_maps.reshape(-1, UNITS),
        adapter_up_maps.reshape(-1, WIDTH), routes.T, tenants, lengths,
    )


def solution(mesh):
    in_specs = (
        P("seq", "exp"),
        P("seq", "exp"),
        P("seq", "exp"),
        P("seq", "exp"),
        P("seq", "exp"),
        P("seq", "exp"),
        P(),
        P(),
        P("exp", None, "seq"),
        P("exp", None, "seq"),
        P("exp", "seq", None),
        P(None, "exp", None, "seq"),
        P("seq", "exp", None, None),
        P(),
        P(),
        P(),
    )
    return jax.shard_map(
        on_device, mesh=mesh, in_specs=in_specs, out_specs=P("seq", "exp"), check_vma=False
    )
```

```python
import functools

import jax
import jax.numpy as jnp
from jax import lax
from jax.experimental import pallas as pl
from jax.experimental.pallas import tpu as pltpu
from jax.sharding import PartitionSpec as P

MESH = pl.DeviceIdType.MESH
F32 = jnp.float32
BF16 = jnp.bfloat16

HEAD = 128
GROUP = 6
KV = 2
HEADS = KV * GROUP
ROWS = 8
SEQ = 32
EXP = 4
CHIPS = SEQ // 2
PAIR = 2 * ROWS
TOTAL = SEQ * ROWS
WIDTH = 6144
HALF = WIDTH // 2
QUARTER = WIDTH // EXP
PREFIX = 2048
UNITS = 256
QB = GROUP * ROWS
BLK = 2 * QB
MSG = BLK + 16
PART = GROUP * HEAD
THIRD = PART // 3
AHEAD = (1, 3, 2, 0)
KEYS = 512
NORM_EPS = 1e-05
LOG2E = 1.4426950408889634
SCALE2 = HEAD**-0.5 * LOG2E


def dot(a, b):
    return jnp.dot(a, b, preferred_element_type=F32)


def dot_t(a, b):
    return lax.dot_general(a, b, (((1,), (1,)), ((), ())), preferred_element_type=F32)


def iota(shape, dim):
    return lax.broadcasted_iota(jnp.int32, shape, dim)


def three_parts(v):
    high = v.astype(BF16).astype(F32)
    rest = v - high
    mid = rest.astype(BF16).astype(F32)
    low = rest - mid
    ax = v.ndim - 1
    return high + pltpu.roll(mid, 16, ax) + pltpu.roll(low, 32, ax)


def whole_of(p):
    ax = p.ndim - 1
    return p + pltpu.roll(p, 128 - 16, ax) + pltpu.roll(p, 128 - 32, ax)


N_SMALL = 9


def kernel(
    hid, qry, skey, sval, pk, pv, gain, rout, wg, wu, wd, adn, aup, routes, tenants_h, lengths_h,
    out,
    tenants, lengths,
    hid_v, qry_v, skey_v, sval_v, rout_v, routes_v, gain_v, gainf, msnd, pairb, qall, kbuf, vbuf, sbuf, pbuf,
    suf_o, suf_l, ksnd, vsnd, xb, wgb, wub, wdb, adnb, upb,
    accg, accu, accs, accl, rpad, rcol, lsnd, lrcv, lsum, lrow, lpair, asnd, arcv, usnd, urcv,
    p2, r2, p3, r3, p4, r4, fpair,
    lsem, ms, mr, ks, kr, qs, qr, ps, pr, gs, gr, hs, hr, ups, upr, ls, lr, lps, lpr, as_, ar,
    ds, dr, us, ur, ss, sr, fs, fr,
):
    s = lax.axis_index("seq")
    z = lax.axis_index("exp")
    k = lax.rem(s, 2)
    c = lax.div(s, 2)
    x = lax.rem(c, 4)
    y = lax.div(c, 4)
    sib = s + 1 - 2 * k
    sent = []

    def remote(src, dst, ssem, rsem, seq, exp):
        return pltpu.make_async_remote_copy(
            src_ref=src, dst_ref=dst, send_sem=ssem, recv_sem=rsem,
            device_id=(seq, exp), device_id_type=MESH,
        )

    def each(n, body, first=0):
        def step(i, carry):
            body(i)
            return carry

        lax.fori_loop(first, n, step, 0)

    def chip_at(i):
        return lax.rem(y + i // 4, 4) * 4 + lax.rem(x + i % 4, 4)

    barrier = pltpu.get_barrier_semaphore()

    def greet(seq, exp):
        pl.semaphore_signal(barrier, inc=1, device_id=(seq, exp), device_id_type=MESH)

    for i in (10, 6, 14, 9, 11, 2, 8, 5, 7, 13, 15, 1, 3, 4, 12):
        greet(chip_at(i) * 2 + k, z)
    for d in (2, 1, 3):
        greet(s, lax.rem(z + d, EXP))
    greet(sib, z)

    own_head = pl.ds(pl.multiple_of(k * HEAD, HEAD), HEAD)
    sib_head = pl.ds(pl.multiple_of(HEAD - k * HEAD, HEAD), HEAD)
    up_row = pl.multiple_of(64 * lax.rem(c, 2) + 32 * k, 32)
    def up_part(zz, core):
        at = pl.multiple_of(zz * QUARTER + core * PART, PART)
        return aup.at[:, pl.ds(at, PART)], upb.at[pl.ds(up_row, 32), pl.ds(zz * PART, PART)]

    def down_part(zz, core):
        at = pl.multiple_of(zz * QUARTER + core * PART, PART)
        rows = 0 if core is k else UNITS
        return wd.at[:, pl.ds(at, PART)], wdb.at[pl.ds(rows, UNITS), pl.ds(zz * PART, PART)]

    loads = [
        (qry, qry_v),
        (hid, hid_v),
        (skey, skey_v),
        (sval, sval_v),
        (gain, gain_v),
        (rout, rout_v),
        (routes, routes_v),
        (tenants_h, tenants),
        (lengths_h, lengths),
        (pk.at[:, own_head], kbuf.at[pl.ds(0, PREFIX), :]),
        (pv.at[:, own_head], vbuf.at[pl.ds(0, PREFIX), :]),
        (pk.at[:, sib_head], ksnd),
        (pv.at[:, sib_head], vsnd),
        (wg, wgb),
        (wu, wub),
        (adn, adnb),
    ] + [part(zz, k) for part in (up_part, down_part) for zz in range(EXP)]
    loads = [pltpu.make_async_copy(a, b, lsem.at[i]) for i, (a, b) in enumerate(loads)]
    for cp in loads:
        cp.start()
    other_rows = pl.multiple_of(64 - 64 * lax.rem(c, 2), 64)
    upb[pl.ds(other_rows, 64), :] = jnp.zeros((64, HALF), BF16)
    for cp in loads[:N_SMALL]:
        cp.wait()
    gainf[...] = gain_v[...].astype(F32).reshape(1, WIDTH)

    q, h = qry_v[...].astype(F32), hid_v[...].astype(F32)
    kv = [skey_v[...].astype(F32), sval_v[...].astype(F32)]
    by_head = []
    for g in range(KV):
        tiles = [a[:, (g * GROUP + j) * HEAD : (g * GROUP + j + 1) * HEAD] for a in (q, h) for j in range(GROUP)]
        tiles = tiles + [a[:, g * HEAD : (g + 1) * HEAD] for a in kv]
        by_head.append(jnp.concatenate(tiles, axis=0))
    pairb[k] = jnp.where(k == 0, by_head[0], by_head[1]).astype(BF16)
    msnd[...] = jnp.where(k == 0, by_head[1], by_head[0]).astype(BF16)
    pl.semaphore_wait(barrier, CHIPS + EXP - 1)

    m_copy = remote(msnd, pairb.at[k], ms.at[0], mr.at[0], sib, z)
    m_copy.start()
    kv_copies = [
        remote(ksnd, kbuf.at[pl.ds(PREFIX, PREFIX), :], ks.at[0], kr.at[0], sib, z),
        remote(vsnd, vbuf.at[pl.ds(PREFIX, PREFIX), :], ks.at[1], kr.at[1], sib, z),
    ]
    for cp in loads[N_SMALL + 2 : N_SMALL + 4]:
        cp.wait()
    sent.append(lambda: [cp.wait_send() for cp in (m_copy, *kv_copies)])
    remote(msnd, pairb.at[1 - k], ms.at[0], mr.at[0], sib, z).wait_recv()

    own = [pairb[kk, 0:QB, :] for kk in range(2)]
    qall[c] = jnp.concatenate(own, axis=0)
    order = (12, 13, 14, 15, 4, 5, 6, 7, 8, 9, 10, 11, 1, 2, 3)

    def q_send(i):
        return remote(qall.at[c], qall.at[c], qs.at[i], qr.at[c], chip_at(i) * 2 + k, z)

    for i in order[:4]:
        q_send(i).start()
    kv_copies[0].start()
    for i in order[4:]:
        q_send(i).start()
    kv_copies[1].start()
    sent.append(lambda: [q_send(i).wait_send() for i in order])
    up_copies = []
    for zz in range(EXP):
        src, dst = up_part(zz, 1 - k)
        up_copies.append(remote(src, dst, ups.at[zz], upr.at[zz], sib, z))
    down_copies = []
    for zz in range(EXP):
        src, dst = down_part(zz, 1 - k)
        down_copies.append(remote(src, dst, ds.at[zz], dr.at[zz], sib, z))
    for cp in up_copies + down_copies:
        cp.start()
    sent.append(lambda: [cp.wait_send() for cp in up_copies + down_copies])

    def stacked(rows):
        index = iota((PAIR, rows.shape[1]), 0)
        got = jnp.zeros(index.shape, F32)
        for i in range(rows.shape[0]):
            got = jnp.where(index == i, rows[i : i + 1], got)
        return got.astype(BF16)

    rpad[...] = stacked(rout_v[...].astype(F32))
    eye = (iota((TOTAL, TOTAL), 0) == iota((TOTAL, TOTAL), 1)).astype(F32).astype(BF16)
    rcol[...] = dot_t(eye, stacked(routes_v[...].astype(F32)))

    row16 = iota((PAIR, 128), 0)
    lane16 = iota((PAIR, 128), 1)
    ten = [tenants[c * PAIR + i] for i in range(PAIR)]
    pos = []
    for i in range(PAIR):
        p = jnp.int32(0)
        for j in range(i // ROWS * ROWS, i):
            p = p + (ten[i] == ten[j]).astype(jnp.int32)
        pos.append(p)
    lens = [lengths[t] for t in ten]

    def spread(values, at):
        got = jnp.full((PAIR, 128), -1, jnp.int32)
        for i, v in enumerate(values):
            got = jnp.where(at == i, v, got)
        return got

    ten_rows = spread(ten, row16)
    pos_c = spread(pos, lane16)
    visible = (lane16 < PAIR) & (ten_rows == spread(ten, lane16))
    visible = visible & (pos_c <= spread(pos, row16)) & (pos_c < spread(lens, row16))
    pairs = [pairb[kk, BLK:, :].astype(F32) for kk in range(2)]
    fill = jnp.zeros((128 - PAIR, HEAD), F32)
    keys = jnp.concatenate([pairs[0][:ROWS], pairs[1][:ROWS], fill], axis=0).astype(BF16)
    values = jnp.concatenate([pairs[0][ROWS:], pairs[1][ROWS:], fill], axis=0).astype(BF16)
    for kk in range(2):
        seen = visible[kk * ROWS : (kk + 1) * ROWS]
        seen = jnp.broadcast_to(seen[None], (GROUP, ROWS, 128))
        sc = dot_t(pairb[kk, 0:QB, :], keys).reshape(GROUP, ROWS, 128)
        sc = jnp.where(seen, sc, -1e30)
        m = jnp.max(sc, axis=2, keepdims=True)
        w = jnp.where(seen, jnp.exp2((sc - m) * SCALE2), 0.0)
        mass = jnp.sum(w, axis=2, keepdims=True)
        acc = dot(w.reshape(QB, 128).astype(BF16), values).reshape(GROUP, ROWS, HEAD)
        suf_o[kk] = acc / mass
        lse = jnp.broadcast_to(m * SCALE2 + jnp.log2(mass), (GROUP, ROWS, 128))
        stat = jnp.zeros((ROWS, 128), F32)
        for j in range(GROUP):
            stat = jnp.where(lane16[:ROWS] == j, lse[j], stat)
        suf_l[kk * ROWS : (kk + 1) * ROWS, :] = stat

    for cp in loads[N_SMALL : N_SMALL + 2]:
        cp.wait()
    for cp in kv_copies:
        cp.wait_recv()

    def q_wait(i):
        chip = chip_at(i)
        remote(qall.at[c], qall.at[chip], qs.at[0], qr.at[chip], chip * 2 + k, z).wait_recv()

    tiles = [(u, at) for u in range(4) for at in range(0, 2 * PREFIX, KEYS)]
    queries = {}
    ones = jnp.ones((KEYS, HEAD), BF16)

    def scores(u, at):
        if at == 0:
            a = AHEAD[u]
            for i in range(4 * a, 4 * a + 4):
                if i:
                    q_wait(i)
            queries[u] = qall[pl.ds(lax.rem(y + a, 4) * 4, 4)].reshape(4 * BLK, HEAD)
        return dot_t(queries[u], kbuf[at : at + KEYS, :])

    def finish(u, m, acc):
        mass = acc[:, HEAD:]
        o = (acc[:, :HEAD] / mass).astype(BF16).reshape(4, BLK, HEAD)
        lse = (m + jnp.log2(mass)).reshape(8, GROUP, ROWS, 128)
        lane = iota((8, ROWS, 128), 2)
        stat = jnp.zeros((8, ROWS, 128), F32)
        for j in range(GROUP):
            stat = jnp.where(lane == j, lse[:, j], stat)
        a = AHEAD[u]
        at = pl.ds(lax.rem(y + a, 4) * 4, 4)
        sbuf[at, 0:BLK, :] = o
        sbuf[at, BLK:, :] = three_parts(stat).reshape(4, PAIR, 128).astype(BF16)
        for i in range(4 * a, 4 * a + 4):
            if i:
                p_copy(i).start()

    def p_copy(i):
        chip = chip_at(i)
        return remote(sbuf.at[chip], pbuf.at[c], ps.at[i], pr.at[c], chip * 2 + k, z)

    coming = scores(*tiles[0])
    m = acc = done = None
    for n, (u, at) in enumerate(tiles):
        sc = coming * SCALE2
        if n + 1 < len(tiles):
            coming = scores(*tiles[n + 1])
        if done is not None:
            finish(*done)
            done = None
        top = jnp.max(sc, axis=1, keepdims=True)
        top = top if at == 0 else jnp.maximum(m, top)
        got = dot(jnp.exp2(sc - top).astype(BF16), jnp.concatenate([vbuf[at : at + KEYS, :], ones], axis=1))
        acc = got if at == 0 else acc * jnp.exp2(m - top) + got
        m = top
        if at + KEYS == 2 * PREFIX:
            done = (u, m, acc)
    finish(*done)
    sent.append(lambda: [p_copy(i).wait_send() for i in range(1, CHIPS)])

    pbuf[c] = sbuf[c]

    def p_wait(i):
        chip = chip_at(i)
        remote(sbuf.at[chip], pbuf.at[chip], ps.at[0], pr.at[chip], chip * 2 + k, z).wait_recv()

    def merged(rows, top, mass, att):
        at = [pl.ds(lax.rem(y + a, 4) * 4, 4) for a in rows]
        lses = whole_of(jnp.concatenate([pbuf[i, BLK:, :] for i in at], axis=0).astype(F32))
        new = jnp.maximum(top, jnp.max(lses, axis=0))
        shares = jnp.exp2(lses - new[None])
        old = jnp.exp2(top - new)
        mass = mass * old + jnp.sum(shares, axis=0)
        for kk in range(2):
            side = slice(kk * ROWS, (kk + 1) * ROWS)
            for j in range(GROUP):
                att[kk, j] = old[side, j : j + 1] * att[kk, j]
        for n, i in enumerate(at):
            part = pbuf[i, 0:BLK, :].astype(F32)
            for m in range(4):
                for kk in range(2):
                    side = slice(kk * ROWS, (kk + 1) * ROWS)
                    for j in range(GROUP):
                        tile = part[m, (kk * GROUP + j) * ROWS : (kk * GROUP + j + 1) * ROWS]
                        att[kk, j] = att[kk, j] + shares[4 * n + m, side, j : j + 1] * tile
        return new, mass, att

    att = {(kk, j): suf_o[kk, j] for kk in range(2) for j in range(GROUP)}
    state = suf_l[...], jnp.ones((PAIR, 128), F32), att
    for i in range(4, CHIPS):
        p_wait(i)
    state = merged((1, 2, 3), *state)
    for i in range(1, 4):
        p_wait(i)
    _, mass, att = merged((0,), *state)
    inverse = 1.0 / mass
    for kk in range(2):
        side = slice(kk * ROWS, (kk + 1) * ROWS)
        hidden = pairb[kk, QB : 2 * QB, :].astype(F32)
        for j in range(GROUP):
            att[kk, j] = hidden[j * ROWS : (j + 1) * ROWS] + inverse[side, j : j + 1] * att[kk, j]

    here = {"x": x, "y": y, "z": z}
    orders = ("xyz", "yzx", "zxy")

    def region(p, step, core=k, **at):
        at = {**here, **at}
        index = [at[a] for a in orders[p][: step - 1 if step else None : -1]]
        return xb.at[(core, p, *index)]

    def peer(axis, d):
        at = {**here, axis: lax.rem(here[axis] + d, 4)}
        return at[axis], (at["y"] * 4 + at["x"]) * 2 + k, at["z"]

    def g_send(p, step, d):
        axis = orders[p][step]
        _, seq, exp = peer(axis, d)
        block = region(p, step)
        return remote(block, block, gs.at[p, step, d], gr.at[p, step, here[axis]], seq, exp)

    def g_wait(p, step, d):
        axis = orders[p][step]
        there, seq, exp = peer(axis, d)
        block = region(p, step, **{axis: there})
        remote(block, block, gs.at[p, step, 0], gr.at[p, step, there], seq, exp).wait_recv()

    def h_copy(p, there, core):
        block = xb.at[core, p, there]
        return remote(block, block, hs.at[p, there], hr.at[p, there], sib, z)

    def own_block(p, core):
        return (core, p, *[here[a] for a in reversed(orders[p])])

    for p in range(3):
        rows = [jnp.concatenate([att[kk, j] for j in (2 * p, 2 * p + 1)], axis=1) for kk in range(2)]
        xb[own_block(p, k)] = jnp.concatenate(rows, axis=0).astype(BF16)
    for d in (2, 1, 3):
        for p in range(3):
            g_send(p, 0, d).start()
    for step in (1, 2):
        for p in range(3):
            for d in (1, 3, 2):
                g_wait(p, step - 1, d)
            for d in (2, 1, 3):
                g_send(p, step, d).start()
    for p in range(3):
        h_copy(p, here[orders[p][2]], k).start()
    for d in (1, 3, 2):
        for p in range(3):
            g_wait(p, 2, d)
            h_copy(p, peer(orders[p][2], d)[0], k).start()

    def rows_sent():
        for p in range(3):
            for step in range(3):
                for d in (1, 2, 3):
                    g_send(p, step, d).wait_send()
            for there in range(4):
                h_copy(p, there, k).wait_send()

    sent.append(rows_sent)

    for cp in loads[N_SMALL + 4 : N_SMALL + 6]:
        cp.wait()
    accg[...] = jnp.zeros_like(accg)
    accu[...] = jnp.zeros_like(accu)
    accs[...] = jnp.zeros_like(accs)
    accl[...] = jnp.zeros_like(accl)

    def project(core):
        def one(zz):
            at = pl.multiple_of(zz * QUARTER + core * PART, PART)
            turned = xb[core, 1, :, zz]
            turned = jnp.stack([turned[i, j] for j in range(4) for i in range(4)])
            rows = [xb[core, 0, zz], turned, xb[core, 2, :, :, zz]]
            rows = jnp.concatenate([r.reshape(TOTAL, THIRD) for r in rows], axis=1).astype(F32)
            squares = rows * rows
            total = squares[:, 0:128]
            for i in range(1, PART // 128):
                total = total + squares[:, i * 128 : (i + 1) * 128]
            accs[...] = accs[...] + total
            rows = (rows * gainf[:, pl.ds(at, PART)]).astype(BF16)
            accg[...] = accg[...] + dot(rows, wgb[pl.ds(at, PART), :])
            accu[...] = accu[...] + dot(rows, wub[pl.ds(at, PART), :])
            accl[...] = accl[...] + dot_t(rows, rpad[:, pl.ds(at, PART)])

        each(EXP, one)

    project(k)
    for p in range(3):
        for there in range(4):
            h_copy(p, there, 1 - k).wait_recv()
    project(1 - k)
    scale = lax.rsqrt(jnp.sum(accs[...], axis=1, keepdims=True) / WIDTH + NORM_EPS)
    gate = accg[...] * scale
    logits = accl[...] * scale
    first, second = rcol[:, 0:1], rcol[:, 1:2]
    expert = iota((TOTAL, PAIR), 1).astype(F32)
    here_e = z.astype(F32)
    mine = jnp.sum(jnp.where(expert == here_e, logits, 0.0), axis=1, keepdims=True)
    theirs = jnp.sum(jnp.where(expert == first + second - here_e, logits, 0.0), axis=1, keepdims=True)
    share = 1.0 / (1.0 + jnp.exp(theirs - mine))
    share = jnp.where((first == here_e) | (second == here_e), share, 0.0)
    units = (gate / (1.0 + jnp.exp(-gate)) * (accu[...] * scale) * share).astype(BF16)

    usnd[...] = units
    u_copy = remote(usnd, urcv, us.at[0], ur.at[0], sib, z)
    u_copy.start()
    sent.append(lambda: u_copy.wait_send())

    for cp in loads[N_SMALL + 6 :]:
        cp.wait()
    for i in range(CHIPS // 2):
        low = dot_t(units[i * 32 : (i + 1) * 32], adnb[i * 128 : (i + 1) * 128, :])
        for j in range(2):
            lsnd[i % 2 * 2 + j, i // 2] = low[j * PAIR : (j + 1) * PAIR].astype(BF16)

    def low_copy(step, d):
        axis = "xy"[step]
        there, seq, exp = peer(axis, d)
        src, dst = ((lsnd, lrcv), (lsum, lrow))[step]
        mine = here[axis]
        return remote(src.at[there], dst.at[mine], ls.at[step, d], lr.at[step, mine], seq, exp)

    def low_sum(step):
        axis = "xy"[step]
        src, dst = ((lsnd, lrcv), (lsum, lrow))[step]
        total = src[here[axis]].astype(F32)
        for d in (1, 3, 2):
            there, seq, exp = peer(axis, d)
            remote(
                src.at[here[axis]], dst.at[there], ls.at[step, 0], lr.at[step, there], seq, exp
            ).wait_recv()
            total = total + dst[there].astype(F32)
        return total

    for d in (2, 1, 3):
        low_copy(0, d).start()
    sent.append(lambda: [low_copy(step, d).wait_send() for step in range(2) for d in (1, 2, 3)])

    sum_orders = ("zyx", "xzy", "yxz")

    def part_of(t, step, there):
        if step == 1 and t == 2:
            return p3.at[t, :, there]
        return (p2, p3, p4)[step].at[t, there]

    def s_send(t, step, d):
        axis = sum_orders[t][step]
        there, seq, exp = peer(axis, d)
        return remote(
            part_of(t, step, there), (r2, r3, r4)[step].at[t, here[axis]],
            ss.at[t, step, d], sr.at[t, step, here[axis]], seq, exp,
        )

    def s_sum(t, step):
        axis = sum_orders[t][step]
        into = (r2, r3, r4)[step]
        total = part_of(t, step, here[axis])[...].astype(F32)
        for d in (1, 3, 2):
            there, seq, exp = peer(axis, d)
            remote(
                part_of(t, step, here[axis]), into.at[t, there],
                ss.at[t, step, 0], sr.at[t, step, there], seq, exp,
            ).wait_recv()
            total = total + into[t, there].astype(F32)
        return total

    def s_start(t, step):
        for d in (2, 1, 3):
            s_send(t, step, d).start()

    u_copy.wait_recv()
    for cp in down_copies:
        cp.wait_recv()
    both_units = jnp.concatenate([units, urcv[...]], axis=1)
    for t in range(3):
        for zz in range(EXP):
            at = zz * PART + t * THIRD
            both = dot(both_units, wdb[:, at : at + THIRD]).astype(BF16).reshape(4, 4, PAIR, THIRD)
            if t == 0:
                p2[t, zz] = both
            elif t == 1:
                for i in range(4):
                    p2[t, i, zz] = both[:, i]
            else:
                p2[t, :, zz] = both
        s_start(t, 0)
    sent.append(
        lambda: [s_send(t, i, d).wait_send() for t in range(3) for i in range(3) for d in (1, 2, 3)]
    )

    lsum[...] = low_sum(0).astype(BF16)
    for d in (2, 1, 3):
        low_copy(1, d).start()
    for t in range(3):
        p3[t] = s_sum(t, 0).astype(BF16)
        s_start(t, 1)

    low = low_sum(1)
    lpair[0] = low.astype(BF16)
    lp_copy = remote(lpair.at[0], lpair.at[1], lps.at[0], lpr.at[0], sib, z)
    lp_copy.start()
    sent.append(lambda: lp_copy.wait_send())
    for cp in up_copies:
        cp.wait_recv()
    lp_copy.wait_recv()
    low = low + lpair[1].astype(F32)
    low = jnp.where(lax.div(lane16, 16) == lax.rem(ten_rows, 8), low, 0.0).astype(BF16)
    for zz in range(EXP):
        asnd[zz] = dot(low, upb[:, zz * PART : (zz + 1) * PART]).astype(BF16)

    def a_copy(d):
        zz = lax.rem(z + d, EXP)
        return remote(asnd.at[zz], arcv.at[z], as_.at[d], ar.at[z], s, zz)

    for d in (2, 1, 3):
        a_copy(d).start()
    sent.append(lambda: [a_copy(d).wait_send() for d in (1, 2, 3)])

    for t in range(3):
        p4[t] = s_sum(t, 1).astype(BF16)
        s_start(t, 2)
    adapter = asnd[z].astype(F32)
    for d in (1, 3, 2):
        zz = lax.rem(z + d, EXP)
        remote(asnd.at[z], arcv.at[zz], as_.at[0], ar.at[zz], s, zz).wait_recv()
        adapter = adapter + arcv[zz].astype(F32)
    total = jnp.concatenate([s_sum(t, 2) for t in range(3)], axis=1) + adapter

    theirs = jnp.where(k == 0, total[ROWS:], total[:ROWS])
    fpair[0] = jnp.concatenate([theirs[:, : PART // 2], theirs[:, PART // 2 :]], axis=0).astype(BF16)
    f_copy = remote(fpair.at[0], fpair.at[1], fs.at[0], fr.at[0], sib, z)
    f_copy.start()
    sent.append(lambda: f_copy.wait_send())
    mine = jnp.where(k == 0, total[:ROWS], total[ROWS:])
    resid = [[xb[own_block(p, kk)].astype(F32) for p in range(3)] for kk in range(2)]
    resid = [jnp.concatenate(r, axis=1) for r in resid]
    resid = [jnp.where(k == 0, r[:ROWS], r[ROWS:]) for r in resid]
    f_copy.wait_recv()
    got = fpair[1].astype(F32)
    got = jnp.concatenate([got[:ROWS], got[ROWS:]], axis=1)
    got = [jnp.where(k == kk, mine, got) for kk in range(2)]
    out[...] = jnp.concatenate([r + g for r, g in zip(resid, got)], axis=1).astype(BF16)

    for wait in sent:
        wait()


def on_device(
    hidden, queries, suffix_row_keys, suffix_row_values, prefix_cached_keys, prefix_cached_values,
    expert_norm_gain, router, gate_weight, up_weight, down_weight, adapter_down_maps,
    adapter_up_maps, routes, tenants, lengths,
):
    vmem = pl.BlockSpec(memory_space=pltpu.VMEM)
    hbm = pl.BlockSpec(memory_space=pl.ANY)
    dma = pltpu.SemaphoreType.DMA
    scratch = [
        pltpu.SMEM((TOTAL,), jnp.int32),
        pltpu.SMEM((64,), jnp.int32),
        pltpu.VMEM((ROWS, QUARTER), BF16),
        pltpu.VMEM((ROWS, QUARTER), BF16),
        pltpu.VMEM((ROWS, KV * HEAD), BF16),
        pltpu.VMEM((ROWS, KV * HEAD), BF16),
        pltpu.VMEM((EXP, WIDTH), BF16),
        pltpu.VMEM((2, TOTAL), jnp.int32),
        pltpu.VMEM((WIDTH,), BF16),
        pltpu.VMEM((1, WIDTH), F32),
        pltpu.VMEM((MSG, HEAD), BF16),
        pltpu.VMEM((2, MSG, HEAD), BF16),
        pltpu.VMEM((CHIPS, BLK, HEAD), BF16),
        pltpu.VMEM((2 * PREFIX, HEAD), BF16),
        pltpu.VMEM((2 * PREFIX, HEAD), BF16),
        pltpu.VMEM((CHIPS, MSG, HEAD), BF16),
        pltpu.VMEM((CHIPS, MSG, HEAD), BF16),
        pltpu.VMEM((2, GROUP, ROWS, HEAD), F32),
        pltpu.VMEM((PAIR, 128), F32),
        pltpu.VMEM((PREFIX, HEAD), BF16),
        pltpu.VMEM((PREFIX, HEAD), BF16),
        pltpu.VMEM((2, 3, 4, 4, 4, PAIR, THIRD), BF16),
        pltpu.VMEM((WIDTH, UNITS), BF16),
        pltpu.VMEM((WIDTH, UNITS), BF16),
        pltpu.VMEM((2 * UNITS, HALF), BF16),
        pltpu.VMEM((1024, UNITS), BF16),
        pltpu.VMEM((128, HALF), BF16),
        pltpu.VMEM((TOTAL, UNITS), F32),
        pltpu.VMEM((TOTAL, UNITS), F32),
        pltpu.VMEM((TOTAL, 128), F32),
        pltpu.VMEM((TOTAL, PAIR), F32),
        pltpu.VMEM((PAIR, WIDTH), BF16),
        pltpu.VMEM((TOTAL, PAIR), F32),
        pltpu.VMEM((4, 4, PAIR, 128), BF16),
        pltpu.VMEM((4, 4, PAIR, 128), BF16),
        pltpu.VMEM((4, PAIR, 128), BF16),
        pltpu.VMEM((4, PAIR, 128), BF16),
        pltpu.VMEM((2, PAIR, 128), BF16),
        pltpu.VMEM((EXP, PAIR, PART), BF16),
        pltpu.VMEM((EXP, PAIR, PART), BF16),
        pltpu.VMEM((TOTAL, UNITS), BF16),
        pltpu.VMEM((TOTAL, UNITS), BF16),
        pltpu.VMEM((3, 4, 4, 4, PAIR, THIRD), BF16),
        pltpu.VMEM((3, 4, 4, 4, PAIR, THIRD), BF16),
        pltpu.VMEM((3, 4, 4, PAIR, THIRD), BF16),
        pltpu.VMEM((3, 4, 4, PAIR, THIRD), BF16),
        pltpu.VMEM((3, 4, PAIR, THIRD), BF16),
        pltpu.VMEM((3, 4, PAIR, THIRD), BF16),
        pltpu.VMEM((2, PAIR, PART // 2), BF16),
        dma((24,)),
        dma((1,)),
        dma((1,)),
        dma((2,)),
        dma((2,)),
        dma((CHIPS,)),
        dma((CHIPS,)),
        dma((CHIPS,)),
        dma((CHIPS,)),
        dma((3, 3, 4)),
        dma((3, 3, 4)),
        dma((3, 4)),
        dma((3, 4)),
        dma((4,)),
        dma((4,)),
        dma((2, 4)),
        dma((2, 4)),
        dma((1,)),
        dma((1,)),
        dma((4,)),
        dma((4,)),
        dma((4,)),
        dma((4,)),
        dma((1,)),
        dma((1,)),
        dma((3, 3, 4)),
        dma((3, 3, 4)),
        dma((1,)),
        dma((1,)),
    ]
    return pl.pallas_call(
        kernel,
        out_shape=jax.ShapeDtypeStruct((ROWS, QUARTER), BF16),
        in_specs=[hbm] * 16,
        out_specs=vmem,
        scratch_shapes=scratch,
        compiler_params=pltpu.CompilerParams(
            collective_id=0, has_side_effects=True, vmem_limit_bytes=58 * 1024 * 1024
        ),
        cost_estimate=pl.CostEstimate(flops=5 * 10**9, bytes_accessed=13 * 2**20, transcendentals=7 * 10**6),
        name="layer",
    )(
        hidden, queries, suffix_row_keys, suffix_row_values, prefix_cached_keys,
        prefix_cached_values, expert_norm_gain, router.T,
        gate_weight.reshape(WIDTH, UNITS), up_weight.reshape(WIDTH, UNITS),
        down_weight.reshape(UNITS, WIDTH), adapter_down_maps.reshape(-1, UNITS),
        adapter_up_maps.reshape(-1, WIDTH), routes.T, tenants, lengths,
    )


def solution(mesh):
    in_specs = (
        P("seq", "exp"),
        P("seq", "exp"),
        P("seq", "exp"),
        P("seq", "exp"),
        P("seq", "exp"),
        P("seq", "exp"),
        P(),
        P(),
        P("exp", None, "seq"),
        P("exp", None, "seq"),
        P("exp", "seq", None),
        P(None, "exp", None, "seq"),
        P("seq", "exp", None, None),
        P(),
        P(),
        P(),
    )
    return jax.shard_map(
        on_device, mesh=mesh, in_specs=in_specs, out_specs=P("seq", "exp"), check_vma=False
    )
```

```python
import functools

import jax
import jax.numpy as jnp
from jax import lax
from jax.experimental import pallas as pl
from jax.experimental.pallas import tpu as pltpu
from jax.sharding import PartitionSpec as P

MESH = pl.DeviceIdType.MESH
F32 = jnp.float32
BF16 = jnp.bfloat16

HEAD = 128
GROUP = 6
KV = 2
HEADS = KV * GROUP
ROWS = 8
SEQ = 32
EXP = 4
CHIPS = SEQ // 2
PAIR = 2 * ROWS
TOTAL = SEQ * ROWS
WIDTH = 6144
HALF = WIDTH // 2
QUARTER = WIDTH // EXP
PREFIX = 2048
UNITS = 256
QB = GROUP * ROWS
BLK = 2 * QB
MSG = BLK + 16
PART = GROUP * HEAD
THIRD = PART // 3
AHEAD = (1, 3, 2, 0)
KEYS = 512
NORM_EPS = 1e-05
LOG2E = 1.4426950408889634
SCALE2 = HEAD**-0.5 * LOG2E


def dot(a, b):
    return jnp.dot(a, b, preferred_element_type=F32)


def dot_t(a, b):
    return lax.dot_general(a, b, (((1,), (1,)), ((), ())), preferred_element_type=F32)


def iota(shape, dim):
    return lax.broadcasted_iota(jnp.int32, shape, dim)


def three_parts(v):
    high = v.astype(BF16).astype(F32)
    rest = v - high
    mid = rest.astype(BF16).astype(F32)
    low = rest - mid
    ax = v.ndim - 1
    return high + pltpu.roll(mid, 16, ax) + pltpu.roll(low, 32, ax)


def whole_of(p):
    ax = p.ndim - 1
    return p + pltpu.roll(p, 128 - 16, ax) + pltpu.roll(p, 128 - 32, ax)


N_SMALL = 9


def kernel(
    hid, qry, skey, sval, pk, pv, gain, rout, wg, wu, wd, adn, aup, routes, tenants_h, lengths_h,
    out,
    tenants, lengths,
    hid_v, qry_v, skey_v, sval_v, rout_v, routes_v, gain_v, gainf, msnd, pairb, qall, kbuf, vbuf, sbuf, pbuf,
    suf_o, suf_l, ksnd, vsnd, xb, wgb, wub, wdb, adnb, upb,
    accg, accu, accs, accl, rpad, rcol, lsnd, lrcv, lsum, lrow, lpair, asnd, arcv, usnd, urcv,
    p2, r2, p3, r3, p4, r4, fpair,
    lsem, ms, mr, ks, kr, qs, qr, ps, pr, gs, gr, hs, hr, ups, upr, ls, lr, lps, lpr, as_, ar,
    ds, dr, us, ur, ss, sr, fs, fr,
):
    s = lax.axis_index("seq")
    z = lax.axis_index("exp")
    k = lax.rem(s, 2)
    c = lax.div(s, 2)
    x = lax.rem(c, 4)
    y = lax.div(c, 4)
    sib = s + 1 - 2 * k
    sent = []

    def remote(src, dst, ssem, rsem, seq, exp):
        return pltpu.make_async_remote_copy(
            src_ref=src, dst_ref=dst, send_sem=ssem, recv_sem=rsem,
            device_id=(seq, exp), device_id_type=MESH,
        )

    def each(n, body, first=0):
        def step(i, carry):
            body(i)
            return carry

        lax.fori_loop(first, n, step, 0)

    def chip_at(i):
        return lax.rem(y + i // 4, 4) * 4 + lax.rem(x + i % 4, 4)

    barrier = pltpu.get_barrier_semaphore()

    def greet(seq, exp):
        pl.semaphore_signal(barrier, inc=1, device_id=(seq, exp), device_id_type=MESH)

    for i in (10, 6, 14, 9, 11, 2, 8, 5, 7, 13, 15, 1, 3, 4, 12):
        greet(chip_at(i) * 2 + k, z)
    for d in (2, 1, 3):
        greet(s, lax.rem(z + d, EXP))
    greet(sib, z)

    own_head = pl.ds(pl.multiple_of(k * HEAD, HEAD), HEAD)
    sib_head = pl.ds(pl.multiple_of(HEAD - k * HEAD, HEAD), HEAD)
    up_row = pl.multiple_of(64 * lax.rem(c, 2) + 32 * k, 32)
    def up_part(zz, core):
        at = pl.multiple_of(zz * QUARTER + core * PART, PART)
        return aup.at[:, pl.ds(at, PART)], upb.at[pl.ds(up_row, 32), pl.ds(zz * PART, PART)]

    def down_part(zz, core):
        at = pl.multiple_of(zz * QUARTER + core * PART, PART)
        rows = 0 if core is k else UNITS
        return wd.at[:, pl.ds(at, PART)], wdb.at[pl.ds(rows, UNITS), pl.ds(zz * PART, PART)]

    loads = [
        (qry, qry_v),
        (hid, hid_v),
        (skey, skey_v),
        (sval, sval_v),
        (gain, gain_v),
        (rout, rout_v),
        (routes, routes_v),
        (tenants_h, tenants),
        (lengths_h, lengths),
        (pk.at[:, own_head], kbuf.at[pl.ds(0, PREFIX), :]),
        (pv.at[:, own_head], vbuf.at[pl.ds(0, PREFIX), :]),
        (pk.at[:, sib_head], ksnd),
        (pv.at[:, sib_head], vsnd),
        (wg, wgb),
        (wu, wub),
        (adn, adnb),
    ] + [part(zz, k) for part in (up_part, down_part) for zz in range(EXP)]
    loads = [pltpu.make_async_copy(a, b, lsem.at[i]) for i, (a, b) in enumerate(loads)]
    for cp in loads:
        cp.start()
    other_rows = pl.multiple_of(64 - 64 * lax.rem(c, 2), 64)
    upb[pl.ds(other_rows, 64), :] = jnp.zeros((64, HALF), BF16)
    for cp in loads[:N_SMALL]:
        cp.wait()
    gainf[...] = gain_v[...].astype(F32).reshape(1, WIDTH)

    q, h = qry_v[...].astype(F32), hid_v[...].astype(F32)
    kv = [skey_v[...].astype(F32), sval_v[...].astype(F32)]
    by_head = []
    for g in range(KV):
        tiles = [a[:, (g * GROUP + j) * HEAD : (g * GROUP + j + 1) * HEAD] for a in (q, h) for j in range(GROUP)]
        tiles = tiles + [a[:, g * HEAD : (g + 1) * HEAD] for a in kv]
        by_head.append(jnp.concatenate(tiles, axis=0))
    pairb[k] = jnp.where(k == 0, by_head[0], by_head[1]).astype(BF16)
    msnd[...] = jnp.where(k == 0, by_head[1], by_head[0]).astype(BF16)
    pl.semaphore_wait(barrier, CHIPS + EXP - 1)

    m_copy = remote(msnd, pairb.at[k], ms.at[0], mr.at[0], sib, z)
    m_copy.start()
    kv_copies = [
        remote(ksnd, kbuf.at[pl.ds(PREFIX, PREFIX), :], ks.at[0], kr.at[0], sib, z),
        remote(vsnd, vbuf.at[pl.ds(PREFIX, PREFIX), :], ks.at[1], kr.at[1], sib, z),
    ]
    for cp in loads[N_SMALL + 2 : N_SMALL + 4]:
        cp.wait()
    sent.append(lambda: [cp.wait_send() for cp in (m_copy, *kv_copies)])
    remote(msnd, pairb.at[1 - k], ms.at[0], mr.at[0], sib, z).wait_recv()

    own = [pairb[kk, 0:QB, :] for kk in range(2)]
    qall[c] = jnp.concatenate(own, axis=0)
    order = (12, 13, 14, 15, 4, 5, 6, 7, 8, 9, 10, 11, 1, 2, 3)

    def q_send(i):
        return remote(qall.at[c], qall.at[c], qs.at[i], qr.at[c], chip_at(i) * 2 + k, z)

    for i in order[:4]:
        q_send(i).start()
    kv_copies[0].start()
    for i in order[4:]:
        q_send(i).start()
    kv_copies[1].start()
    sent.append(lambda: [q_send(i).wait_send() for i in order])
    up_copies = []
    for zz in range(EXP):
        src, dst = up_part(zz, 1 - k)
        up_copies.append(remote(src, dst, ups.at[zz], upr.at[zz], sib, z))
    down_copies = []
    for zz in range(EXP):
        src, dst = down_part(zz, 1 - k)
        down_copies.append(remote(src, dst, ds.at[zz], dr.at[zz], sib, z))
    for cp in up_copies + down_copies:
        cp.start()
    sent.append(lambda: [cp.wait_send() for cp in up_copies + down_copies])

    def stacked(rows):
        index = iota((PAIR, rows.shape[1]), 0)
        got = jnp.zeros(index.shape, F32)
        for i in range(rows.shape[0]):
            got = jnp.where(index == i, rows[i : i + 1], got)
        return got.astype(BF16)

    rpad[...] = stacked(rout_v[...].astype(F32))
    eye = (iota((TOTAL, TOTAL), 0) == iota((TOTAL, TOTAL), 1)).astype(F32).astype(BF16)
    rcol[...] = dot_t(eye, stacked(routes_v[...].astype(F32)))

    row16 = iota((PAIR, 128), 0)
    lane16 = iota((PAIR, 128), 1)
    ten = [tenants[c * PAIR + i] for i in range(PAIR)]
    pos = []
    for i in range(PAIR):
        p = jnp.int32(0)
        for j in range(i // ROWS * ROWS, i):
            p = p + (ten[i] == ten[j]).astype(jnp.int32)
        pos.append(p)
    lens = [lengths[t] for t in ten]

    def spread(values, at):
        got = jnp.full((PAIR, 128), -1, jnp.int32)
        for i, v in enumerate(values):
            got = jnp.where(at == i, v, got)
        return got

    ten_rows = spread(ten, row16)
    pos_c = spread(pos, lane16)
    visible = (lane16 < PAIR) & (ten_rows == spread(ten, lane16))
    visible = visible & (pos_c <= spread(pos, row16)) & (pos_c < spread(lens, row16))
    pairs = [pairb[kk, BLK:, :].astype(F32) for kk in range(2)]
    fill = jnp.zeros((128 - PAIR, HEAD), F32)
    keys = jnp.concatenate([pairs[0][:ROWS], pairs[1][:ROWS], fill], axis=0).astype(BF16)
    values = jnp.concatenate([pairs[0][ROWS:], pairs[1][ROWS:], fill], axis=0).astype(BF16)
    for kk in range(2):
        seen = visible[kk * ROWS : (kk + 1) * ROWS]
        seen = jnp.broadcast_to(seen[None], (GROUP, ROWS, 128))
        sc = dot_t(pairb[kk, 0:QB, :], keys).reshape(GROUP, ROWS, 128)
        sc = jnp.where(seen, sc, -1e30)
        m = jnp.max(sc, axis=2, keepdims=True)
        w = jnp.where(seen, jnp.exp2((sc - m) * SCALE2), 0.0)
        mass = jnp.sum(w, axis=2, keepdims=True)
        acc = dot(w.reshape(QB, 128).astype(BF16), values).reshape(GROUP, ROWS, HEAD)
        suf_o[kk] = acc / mass
        lse = jnp.broadcast_to(m * SCALE2 + jnp.log2(mass), (GROUP, ROWS, 128))
        stat = jnp.zeros((ROWS, 128), F32)
        for j in range(GROUP):
            stat = jnp.where(lane16[:ROWS] == j, lse[j], stat)
        suf_l[kk * ROWS : (kk + 1) * ROWS, :] = stat

    for cp in loads[N_SMALL : N_SMALL + 2]:
        cp.wait()
    for cp in kv_copies:
        cp.wait_recv()

    def q_wait(i):
        chip = chip_at(i)
        remote(qall.at[c], qall.at[chip], qs.at[0], qr.at[chip], chip * 2 + k, z).wait_recv()

    tiles = [(u, at) for u in range(4) for at in range(0, 2 * PREFIX, KEYS)]
    queries = {}
    ones = jnp.ones((KEYS, HEAD), BF16)

    def scores(u, at):
        if at == 0:
            a = AHEAD[u]
            for i in range(4 * a, 4 * a + 4):
                if i:
                    q_wait(i)
            queries[u] = qall[pl.ds(lax.rem(y + a, 4) * 4, 4)].reshape(4 * BLK, HEAD)
        return dot_t(queries[u], kbuf[at : at + KEYS, :])

    def finish(u, m, acc):
        mass = acc[:, HEAD:]
        o = (acc[:, :HEAD] / mass).astype(BF16).reshape(4, BLK, HEAD)
        lse = (m + jnp.log2(mass)).reshape(8, GROUP, ROWS, 128)
        lane = iota((8, ROWS, 128), 2)
        stat = jnp.zeros((8, ROWS, 128), F32)
        for j in range(GROUP):
            stat = jnp.where(lane == j, lse[:, j], stat)
        a = AHEAD[u]
        at = pl.ds(lax.rem(y + a, 4) * 4, 4)
        sbuf[at, 0:BLK, :] = o
        sbuf[at, BLK:, :] = three_parts(stat).reshape(4, PAIR, 128).astype(BF16)
        for i in range(4 * a, 4 * a + 4):
            if i:
                p_copy(i).start()

    def p_copy(i):
        chip = chip_at(i)
        return remote(sbuf.at[chip], pbuf.at[c], ps.at[i], pr.at[c], chip * 2 + k, z)

    coming = scores(*tiles[0])
    m = acc = done = None
    for n, (u, at) in enumerate(tiles):
        sc = coming * SCALE2
        if n + 1 < len(tiles):
            coming = scores(*tiles[n + 1])
        if done is not None:
            finish(*done)
            done = None
        top = jnp.max(sc, axis=1, keepdims=True)
        top = top if at == 0 else jnp.maximum(m, top)
        got = dot(jnp.exp2(sc - top).astype(BF16), jnp.concatenate([vbuf[at : at + KEYS, :], ones], axis=1))
        acc = got if at == 0 else acc * jnp.exp2(m - top) + got
        m = top
        if at + KEYS == 2 * PREFIX:
            done = (u, m, acc)
    finish(*done)
    sent.append(lambda: [p_copy(i).wait_send() for i in range(1, CHIPS)])

    pbuf[c] = sbuf[c]

    def p_wait(i):
        chip = chip_at(i)
        remote(sbuf.at[chip], pbuf.at[chip], ps.at[0], pr.at[chip], chip * 2 + k, z).wait_recv()

    def merged(rows, top, mass, att):
        at = [pl.ds(lax.rem(y + a, 4) * 4, 4) for a in rows]
        lses = whole_of(jnp.concatenate([pbuf[i, BLK:, :] for i in at], axis=0).astype(F32))
        new = jnp.maximum(top, jnp.max(lses, axis=0))
        shares = jnp.exp2(lses - new[None])
        old = jnp.exp2(top - new)
        mass = mass * old + jnp.sum(shares, axis=0)
        for kk in range(2):
            side = slice(kk * ROWS, (kk + 1) * ROWS)
            for j in range(GROUP):
                att[kk, j] = old[side, j : j + 1] * att[kk, j]
        for n, i in enumerate(at):
            part = pbuf[i, 0:BLK, :].astype(F32)
            for m in range(4):
                for kk in range(2):
                    side = slice(kk * ROWS, (kk + 1) * ROWS)
                    for j in range(GROUP):
                        tile = part[m, (kk * GROUP + j) * ROWS : (kk * GROUP + j + 1) * ROWS]
                        att[kk, j] = att[kk, j] + shares[4 * n + m, side, j : j + 1] * tile
        return new, mass, att

    att = {(kk, j): suf_o[kk, j] for kk in range(2) for j in range(GROUP)}
    state = suf_l[...], jnp.ones((PAIR, 128), F32), att
    for i in range(4, CHIPS):
        p_wait(i)
    state = merged((1, 2, 3), *state)
    for i in range(1, 4):
        p_wait(i)
    _, mass, att = merged((0,), *state)
    inverse = 1.0 / mass
    for kk in range(2):
        side = slice(kk * ROWS, (kk + 1) * ROWS)
        hidden = pairb[kk, QB : 2 * QB, :].astype(F32)
        for j in range(GROUP):
            att[kk, j] = hidden[j * ROWS : (j + 1) * ROWS] + inverse[side, j : j + 1] * att[kk, j]

    here = {"x": x, "y": y, "z": z}
    orders = ("xyz", "yzx", "zxy")

    def region(p, step, core=k, **at):
        at = {**here, **at}
        index = [at[a] for a in orders[p][: step - 1 if step else None : -1]]
        return xb.at[(core, p, *index)]

    def peer(axis, d):
        at = {**here, axis: lax.rem(here[axis] + d, 4)}
        return at[axis], (at["y"] * 4 + at["x"]) * 2 + k, at["z"]

    def g_send(p, step, d):
        axis = orders[p][step]
        _, seq, exp = peer(axis, d)
        block = region(p, step)
        return remote(block, block, gs.at[p, step, d], gr.at[p, step, here[axis]], seq, exp)

    def g_wait(p, step, d):
        axis = orders[p][step]
        there, seq, exp = peer(axis, d)
        block = region(p, step, **{axis: there})
        remote(block, block, gs.at[p, step, 0], gr.at[p, step, there], seq, exp).wait_recv()

    def h_copy(p, there, core):
        block = xb.at[core, p, there]
        return remote(block, block, hs.at[p, there], hr.at[p, there], sib, z)

    def own_block(p, core):
        return (core, p, *[here[a] for a in reversed(orders[p])])

    for p in range(3):
        rows = [jnp.concatenate([att[kk, j] for j in (2 * p, 2 * p + 1)], axis=1) for kk in range(2)]
        xb[own_block(p, k)] = jnp.concatenate(rows, axis=0).astype(BF16)
    for d in (2, 1, 3):
        for p in range(3):
            g_send(p, 0, d).start()
    for step in (1, 2):
        for p in range(3):
            for d in (1, 3, 2):
                g_wait(p, step - 1, d)
            for d in (2, 1, 3):
                g_send(p, step, d).start()
    for p in range(3):
        h_copy(p, here[orders[p][2]], k).start()
    for d in (1, 3, 2):
        for p in range(3):
            g_wait(p, 2, d)
            h_copy(p, peer(orders[p][2], d)[0], k).start()

    def rows_sent():
        for p in range(3):
            for step in range(3):
                for d in (1, 2, 3):
                    g_send(p, step, d).wait_send()
            for there in range(4):
                h_copy(p, there, k).wait_send()

    sent.append(rows_sent)

    for cp in loads[N_SMALL + 4 : N_SMALL + 6]:
        cp.wait()

    def project(core, sums):
        for zz in range(EXP):
            at = pl.multiple_of(zz * QUARTER + core * PART, PART)
            turned = xb[core, 1, :, zz]
            turned = jnp.stack([turned[i, j] for j in range(4) for i in range(4)])
            rows = [xb[core, 0, zz], turned, xb[core, 2, :, :, zz]]
            rows = jnp.concatenate([r.reshape(TOTAL, THIRD) for r in rows], axis=1).astype(F32)
            squares = rows * rows
            total = squares[:, 0:128]
            for i in range(1, PART // 128):
                total = total + squares[:, i * 128 : (i + 1) * 128]
            rows = (rows * gainf[:, pl.ds(at, PART)]).astype(BF16)
            got = (
                total,
                dot(rows, wgb[pl.ds(at, PART), :]),
                dot(rows, wub[pl.ds(at, PART), :]),
                dot_t(rows, rpad[:, pl.ds(at, PART)]),
            )
            sums = got if sums is None else tuple(a + b for a, b in zip(sums, got))
        return sums

    for ref, value in zip((accs, accg, accu, accl), project(k, None)):
        ref[...] = value
    for p in range(3):
        for there in range(4):
            h_copy(p, there, 1 - k).wait_recv()
    squares, gate, up, logits = project(1 - k, tuple(ref[...] for ref in (accs, accg, accu, accl)))
    scale = lax.rsqrt(jnp.sum(squares, axis=1, keepdims=True) / WIDTH + NORM_EPS)
    gate = gate * scale
    logits = logits * scale
    first, second = rcol[:, 0:1], rcol[:, 1:2]
    expert = iota((TOTAL, PAIR), 1).astype(F32)
    here_e = z.astype(F32)
    mine = jnp.sum(jnp.where(expert == here_e, logits, 0.0), axis=1, keepdims=True)
    theirs = jnp.sum(jnp.where(expert == first + second - here_e, logits, 0.0), axis=1, keepdims=True)
    share = 1.0 / (1.0 + jnp.exp(theirs - mine))
    share = jnp.where((first == here_e) | (second == here_e), share, 0.0)
    units = (gate / (1.0 + jnp.exp(-gate)) * (up * scale) * share).astype(BF16)

    usnd[...] = units
    u_copy = remote(usnd, urcv, us.at[0], ur.at[0], sib, z)
    u_copy.start()
    sent.append(lambda: u_copy.wait_send())

    for cp in loads[N_SMALL + 6 :]:
        cp.wait()
    for i in range(CHIPS // 2):
        low = dot_t(units[i * 32 : (i + 1) * 32], adnb[i * 128 : (i + 1) * 128, :])
        for j in range(2):
            lsnd[i % 2 * 2 + j, i // 2] = low[j * PAIR : (j + 1) * PAIR].astype(BF16)

    def low_copy(step, d):
        axis = "xy"[step]
        there, seq, exp = peer(axis, d)
        src, dst = ((lsnd, lrcv), (lsum, lrow))[step]
        mine = here[axis]
        return remote(src.at[there], dst.at[mine], ls.at[step, d], lr.at[step, mine], seq, exp)

    def low_sum(step):
        axis = "xy"[step]
        src, dst = ((lsnd, lrcv), (lsum, lrow))[step]
        total = src[here[axis]].astype(F32)
        for d in (1, 3, 2):
            there, seq, exp = peer(axis, d)
            remote(
                src.at[here[axis]], dst.at[there], ls.at[step, 0], lr.at[step, there], seq, exp
            ).wait_recv()
            total = total + dst[there].astype(F32)
        return total

    for d in (2, 1, 3):
        low_copy(0, d).start()
    sent.append(lambda: [low_copy(step, d).wait_send() for step in range(2) for d in (1, 2, 3)])

    sum_orders = ("zyx", "xzy", "yxz")

    def part_of(t, step, there):
        if step == 1 and t == 2:
            return p3.at[t, :, there]
        return (p2, p3, p4)[step].at[t, there]

    def s_send(t, step, d):
        axis = sum_orders[t][step]
        there, seq, exp = peer(axis, d)
        return remote(
            part_of(t, step, there), (r2, r3, r4)[step].at[t, here[axis]],
            ss.at[t, step, d], sr.at[t, step, here[axis]], seq, exp,
        )

    def s_sum(t, step):
        axis = sum_orders[t][step]
        into = (r2, r3, r4)[step]
        total = part_of(t, step, here[axis])[...].astype(F32)
        for d in (1, 3, 2):
            there, seq, exp = peer(axis, d)
            remote(
                part_of(t, step, here[axis]), into.at[t, there],
                ss.at[t, step, 0], sr.at[t, step, there], seq, exp,
            ).wait_recv()
            total = total + into[t, there].astype(F32)
        return total

    def s_start(t, step):
        for d in (2, 1, 3):
            s_send(t, step, d).start()

    u_copy.wait_recv()
    for cp in down_copies:
        cp.wait_recv()
    both_units = jnp.concatenate([units, urcv[...]], axis=1)
    for t in range(3):
        for zz in range(EXP):
            at = zz * PART + t * THIRD
            both = dot(both_units, wdb[:, at : at + THIRD]).astype(BF16).reshape(4, 4, PAIR, THIRD)
            if t == 0:
                p2[t, zz] = both
            elif t == 1:
                for i in range(4):
                    p2[t, i, zz] = both[:, i]
            else:
                p2[t, :, zz] = both
        s_start(t, 0)
    sent.append(
        lambda: [s_send(t, i, d).wait_send() for t in range(3) for i in range(3) for d in (1, 2, 3)]
    )

    lsum[...] = low_sum(0).astype(BF16)
    for d in (2, 1, 3):
        low_copy(1, d).start()
    for t in range(3):
        p3[t] = s_sum(t, 0).astype(BF16)
        s_start(t, 1)

    low = low_sum(1)
    lpair[0] = low.astype(BF16)
    lp_copy = remote(lpair.at[0], lpair.at[1], lps.at[0], lpr.at[0], sib, z)
    lp_copy.start()
    sent.append(lambda: lp_copy.wait_send())
    for cp in up_copies:
        cp.wait_recv()
    lp_copy.wait_recv()
    low = low + lpair[1].astype(F32)
    low = jnp.where(lax.div(lane16, 16) == lax.rem(ten_rows, 8), low, 0.0).astype(BF16)
    for zz in range(EXP):
        asnd[zz] = dot(low, upb[:, zz * PART : (zz + 1) * PART]).astype(BF16)

    def a_copy(d):
        zz = lax.rem(z + d, EXP)
        return remote(asnd.at[zz], arcv.at[z], as_.at[d], ar.at[z], s, zz)

    for d in (2, 1, 3):
        a_copy(d).start()
    sent.append(lambda: [a_copy(d).wait_send() for d in (1, 2, 3)])

    for t in range(3):
        p4[t] = s_sum(t, 1).astype(BF16)
        s_start(t, 2)
    adapter = asnd[z].astype(F32)
    for d in (1, 3, 2):
        zz = lax.rem(z + d, EXP)
        remote(asnd.at[z], arcv.at[zz], as_.at[0], ar.at[zz], s, zz).wait_recv()
        adapter = adapter + arcv[zz].astype(F32)
    total = jnp.concatenate([s_sum(t, 2) for t in range(3)], axis=1) + adapter

    theirs = jnp.where(k == 0, total[ROWS:], total[:ROWS])
    fpair[0] = jnp.concatenate([theirs[:, : PART // 2], theirs[:, PART // 2 :]], axis=0).astype(BF16)
    f_copy = remote(fpair.at[0], fpair.at[1], fs.at[0], fr.at[0], sib, z)
    f_copy.start()
    sent.append(lambda: f_copy.wait_send())
    mine = jnp.where(k == 0, total[:ROWS], total[ROWS:])
    resid = [[xb[own_block(p, kk)].astype(F32) for p in range(3)] for kk in range(2)]
    resid = [jnp.concatenate(r, axis=1) for r in resid]
    resid = [jnp.where(k == 0, r[:ROWS], r[ROWS:]) for r in resid]
    f_copy.wait_recv()
    got = fpair[1].astype(F32)
    got = jnp.concatenate([got[:ROWS], got[ROWS:]], axis=1)
    got = [jnp.where(k == kk, mine, got) for kk in range(2)]
    out[...] = jnp.concatenate([r + g for r, g in zip(resid, got)], axis=1).astype(BF16)

    for wait in sent:
        wait()


def on_device(
    hidden, queries, suffix_row_keys, suffix_row_values, prefix_cached_keys, prefix_cached_values,
    expert_norm_gain, router, gate_weight, up_weight, down_weight, adapter_down_maps,
    adapter_up_maps, routes, tenants, lengths,
):
    vmem = pl.BlockSpec(memory_space=pltpu.VMEM)
    hbm = pl.BlockSpec(memory_space=pl.ANY)
    dma = pltpu.SemaphoreType.DMA
    scratch = [
        pltpu.SMEM((TOTAL,), jnp.int32),
        pltpu.SMEM((64,), jnp.int32),
        pltpu.VMEM((ROWS, QUARTER), BF16),
        pltpu.VMEM((ROWS, QUARTER), BF16),
        pltpu.VMEM((ROWS, KV * HEAD), BF16),
        pltpu.VMEM((ROWS, KV * HEAD), BF16),
        pltpu.VMEM((EXP, WIDTH), BF16),
        pltpu.VMEM((2, TOTAL), jnp.int32),
        pltpu.VMEM((WIDTH,), BF16),
        pltpu.VMEM((1, WIDTH), F32),
        pltpu.VMEM((MSG, HEAD), BF16),
        pltpu.VMEM((2, MSG, HEAD), BF16),
        pltpu.VMEM((CHIPS, BLK, HEAD), BF16),
        pltpu.VMEM((2 * PREFIX, HEAD), BF16),
        pltpu.VMEM((2 * PREFIX, HEAD), BF16),
        pltpu.VMEM((CHIPS, MSG, HEAD), BF16),
        pltpu.VMEM((CHIPS, MSG, HEAD), BF16),
        pltpu.VMEM((2, GROUP, ROWS, HEAD), F32),
        pltpu.VMEM((PAIR, 128), F32),
        pltpu.VMEM((PREFIX, HEAD), BF16),
        pltpu.VMEM((PREFIX, HEAD), BF16),
        pltpu.VMEM((2, 3, 4, 4, 4, PAIR, THIRD), BF16),
        pltpu.VMEM((WIDTH, UNITS), BF16),
        pltpu.VMEM((WIDTH, UNITS), BF16),
        pltpu.VMEM((2 * UNITS, HALF), BF16),
        pltpu.VMEM((1024, UNITS), BF16),
        pltpu.VMEM((128, HALF), BF16),
        pltpu.VMEM((TOTAL, UNITS), F32),
        pltpu.VMEM((TOTAL, UNITS), F32),
        pltpu.VMEM((TOTAL, 128), F32),
        pltpu.VMEM((TOTAL, PAIR), F32),
        pltpu.VMEM((PAIR, WIDTH), BF16),
        pltpu.VMEM((TOTAL, PAIR), F32),
        pltpu.VMEM((4, 4, PAIR, 128), BF16),
        pltpu.VMEM((4, 4, PAIR, 128), BF16),
        pltpu.VMEM((4, PAIR, 128), BF16),
        pltpu.VMEM((4, PAIR, 128), BF16),
        pltpu.VMEM((2, PAIR, 128), BF16),
        pltpu.VMEM((EXP, PAIR, PART), BF16),
        pltpu.VMEM((EXP, PAIR, PART), BF16),
        pltpu.VMEM((TOTAL, UNITS), BF16),
        pltpu.VMEM((TOTAL, UNITS), BF16),
        pltpu.VMEM((3, 4, 4, 4, PAIR, THIRD), BF16),
        pltpu.VMEM((3, 4, 4, 4, PAIR, THIRD), BF16),
        pltpu.VMEM((3, 4, 4, PAIR, THIRD), BF16),
        pltpu.VMEM((3, 4, 4, PAIR, THIRD), BF16),
        pltpu.VMEM((3, 4, PAIR, THIRD), BF16),
        pltpu.VMEM((3, 4, PAIR, THIRD), BF16),
        pltpu.VMEM((2, PAIR, PART // 2), BF16),
        dma((24,)),
        dma((1,)),
        dma((1,)),
        dma((2,)),
        dma((2,)),
        dma((CHIPS,)),
        dma((CHIPS,)),
        dma((CHIPS,)),
        dma((CHIPS,)),
        dma((3, 3, 4)),
        dma((3, 3, 4)),
        dma((3, 4)),
        dma((3, 4)),
        dma((4,)),
        dma((4,)),
        dma((2, 4)),
        dma((2, 4)),
        dma((1,)),
        dma((1,)),
        dma((4,)),
        dma((4,)),
        dma((4,)),
        dma((4,)),
        dma((1,)),
        dma((1,)),
        dma((3, 3, 4)),
        dma((3, 3, 4)),
        dma((1,)),
        dma((1,)),
    ]
    return pl.pallas_call(
        kernel,
        out_shape=jax.ShapeDtypeStruct((ROWS, QUARTER), BF16),
        in_specs=[hbm] * 16,
        out_specs=vmem,
        scratch_shapes=scratch,
        compiler_params=pltpu.CompilerParams(
            collective_id=0, has_side_effects=True, vmem_limit_bytes=58 * 1024 * 1024
        ),
        cost_estimate=pl.CostEstimate(flops=5 * 10**9, bytes_accessed=13 * 2**20, transcendentals=7 * 10**6),
        name="layer",
    )(
        hidden, queries, suffix_row_keys, suffix_row_values, prefix_cached_keys,
        prefix_cached_values, expert_norm_gain, router.T,
        gate_weight.reshape(WIDTH, UNITS), up_weight.reshape(WIDTH, UNITS),
        down_weight.reshape(UNITS, WIDTH), adapter_down_maps.reshape(-1, UNITS),
        adapter_up_maps.reshape(-1, WIDTH), routes.T, tenants, lengths,
    )


def solution(mesh):
    in_specs = (
        P("seq", "exp"),
        P("seq", "exp"),
        P("seq", "exp"),
        P("seq", "exp"),
        P("seq", "exp"),
        P("seq", "exp"),
        P(),
        P(),
        P("exp", None, "seq"),
        P("exp", None, "seq"),
        P("exp", "seq", None),
        P(None, "exp", None, "seq"),
        P("seq", "exp", None, None),
        P(),
        P(),
        P(),
    )
    return jax.shard_map(
        on_device, mesh=mesh, in_specs=in_specs, out_specs=P("seq", "exp"), check_vma=False
    )
```

```python
import functools

import jax
import jax.numpy as jnp
from jax import lax
from jax.experimental import pallas as pl
from jax.experimental.pallas import tpu as pltpu
from jax.sharding import PartitionSpec as P

MESH = pl.DeviceIdType.MESH
F32 = jnp.float32
BF16 = jnp.bfloat16

HEAD = 128
GROUP = 6
KV = 2
HEADS = KV * GROUP
ROWS = 8
SEQ = 32
EXP = 4
CHIPS = SEQ // 2
PAIR = 2 * ROWS
TOTAL = SEQ * ROWS
WIDTH = 6144
HALF = WIDTH // 2
QUARTER = WIDTH // EXP
PREFIX = 2048
UNITS = 256
QB = GROUP * ROWS
BLK = 2 * QB
MSG = BLK + 16
PART = GROUP * HEAD
THIRD = PART // 3
AHEAD = (1, 3, 2, 0)
KEYS = 512
NORM_EPS = 1e-05
LOG2E = 1.4426950408889634
SCALE2 = HEAD**-0.5 * LOG2E


def dot(a, b):
    return jnp.dot(a, b, preferred_element_type=F32)


def dot_t(a, b):
    return lax.dot_general(a, b, (((1,), (1,)), ((), ())), preferred_element_type=F32)


def iota(shape, dim):
    return lax.broadcasted_iota(jnp.int32, shape, dim)


def three_parts(v):
    high = v.astype(BF16).astype(F32)
    rest = v - high
    mid = rest.astype(BF16).astype(F32)
    low = rest - mid
    ax = v.ndim - 1
    return high + pltpu.roll(mid, 16, ax) + pltpu.roll(low, 32, ax)


def whole_of(p):
    ax = p.ndim - 1
    return p + pltpu.roll(p, 128 - 16, ax) + pltpu.roll(p, 128 - 32, ax)


N_SMALL = 9


def kernel(
    hid, qry, skey, sval, pk, pv, gain, rout, wg, wu, wd, adn, aup, routes, tenants_h, lengths_h,
    out,
    tenants, lengths,
    hid_v, qry_v, skey_v, sval_v, rout_v, routes_v, gain_v, gainf, msnd, pairb, qall, kbuf, vbuf, sbuf, pbuf,
    suf_o, suf_l, ksnd, vsnd, xb, wgb, wub, wdb, adnb, upb,
    accg, accu, accs, accl, rpad, rcol, lsnd, lrcv, lsum, lrow, lpair, asnd, arcv, usnd, urcv,
    p2, r2, p3, r3, p4, r4, fpair,
    lsem, ms, mr, ks, kr, qs, qr, ps, pr, gs, gr, hs, hr, ups, upr, ls, lr, lps, lpr, as_, ar,
    ds, dr, us, ur, ss, sr, fs, fr,
):
    s = lax.axis_index("seq")
    z = lax.axis_index("exp")
    k = lax.rem(s, 2)
    c = lax.div(s, 2)
    x = lax.rem(c, 4)
    y = lax.div(c, 4)
    sib = s + 1 - 2 * k
    sent = []

    def remote(src, dst, ssem, rsem, seq, exp):
        return pltpu.make_async_remote_copy(
            src_ref=src, dst_ref=dst, send_sem=ssem, recv_sem=rsem,
            device_id=(seq, exp), device_id_type=MESH,
        )

    def each(n, body, first=0):
        def step(i, carry):
            body(i)
            return carry

        lax.fori_loop(first, n, step, 0)

    def chip_at(i):
        return lax.rem(y + i // 4, 4) * 4 + lax.rem(x + i % 4, 4)

    barrier = pltpu.get_barrier_semaphore()

    def greet(seq, exp):
        pl.semaphore_signal(barrier, inc=1, device_id=(seq, exp), device_id_type=MESH)

    for i in (10, 6, 14, 9, 11, 2, 8, 5, 7, 13, 15, 1, 3, 4, 12):
        greet(chip_at(i) * 2 + k, z)
    for d in (2, 1, 3):
        greet(s, lax.rem(z + d, EXP))
    greet(sib, z)

    own_head = pl.ds(pl.multiple_of(k * HEAD, HEAD), HEAD)
    sib_head = pl.ds(pl.multiple_of(HEAD - k * HEAD, HEAD), HEAD)
    up_row = pl.multiple_of(64 * lax.rem(c, 2) + 32 * k, 32)
    def up_part(zz, core):
        at = pl.multiple_of(zz * QUARTER + core * PART, PART)
        return aup.at[:, pl.ds(at, PART)], upb.at[pl.ds(up_row, 32), pl.ds(zz * PART, PART)]

    def down_part(zz, core):
        at = pl.multiple_of(zz * QUARTER + core * PART, PART)
        rows = 0 if core is k else UNITS
        return wd.at[:, pl.ds(at, PART)], wdb.at[pl.ds(rows, UNITS), pl.ds(zz * PART, PART)]

    loads = [
        (qry, qry_v),
        (hid, hid_v),
        (skey, skey_v),
        (sval, sval_v),
        (gain, gain_v),
        (rout, rout_v),
        (routes, routes_v),
        (tenants_h, tenants),
        (lengths_h, lengths),
        (pk.at[:, own_head], kbuf.at[pl.ds(0, PREFIX), :]),
        (pv.at[:, own_head], vbuf.at[pl.ds(0, PREFIX), :]),
        (pk.at[:, sib_head], ksnd),
        (pv.at[:, sib_head], vsnd),
        (wg, wgb),
        (wu, wub),
        (adn, adnb),
    ] + [part(zz, k) for part in (up_part, down_part) for zz in range(EXP)]
    loads = [pltpu.make_async_copy(a, b, lsem.at[i]) for i, (a, b) in enumerate(loads)]
    for cp in loads:
        cp.start()
    other_rows = pl.multiple_of(64 - 64 * lax.rem(c, 2), 64)
    upb[pl.ds(other_rows, 64), :] = jnp.zeros((64, HALF), BF16)
    for cp in loads[:N_SMALL]:
        cp.wait()
    gainf[...] = gain_v[...].astype(F32).reshape(1, WIDTH)

    q, h = qry_v[...].astype(F32), hid_v[...].astype(F32)
    kv = [skey_v[...].astype(F32), sval_v[...].astype(F32)]
    by_head = []
    for g in range(KV):
        tiles = [a[:, (g * GROUP + j) * HEAD : (g * GROUP + j + 1) * HEAD] for a in (q, h) for j in range(GROUP)]
        tiles = tiles + [a[:, g * HEAD : (g + 1) * HEAD] for a in kv]
        by_head.append(jnp.concatenate(tiles, axis=0))
    pairb[k] = jnp.where(k == 0, by_head[0], by_head[1]).astype(BF16)
    msnd[...] = jnp.where(k == 0, by_head[1], by_head[0]).astype(BF16)
    pl.semaphore_wait(barrier, CHIPS + EXP - 1)

    m_copy = remote(msnd, pairb.at[k], ms.at[0], mr.at[0], sib, z)
    m_copy.start()
    kv_copies = [
        remote(ksnd, kbuf.at[pl.ds(PREFIX, PREFIX), :], ks.at[0], kr.at[0], sib, z),
        remote(vsnd, vbuf.at[pl.ds(PREFIX, PREFIX), :], ks.at[1], kr.at[1], sib, z),
    ]
    for cp in loads[N_SMALL + 2 : N_SMALL + 4]:
        cp.wait()
    sent.append(lambda: [cp.wait_send() for cp in (m_copy, *kv_copies)])
    remote(msnd, pairb.at[1 - k], ms.at[0], mr.at[0], sib, z).wait_recv()

    own = [pairb[kk, 0:QB, :] for kk in range(2)]
    qall[c] = jnp.concatenate(own, axis=0)
    order = (12, 13, 14, 15, 4, 5, 6, 7, 8, 9, 10, 11, 1, 2, 3)

    def q_send(i):
        return remote(qall.at[c], qall.at[c], qs.at[i], qr.at[c], chip_at(i) * 2 + k, z)

    for i in order[:4]:
        q_send(i).start()
    kv_copies[0].start()
    for i in order[4:]:
        q_send(i).start()
    kv_copies[1].start()
    sent.append(lambda: [q_send(i).wait_send() for i in order])
    up_copies = []
    for zz in range(EXP):
        src, dst = up_part(zz, 1 - k)
        up_copies.append(remote(src, dst, ups.at[zz], upr.at[zz], sib, z))
    down_copies = []
    for zz in range(EXP):
        src, dst = down_part(zz, 1 - k)
        down_copies.append(remote(src, dst, ds.at[zz], dr.at[zz], sib, z))
    for cp in up_copies + down_copies:
        cp.start()
    sent.append(lambda: [cp.wait_send() for cp in up_copies + down_copies])

    def stacked(rows):
        index = iota((PAIR, rows.shape[1]), 0)
        got = jnp.zeros(index.shape, F32)
        for i in range(rows.shape[0]):
            got = jnp.where(index == i, rows[i : i + 1], got)
        return got.astype(BF16)

    rpad[...] = stacked(rout_v[...].astype(F32))
    eye = (iota((TOTAL, TOTAL), 0) == iota((TOTAL, TOTAL), 1)).astype(F32).astype(BF16)
    rcol[...] = dot_t(eye, stacked(routes_v[...].astype(F32)))

    row16 = iota((PAIR, 128), 0)
    lane16 = iota((PAIR, 128), 1)
    ten = [tenants[c * PAIR + i] for i in range(PAIR)]
    pos = []
    for i in range(PAIR):
        p = jnp.int32(0)
        for j in range(i // ROWS * ROWS, i):
            p = p + (ten[i] == ten[j]).astype(jnp.int32)
        pos.append(p)
    lens = [lengths[t] for t in ten]

    def spread(values, at):
        got = jnp.full((PAIR, 128), -1, jnp.int32)
        for i, v in enumerate(values):
            got = jnp.where(at == i, v, got)
        return got

    ten_rows = spread(ten, row16)
    pos_c = spread(pos, lane16)
    visible = (lane16 < PAIR) & (ten_rows == spread(ten, lane16))
    visible = visible & (pos_c <= spread(pos, row16)) & (pos_c < spread(lens, row16))
    pairs = [pairb[kk, BLK:, :].astype(F32) for kk in range(2)]
    fill = jnp.zeros((128 - PAIR, HEAD), F32)
    keys = jnp.concatenate([pairs[0][:ROWS], pairs[1][:ROWS], fill], axis=0).astype(BF16)
    values = jnp.concatenate([pairs[0][ROWS:], pairs[1][ROWS:], fill], axis=0).astype(BF16)
    for kk in range(2):
        seen = visible[kk * ROWS : (kk + 1) * ROWS]
        seen = jnp.broadcast_to(seen[None], (GROUP, ROWS, 128))
        sc = dot_t(pairb[kk, 0:QB, :], keys).reshape(GROUP, ROWS, 128)
        sc = jnp.where(seen, sc, -1e30)
        m = jnp.max(sc, axis=2, keepdims=True)
        w = jnp.where(seen, jnp.exp2((sc - m) * SCALE2), 0.0)
        mass = jnp.sum(w, axis=2, keepdims=True)
        acc = dot(w.reshape(QB, 128).astype(BF16), values).reshape(GROUP, ROWS, HEAD)
        suf_o[kk] = acc / mass
        lse = jnp.broadcast_to(m * SCALE2 + jnp.log2(mass), (GROUP, ROWS, 128))
        stat = jnp.zeros((ROWS, 128), F32)
        for j in range(GROUP):
            stat = jnp.where(lane16[:ROWS] == j, lse[j], stat)
        suf_l[kk * ROWS : (kk + 1) * ROWS, :] = stat

    for cp in loads[N_SMALL : N_SMALL + 2]:
        cp.wait()
    for cp in kv_copies:
        cp.wait_recv()

    def q_wait(i):
        chip = chip_at(i)
        remote(qall.at[c], qall.at[chip], qs.at[0], qr.at[chip], chip * 2 + k, z).wait_recv()

    tiles = [(u, at) for u in range(4) for at in range(0, 2 * PREFIX, KEYS)]
    queries = {}
    ones = jnp.ones((KEYS, HEAD), BF16)

    def scores(u, at):
        if at == 0:
            a = AHEAD[u]
            for i in range(4 * a, 4 * a + 4):
                if i:
                    q_wait(i)
            queries[u] = qall[pl.ds(lax.rem(y + a, 4) * 4, 4)].reshape(4 * BLK, HEAD)
        return dot_t(queries[u], kbuf[at : at + KEYS, :])

    def finish(u, m, acc):
        mass = acc[:, HEAD:]
        o = (acc[:, :HEAD] / mass).astype(BF16).reshape(4, BLK, HEAD)
        lse = (m + jnp.log2(mass)).reshape(8, GROUP, ROWS, 128)
        lane = iota((8, ROWS, 128), 2)
        stat = jnp.zeros((8, ROWS, 128), F32)
        for j in range(GROUP):
            stat = jnp.where(lane == j, lse[:, j], stat)
        a = AHEAD[u]
        at = pl.ds(lax.rem(y + a, 4) * 4, 4)
        sbuf[at, 0:BLK, :] = o
        sbuf[at, BLK:, :] = three_parts(stat).reshape(4, PAIR, 128).astype(BF16)
        for i in range(4 * a, 4 * a + 4):
            if i:
                p_copy(i).start()

    def p_copy(i):
        chip = chip_at(i)
        return remote(sbuf.at[chip], pbuf.at[c], ps.at[i], pr.at[c], chip * 2 + k, z)

    coming = scores(*tiles[0])
    m = acc = done = None
    for n, (u, at) in enumerate(tiles):
        sc = coming * SCALE2
        if n + 1 < len(tiles):
            coming = scores(*tiles[n + 1])
        if done is not None:
            finish(*done)
            done = None
        top = jnp.max(sc, axis=1, keepdims=True)
        top = top if at == 0 else jnp.maximum(m, top)
        got = dot(jnp.exp2(sc - top).astype(BF16), jnp.concatenate([vbuf[at : at + KEYS, :], ones], axis=1))
        acc = got if at == 0 else acc * jnp.exp2(m - top) + got
        m = top
        if at + KEYS == 2 * PREFIX:
            done = (u, m, acc)
    finish(*done)
    sent.append(lambda: [p_copy(i).wait_send() for i in range(1, CHIPS)])

    pbuf[c] = sbuf[c]

    def p_wait(i):
        chip = chip_at(i)
        remote(sbuf.at[chip], pbuf.at[chip], ps.at[0], pr.at[chip], chip * 2 + k, z).wait_recv()

    def merged(rows, top, mass, att):
        at = [pl.ds(lax.rem(y + a, 4) * 4, 4) for a in rows]
        lses = whole_of(jnp.concatenate([pbuf[i, BLK:, :] for i in at], axis=0).astype(F32))
        new = jnp.maximum(top, jnp.max(lses, axis=0))
        shares = jnp.exp2(lses - new[None])
        old = jnp.exp2(top - new)
        mass = mass * old + jnp.sum(shares, axis=0)
        for kk in range(2):
            side = slice(kk * ROWS, (kk + 1) * ROWS)
            for j in range(GROUP):
                att[kk, j] = old[side, j : j + 1] * att[kk, j]
        for n, i in enumerate(at):
            part = pbuf[i, 0:BLK, :].astype(F32)
            for m in range(4):
                for kk in range(2):
                    side = slice(kk * ROWS, (kk + 1) * ROWS)
                    for j in range(GROUP):
                        tile = part[m, (kk * GROUP + j) * ROWS : (kk * GROUP + j + 1) * ROWS]
                        att[kk, j] = att[kk, j] + shares[4 * n + m, side, j : j + 1] * tile
        return new, mass, att

    att = {(kk, j): suf_o[kk, j] for kk in range(2) for j in range(GROUP)}
    state = suf_l[...], jnp.ones((PAIR, 128), F32), att
    for i in range(4, CHIPS):
        p_wait(i)
    state = merged((1, 2, 3), *state)
    for i in range(1, 4):
        p_wait(i)
    _, mass, att = merged((0,), *state)
    inverse = 1.0 / mass
    for kk in range(2):
        side = slice(kk * ROWS, (kk + 1) * ROWS)
        hidden = pairb[kk, QB : 2 * QB, :].astype(F32)
        for j in range(GROUP):
            att[kk, j] = hidden[j * ROWS : (j + 1) * ROWS] + inverse[side, j : j + 1] * att[kk, j]

    here = {"x": x, "y": y, "z": z}
    orders = ("xyz", "yzx", "zxy")

    def region(p, step, core=k, **at):
        at = {**here, **at}
        index = [at[a] for a in orders[p][: step - 1 if step else None : -1]]
        return xb.at[(core, p, *index)]

    def peer(axis, d):
        at = {**here, axis: lax.rem(here[axis] + d, 4)}
        return at[axis], (at["y"] * 4 + at["x"]) * 2 + k, at["z"]

    def g_send(p, step, d):
        axis = orders[p][step]
        _, seq, exp = peer(axis, d)
        block = region(p, step)
        return remote(block, block, gs.at[p, step, d], gr.at[p, step, here[axis]], seq, exp)

    def g_wait(p, step, d):
        axis = orders[p][step]
        there, seq, exp = peer(axis, d)
        block = region(p, step, **{axis: there})
        remote(block, block, gs.at[p, step, 0], gr.at[p, step, there], seq, exp).wait_recv()

    def h_copy(p, there, core):
        block = xb.at[core, p, there]
        return remote(block, block, hs.at[p, there], hr.at[p, there], sib, z)

    def own_block(p, core):
        return (core, p, *[here[a] for a in reversed(orders[p])])

    for p in range(3):
        rows = [jnp.concatenate([att[kk, j] for j in (2 * p, 2 * p + 1)], axis=1) for kk in range(2)]
        xb[own_block(p, k)] = jnp.concatenate(rows, axis=0).astype(BF16)
    for d in (2, 1, 3):
        for p in range(3):
            g_send(p, 0, d).start()
    for step in (1, 2):
        for p in range(3):
            for d in (1, 3, 2):
                g_wait(p, step - 1, d)
            for d in (2, 1, 3):
                g_send(p, step, d).start()
    for p in range(3):
        h_copy(p, here[orders[p][2]], k).start()
    for d in (1, 3, 2):
        for p in range(3):
            g_wait(p, 2, d)
            h_copy(p, peer(orders[p][2], d)[0], k).start()

    def rows_sent():
        for p in range(3):
            for step in range(3):
                for d in (1, 2, 3):
                    g_send(p, step, d).wait_send()
            for there in range(4):
                h_copy(p, there, k).wait_send()

    sent.append(rows_sent)

    for cp in loads[N_SMALL + 4 : N_SMALL + 6]:
        cp.wait()

    def project(core, sums):
        for zz in range(EXP):
            at = pl.multiple_of(zz * QUARTER + core * PART, PART)
            turned = xb[core, 1, :, zz]
            turned = jnp.stack([turned[i, j] for j in range(4) for i in range(4)])
            rows = [xb[core, 0, zz], turned, xb[core, 2, :, :, zz]]
            rows = jnp.concatenate([r.reshape(TOTAL, THIRD) for r in rows], axis=1).astype(F32)
            squares = rows * rows
            total = squares[:, 0:128]
            for i in range(1, PART // 128):
                total = total + squares[:, i * 128 : (i + 1) * 128]
            rows = (rows * gainf[:, pl.ds(at, PART)]).astype(BF16)
            got = (
                total,
                dot(rows, wgb[pl.ds(at, PART), :]),
                dot(rows, wub[pl.ds(at, PART), :]),
                dot_t(rows, rpad[:, pl.ds(at, PART)]),
            )
            sums = got if sums is None else tuple(a + b for a, b in zip(sums, got))
        return sums

    for ref, value in zip((accs, accg, accu, accl), project(k, None)):
        ref[...] = value
    for p in range(3):
        for there in range(4):
            h_copy(p, there, 1 - k).wait_recv()
    squares, gate, up, logits = project(1 - k, tuple(ref[...] for ref in (accs, accg, accu, accl)))
    scale = lax.rsqrt(jnp.sum(squares, axis=1, keepdims=True) / WIDTH + NORM_EPS)
    gate = gate * scale
    logits = logits * scale
    first, second = rcol[:, 0:1], rcol[:, 1:2]
    expert = iota((TOTAL, PAIR), 1).astype(F32)
    here_e = z.astype(F32)
    mine = jnp.sum(jnp.where(expert == here_e, logits, 0.0), axis=1, keepdims=True)
    theirs = jnp.sum(jnp.where(expert == first + second - here_e, logits, 0.0), axis=1, keepdims=True)
    share = 1.0 / (1.0 + jnp.exp(theirs - mine))
    share = jnp.where((first == here_e) | (second == here_e), share, 0.0)
    units = (gate / (1.0 + jnp.exp(-gate)) * (up * scale) * share).astype(BF16)

    usnd[...] = units
    u_copy = remote(usnd, urcv, us.at[0], ur.at[0], sib, z)
    u_copy.start()
    sent.append(lambda: u_copy.wait_send())

    for cp in loads[N_SMALL + 6 :]:
        cp.wait()
    for i in range(CHIPS // 2):
        low = dot_t(units[i * 32 : (i + 1) * 32], adnb[i * 128 : (i + 1) * 128, :])
        for j in range(2):
            lsnd[i % 2 * 2 + j, i // 2] = low[j * PAIR : (j + 1) * PAIR].astype(BF16)

    def low_copy(step, d):
        axis = "xy"[step]
        there, seq, exp = peer(axis, d)
        src, dst = ((lsnd, lrcv), (lsum, lrow))[step]
        mine = here[axis]
        return remote(src.at[there], dst.at[mine], ls.at[step, d], lr.at[step, mine], seq, exp)

    def low_sum(step):
        axis = "xy"[step]
        src, dst = ((lsnd, lrcv), (lsum, lrow))[step]
        total = src[here[axis]].astype(F32)
        for d in (1, 3, 2):
            there, seq, exp = peer(axis, d)
            remote(
                src.at[here[axis]], dst.at[there], ls.at[step, 0], lr.at[step, there], seq, exp
            ).wait_recv()
            total = total + dst[there].astype(F32)
        return total

    for d in (2, 1, 3):
        low_copy(0, d).start()
    sent.append(lambda: [low_copy(step, d).wait_send() for step in range(2) for d in (1, 2, 3)])

    sum_orders = ("zyx", "xzy", "yxz")

    def part_of(t, step, there):
        if step == 1 and t == 2:
            return p3.at[t, :, there]
        return (p2, p3, p4)[step].at[t, there]

    def s_send(t, step, d):
        axis = sum_orders[t][step]
        there, seq, exp = peer(axis, d)
        return remote(
            part_of(t, step, there), (r2, r3, r4)[step].at[t, here[axis]],
            ss.at[t, step, d], sr.at[t, step, here[axis]], seq, exp,
        )

    def s_sum(t, step):
        axis = sum_orders[t][step]
        into = (r2, r3, r4)[step]
        total = part_of(t, step, here[axis])[...].astype(F32)
        for d in (1, 3, 2):
            there, seq, exp = peer(axis, d)
            remote(
                part_of(t, step, here[axis]), into.at[t, there],
                ss.at[t, step, 0], sr.at[t, step, there], seq, exp,
            ).wait_recv()
            total = total + into[t, there].astype(F32)
        return total

    def s_start(t, step):
        for d in (2, 1, 3):
            s_send(t, step, d).start()

    ahead = [dot(units, wdb[0:UNITS, zz * PART : zz * PART + THIRD]) for zz in range(EXP)]
    u_copy.wait_recv()
    for cp in down_copies:
        cp.wait_recv()
    both_units = jnp.concatenate([units, urcv[...]], axis=1)
    for t in range(3):
        for zz in range(EXP):
            at = zz * PART + t * THIRD
            if t == 0:
                both = ahead[zz] + dot(urcv[...], wdb[UNITS:, at : at + THIRD])
            else:
                both = dot(both_units, wdb[:, at : at + THIRD])
            both = both.astype(BF16).reshape(4, 4, PAIR, THIRD)
            if t == 0:
                p2[t, zz] = both
            elif t == 1:
                for i in range(4):
                    p2[t, i, zz] = both[:, i]
            else:
                p2[t, :, zz] = both
        s_start(t, 0)
    sent.append(
        lambda: [s_send(t, i, d).wait_send() for t in range(3) for i in range(3) for d in (1, 2, 3)]
    )

    lsum[...] = low_sum(0).astype(BF16)
    for d in (2, 1, 3):
        low_copy(1, d).start()
    for t in range(3):
        p3[t] = s_sum(t, 0).astype(BF16)
        s_start(t, 1)

    low = low_sum(1)
    lpair[0] = low.astype(BF16)
    lp_copy = remote(lpair.at[0], lpair.at[1], lps.at[0], lpr.at[0], sib, z)
    lp_copy.start()
    sent.append(lambda: lp_copy.wait_send())
    for cp in up_copies:
        cp.wait_recv()
    lp_copy.wait_recv()
    low = low + lpair[1].astype(F32)
    low = jnp.where(lax.div(lane16, 16) == lax.rem(ten_rows, 8), low, 0.0).astype(BF16)
    for zz in range(EXP):
        asnd[zz] = dot(low, upb[:, zz * PART : (zz + 1) * PART]).astype(BF16)

    def a_copy(d):
        zz = lax.rem(z + d, EXP)
        return remote(asnd.at[zz], arcv.at[z], as_.at[d], ar.at[z], s, zz)

    for d in (2, 1, 3):
        a_copy(d).start()
    sent.append(lambda: [a_copy(d).wait_send() for d in (1, 2, 3)])

    for t in range(3):
        p4[t] = s_sum(t, 1).astype(BF16)
        s_start(t, 2)
    adapter = asnd[z].astype(F32)
    for d in (1, 3, 2):
        zz = lax.rem(z + d, EXP)
        remote(asnd.at[z], arcv.at[zz], as_.at[0], ar.at[zz], s, zz).wait_recv()
        adapter = adapter + arcv[zz].astype(F32)
    total = jnp.concatenate([s_sum(t, 2) for t in range(3)], axis=1) + adapter

    theirs = jnp.where(k == 0, total[ROWS:], total[:ROWS])
    fpair[0] = jnp.concatenate([theirs[:, : PART // 2], theirs[:, PART // 2 :]], axis=0).astype(BF16)
    f_copy = remote(fpair.at[0], fpair.at[1], fs.at[0], fr.at[0], sib, z)
    f_copy.start()
    sent.append(lambda: f_copy.wait_send())
    mine = jnp.where(k == 0, total[:ROWS], total[ROWS:])
    resid = [[xb[own_block(p, kk)].astype(F32) for p in range(3)] for kk in range(2)]
    resid = [jnp.concatenate(r, axis=1) for r in resid]
    resid = [jnp.where(k == 0, r[:ROWS], r[ROWS:]) for r in resid]
    f_copy.wait_recv()
    got = fpair[1].astype(F32)
    got = jnp.concatenate([got[:ROWS], got[ROWS:]], axis=1)
    got = [jnp.where(k == kk, mine, got) for kk in range(2)]
    out[...] = jnp.concatenate([r + g for r, g in zip(resid, got)], axis=1).astype(BF16)

    for wait in sent:
        wait()


def on_device(
    hidden, queries, suffix_row_keys, suffix_row_values, prefix_cached_keys, prefix_cached_values,
    expert_norm_gain, router, gate_weight, up_weight, down_weight, adapter_down_maps,
    adapter_up_maps, routes, tenants, lengths,
):
    vmem = pl.BlockSpec(memory_space=pltpu.VMEM)
    hbm = pl.BlockSpec(memory_space=pl.ANY)
    dma = pltpu.SemaphoreType.DMA
    scratch = [
        pltpu.SMEM((TOTAL,), jnp.int32),
        pltpu.SMEM((64,), jnp.int32),
        pltpu.VMEM((ROWS, QUARTER), BF16),
        pltpu.VMEM((ROWS, QUARTER), BF16),
        pltpu.VMEM((ROWS, KV * HEAD), BF16),
        pltpu.VMEM((ROWS, KV * HEAD), BF16),
        pltpu.VMEM((EXP, WIDTH), BF16),
        pltpu.VMEM((2, TOTAL), jnp.int32),
        pltpu.VMEM((WIDTH,), BF16),
        pltpu.VMEM((1, WIDTH), F32),
        pltpu.VMEM((MSG, HEAD), BF16),
        pltpu.VMEM((2, MSG, HEAD), BF16),
        pltpu.VMEM((CHIPS, BLK, HEAD), BF16),
        pltpu.VMEM((2 * PREFIX, HEAD), BF16),
        pltpu.VMEM((2 * PREFIX, HEAD), BF16),
        pltpu.VMEM((CHIPS, MSG, HEAD), BF16),
        pltpu.VMEM((CHIPS, MSG, HEAD), BF16),
        pltpu.VMEM((2, GROUP, ROWS, HEAD), F32),
        pltpu.VMEM((PAIR, 128), F32),
        pltpu.VMEM((PREFIX, HEAD), BF16),
        pltpu.VMEM((PREFIX, HEAD), BF16),
        pltpu.VMEM((2, 3, 4, 4, 4, PAIR, THIRD), BF16),
        pltpu.VMEM((WIDTH, UNITS), BF16),
        pltpu.VMEM((WIDTH, UNITS), BF16),
        pltpu.VMEM((2 * UNITS, HALF), BF16),
        pltpu.VMEM((1024, UNITS), BF16),
        pltpu.VMEM((128, HALF), BF16),
        pltpu.VMEM((TOTAL, UNITS), F32),
        pltpu.VMEM((TOTAL, UNITS), F32),
        pltpu.VMEM((TOTAL, 128), F32),
        pltpu.VMEM((TOTAL, PAIR), F32),
        pltpu.VMEM((PAIR, WIDTH), BF16),
        pltpu.VMEM((TOTAL, PAIR), F32),
        pltpu.VMEM((4, 4, PAIR, 128), BF16),
        pltpu.VMEM((4, 4, PAIR, 128), BF16),
        pltpu.VMEM((4, PAIR, 128), BF16),
        pltpu.VMEM((4, PAIR, 128), BF16),
        pltpu.VMEM((2, PAIR, 128), BF16),
        pltpu.VMEM((EXP, PAIR, PART), BF16),
        pltpu.VMEM((EXP, PAIR, PART), BF16),
        pltpu.VMEM((TOTAL, UNITS), BF16),
        pltpu.VMEM((TOTAL, UNITS), BF16),
        pltpu.VMEM((3, 4, 4, 4, PAIR, THIRD), BF16),
        pltpu.VMEM((3, 4, 4, 4, PAIR, THIRD), BF16),
        pltpu.VMEM((3, 4, 4, PAIR, THIRD), BF16),
        pltpu.VMEM((3, 4, 4, PAIR, THIRD), BF16),
        pltpu.VMEM((3, 4, PAIR, THIRD), BF16),
        pltpu.VMEM((3, 4, PAIR, THIRD), BF16),
        pltpu.VMEM((2, PAIR, PART // 2), BF16),
        dma((24,)),
        dma((1,)),
        dma((1,)),
        dma((2,)),
        dma((2,)),
        dma((CHIPS,)),
        dma((CHIPS,)),
        dma((CHIPS,)),
        dma((CHIPS,)),
        dma((3, 3, 4)),
        dma((3, 3, 4)),
        dma((3, 4)),
        dma((3, 4)),
        dma((4,)),
        dma((4,)),
        dma((2, 4)),
        dma((2, 4)),
        dma((1,)),
        dma((1,)),
        dma((4,)),
        dma((4,)),
        dma((4,)),
        dma((4,)),
        dma((1,)),
        dma((1,)),
        dma((3, 3, 4)),
        dma((3, 3, 4)),
        dma((1,)),
        dma((1,)),
    ]
    return pl.pallas_call(
        kernel,
        out_shape=jax.ShapeDtypeStruct((ROWS, QUARTER), BF16),
        in_specs=[hbm] * 16,
        out_specs=vmem,
        scratch_shapes=scratch,
        compiler_params=pltpu.CompilerParams(
            collective_id=0, has_side_effects=True, vmem_limit_bytes=58 * 1024 * 1024
        ),
        cost_estimate=pl.CostEstimate(flops=5 * 10**9, bytes_accessed=13 * 2**20, transcendentals=7 * 10**6),
        name="layer",
    )(
        hidden, queries, suffix_row_keys, suffix_row_values, prefix_cached_keys,
        prefix_cached_values, expert_norm_gain, router.T,
        gate_weight.reshape(WIDTH, UNITS), up_weight.reshape(WIDTH, UNITS),
        down_weight.reshape(UNITS, WIDTH), adapter_down_maps.reshape(-1, UNITS),
        adapter_up_maps.reshape(-1, WIDTH), routes.T, tenants, lengths,
    )


def solution(mesh):
    in_specs = (
        P("seq", "exp"),
        P("seq", "exp"),
        P("seq", "exp"),
        P("seq", "exp"),
        P("seq", "exp"),
        P("seq", "exp"),
        P(),
        P(),
        P("exp", None, "seq"),
        P("exp", None, "seq"),
        P("exp", "seq", None),
        P(None, "exp", None, "seq"),
        P("seq", "exp", None, None),
        P(),
        P(),
        P(),
    )
    return jax.shard_map(
        on_device, mesh=mesh, in_specs=in_specs, out_specs=P("seq", "exp"), check_vma=False
    )
```
